32 devices in a mesh: seq: 4 (over y, x), fsdp: 8 (over z, core).
Axes of the slice: x: 2, y: 2, z: 4, core: 2. Of those that a mesh axis runs over, the one named last changes fastest.
Arguments:
- hidden_in: bfloat16 [8, 512, 2048], P('fsdp', 'seq'), may hold values from -6 to 6
- norm_one: bfloat16 [2048], P('fsdp'), may hold values from 0.5 to 1.5
- w_qkv: bfloat16 [2048, 6144], P('fsdp'), may hold values from -0.125 to 0.125
- w_out: bfloat16 [2048, 2048], P('fsdp'), may hold values from -1 to 1
- norm_two: bfloat16 [2048], P('fsdp'), may hold values from 0.5 to 1.5
- w_gate_up: bfloat16 [2048, 16384], P('fsdp'), may hold values from -0.125 to 0.125
- w_down: bfloat16 [8192, 2048], P('fsdp'), may hold values from -0.0625 to 0.0625
- grad_out: bfloat16 [8, 512, 2048], P('fsdp', 'seq'), may hold values from -6 to 6
Outputs:
- out_hidden: bfloat16 [8, 512, 2048], P('fsdp', 'seq')
- grad_input: float32 [8, 512, 2048], P('fsdp', 'seq')
- grad_norm_one: float32 [2048], P('fsdp')
- grad_qkv: float32 [2048, 6144], P('fsdp')
- grad_out_proj: float32 [2048, 2048], P('fsdp')
- grad_norm_two: float32 [2048], P('fsdp')
- grad_gate_up: float32 [2048, 16384], P('fsdp')
- grad_down: float32 [8192, 2048], P('fsdp')
The draws below stay inside these ranges and needn't reach their ends.
All inputs are finite; a program needn't handle non-finite values.
Results may differ from the reference program's by a relative error of at most 0.02.
Values may be sent and summed in bfloat16 or wider, within the bound.
No kernel may reach another device: no remote copies, remote signals or barrier semaphores. Data moves between devices by JAX's collectives and lax.ppermute only.
A program may use at most 576 MiB of HBM per device.

```python
import jax
import jax.numpy as jnp
from jax import lax

D = 2048
FF = 8192
HEAD_DIM = 64
SEQ_LEN = 512
SEQS = 8


def levels(own_key, extent, shards, least, largest):
    def one(axis_at, parts):
        heights = jax.random.uniform(jax.random.fold_in(jax.random.fold_in(own_key, 6), axis_at), (parts,), jnp.float32, least / len(shards), largest / len(shards))
        return jnp.repeat(jnp.exp(heights), extent[axis_at] // parts).reshape((-1,) + (1,) * (len(extent) - axis_at - 1))

    factor_of = one(*shards[0])
    for cut in shards[1:]:
        factor_of = factor_of * one(*cut)
    return factor_of


def bell_draw(stream_key, extent, scale, limit, shards=(), kind=jnp.bfloat16):
    array = scale * jax.random.normal(stream_key, extent, jnp.float32)
    if shards:
        array = array * levels(stream_key, extent, shards, -0.22, 0.18)
    return jnp.clip(array, -limit, limit).astype(kind)


def setup_inputs(seed: int = 0) -> dict:
    key_list = jax.random.split(jax.random.key(seed), 9)
    return {
        "hidden_in": bell_draw(key_list[0], (SEQS, SEQ_LEN, D), 1.0, 6.0, ((0, 8), (1, 4))),
        "norm_one": jnp.clip(1.0 + 0.1 * jax.random.normal(key_list[1], (D,), jnp.float32), 0.5, 1.5).astype(jnp.bfloat16),
        "w_qkv": bell_draw(key_list[2], (D, 3 * D), D ** -0.5, 0.125, ((0, 8),)),
        "w_out": bell_draw(key_list[3], (D, D), (D // 64) ** -0.5, 1.0, ((0, 8),)),
        "norm_two": jnp.clip(1.0 + 0.1 * jax.random.normal(key_list[4], (D,), jnp.float32), 0.5, 1.5).astype(jnp.bfloat16),
        "w_gate_up": bell_draw(key_list[5], (D, 2 * FF), D ** -0.5, 0.125, ((0, 8),)),
        "w_down": bell_draw(key_list[6], (FF, D), FF ** -0.5, 0.0625, ((0, 8),)),
        "grad_out": bell_draw(key_list[7], (SEQS, SEQ_LEN, D), 1.0, 6.0, ((0, 8), (1, 4))),
    }


EPSILON = 1e-05
THETA = 130000.0
SCALE = 0.125

@jax.custom_vjp
def low(v):
    return lax.optimization_barrier(v.astype(jnp.bfloat16)).astype(jnp.float32)

@jax.custom_vjp
def low_back(v):
    return v

def low_keep(v):
    return (low(v), None)

def low_pass(kept, grad):
    return (grad,)

def back_keep(v):
    return (v, None)

def back_low(kept, grad):
    return (low(grad),)
low.defvjp(low_keep, low_pass)
low_back.defvjp(back_keep, back_low)

def matmul(left, right):
    return jnp.dot(left, right, precision=lax.Precision.HIGHEST)

def rope_tables(length):
    half = HEAD_DIM // 2
    freqs = THETA ** (-(jnp.arange(half, dtype=jnp.float32) * 2.0) / HEAD_DIM)
    angles = jnp.arange(length, dtype=jnp.float32)[:, None] * freqs[None, :]
    angles = jnp.concatenate([angles, angles], axis=1)
    return (jnp.cos(angles)[:, None, :], jnp.sin(angles)[:, None, :])

def rotate(values, cosine, sine):
    half = values.shape[-1] // 2
    turned = jnp.concatenate([-values[..., half:], values[..., :half]], axis=-1)
    return values * cosine + turned * sine

def attend_head(operands):
    query, keys, values = operands
    length = query.shape[0]
    scores = low_back(matmul(query, keys.T) * SCALE)
    rows = jnp.arange(length)[:, None]
    columns = jnp.arange(length)[None, :]
    scores = jnp.where(columns <= rows, scores, -1e+30)
    highest = lax.optimization_barrier(jnp.max(scores, axis=-1, keepdims=True))
    weights = jnp.exp(scores - highest)
    probabilities = weights / lax.optimization_barrier(jnp.sum(weights, axis=-1, keepdims=True))
    return matmul(low(probabilities), values)

def layer(inputs, params):
    norm_one, w_qkv, w_out, norm_two, w_gate_up, w_down = params
    length = inputs.shape[0]
    width = inputs.shape[1]
    heads = width // HEAD_DIM
    factor_one = lax.rsqrt(lax.optimization_barrier(jnp.mean(inputs * inputs, axis=-1, keepdims=True)) + EPSILON)
    normed = low(inputs * factor_one * norm_one)
    mixed = low_back(low(matmul(normed, w_qkv))).reshape(length, 3, heads, HEAD_DIM)
    cosine, sine = rope_tables(length)
    query = low(rotate(mixed[:, 0], cosine, sine))
    keys = low(rotate(mixed[:, 1], cosine, sine))
    values = mixed[:, 2]
    heads_first = (jnp.transpose(query, (1, 0, 2)), jnp.transpose(keys, (1, 0, 2)), jnp.transpose(values, (1, 0, 2)))
    attended = lax.map(jax.checkpoint(attend_head), heads_first)
    attended = low_back(low(jnp.transpose(attended, (1, 0, 2)).reshape(length, width)))
    middle = inputs + low_back(matmul(attended, w_out))
    factor_two = lax.rsqrt(lax.optimization_barrier(jnp.mean(middle * middle, axis=-1, keepdims=True)) + EPSILON)
    normed_two = low(middle * factor_two * norm_two)
    gate_up = low_back(matmul(normed_two, w_gate_up))
    hidden = low(jax.nn.silu(gate_up[:, :FF]) * gate_up[:, FF:])
    return middle + low_back(matmul(hidden, w_down))

def reference(hidden_in, norm_one, w_qkv, w_out, norm_two, w_gate_up, w_down, grad_out):
    params = tuple((weight.astype(jnp.float32) for weight in (norm_one, w_qkv, w_out, norm_two, w_gate_up, w_down)))

    def per_sequence(totals, pair):
        inputs, cotangent = pair
        output, pull = jax.vjp(layer, inputs.astype(jnp.float32), params)
        grad_inputs, grad_params = pull(cotangent.astype(jnp.float32))
        totals = jax.tree.map(lambda first, second: first + second, totals, grad_params)
        return (totals, (output.astype(jnp.bfloat16), grad_inputs))
    zeros = jax.tree.map(jnp.zeros_like, params)
    totals, (outputs, grad_inputs) = lax.scan(per_sequence, zeros, (hidden_in, grad_out))
    return (outputs, grad_inputs, totals[0], totals[1], totals[2], totals[3], totals[4], totals[5])
```

```python
import functools

import jax
import jax.numpy as jnp
from jax import lax
from jax.experimental import pallas as pl
from jax.experimental.pallas import tpu as pltpu
from jax.sharding import PartitionSpec as P

HEAD_DIM = 64


EPSILON = 1e-05
THETA = 130000.0
SCALE = 0.125
LANES = 128


def outer_sum(left, right):
    return lax.dot_general(
        left, right, (((0,), (0,)), ((), ())), preferred_element_type=jnp.float32
    )


def back_product(grad, weight):
    return lax.dot_general(
        grad, weight, (((1,), (1,)), ((), ())), preferred_element_type=jnp.float32
    )


def rope_tables(length):
    half = HEAD_DIM // 2
    freqs = THETA ** (-(jnp.arange(half, dtype=jnp.float32) * 2.0) / HEAD_DIM)
    angles = jnp.arange(length, dtype=jnp.float32)[:, None] * freqs[None, :]
    angles = jnp.concatenate([angles, angles], axis=1)
    return (jnp.cos(angles)[:, None, :], jnp.sin(angles)[:, None, :])


def rotate(values, cosine, sine):
    half = values.shape[-1] // 2
    turned = jnp.concatenate([-values[..., half:], values[..., :half]], axis=-1)
    return values * cosine + turned * sine


def unrotate(grads, cosine, sine):
    half = grads.shape[-1] // 2
    scaled = grads * sine
    turned = jnp.concatenate([scaled[..., half:], -scaled[..., :half]], axis=-1)
    return grads * cosine + turned


def norm_forward(values, gain):
    factor = lax.rsqrt(jnp.mean(values * values, axis=-1, keepdims=True) + EPSILON)
    return (values * factor * gain, factor)


def norm_backward(values, factor, gain, grad):
    grad_gain = jnp.sum(grad * values * factor, axis=0)
    scaled = grad * gain
    grad_values = factor * scaled - values * factor**3 * jnp.mean(
        scaled * values, axis=-1, keepdims=True
    )
    return (grad_values, grad_gain)


def fetch_rows(gain, first, second):
    return (
        lax.all_gather(gain, "fsdp", axis=0, tiled=True),
        lax.all_gather(first, "fsdp", axis=0, tiled=True),
        lax.all_gather(second, "fsdp", axis=0, tiled=True),
    )


def weight_term(left, right):
    return outer_sum(left, right)


def reduce_grads(terms):
    partial_sums = (
        lax.psum_scatter(
            terms[0].astype(jnp.bfloat16), "fsdp", scatter_dimension=0, tiled=True
        ).astype(jnp.float32),
        lax.psum_scatter(
            terms[1].astype(jnp.bfloat16), "fsdp", scatter_dimension=0, tiled=True
        ).astype(jnp.float32),
    )
    return (
        lax.psum(partial_sums[0].astype(jnp.bfloat16), "seq").astype(jnp.float32),
        lax.psum(partial_sums[1].astype(jnp.bfloat16), "seq").astype(jnp.float32),
    )


def block_scores(query_block, key_rows, offset):
    scores = (
        jnp.einsum("qhd,khd->hqk", query_block, key_rows, preferred_element_type=jnp.float32)
        * SCALE
    )
    rows = offset + jnp.arange(query_block.shape[0])[:, None]
    columns = jnp.arange(key_rows.shape[0])[None, :]
    return jnp.where((columns <= rows)[None], scores, -1e30)


def gathered_plan(hidden_in, norm_one, w_qkv, w_out, norm_two, w_gate_up, w_down, grad_out):
    inputs = hidden_in[0].astype(jnp.float32)
    tokens = inputs.shape[0]
    width = inputs.shape[1]
    gain_one, qkv_full, out_full = fetch_rows(norm_one, w_qkv, w_out)
    normed, factor_one = norm_forward(inputs, gain_one.astype(jnp.float32))
    normed_low = normed.astype(jnp.bfloat16)
    mixed = jnp.dot(normed_low, qkv_full, preferred_element_type=jnp.float32).astype(jnp.bfloat16)
    regrouped = lax.all_to_all(
        mixed.reshape(tokens, 3, width), "seq", split_axis=2, concat_axis=0, tiled=True
    )
    length = regrouped.shape[0]
    local_width = regrouped.shape[2]
    heads = local_width // HEAD_DIM
    regrouped = regrouped.reshape(length, 3, heads, HEAD_DIM)
    cosine, sine = rope_tables(length)
    query = rotate(regrouped[:, 0].astype(jnp.float32), cosine, sine).astype(jnp.bfloat16)
    keys = rotate(regrouped[:, 1].astype(jnp.float32), cosine, sine).astype(jnp.bfloat16)
    values = regrouped[:, 2]
    block = min(512, length)
    attended_parts = []
    logsums = []
    for start in range(0, length, block):
        stop = start + block
        scores = block_scores(query[start:stop], keys[:stop], start)
        highest = jnp.max(scores, axis=-1, keepdims=True)
        weights = jnp.exp(scores - highest)
        total = jnp.sum(weights, axis=-1, keepdims=True)
        probabilities = (weights / total).astype(jnp.bfloat16)
        logsums.append(highest + jnp.log(total))
        attended_parts.append(
            jnp.einsum(
                "hqk,khd->qhd", probabilities, values[:stop], preferred_element_type=jnp.float32
            )
        )
    attended = (
        jnp.concatenate(attended_parts, axis=0).reshape(length, local_width).astype(jnp.bfloat16)
    )
    back_rows = lax.all_to_all(attended, "seq", split_axis=0, concat_axis=1, tiled=True)
    middle = inputs + jnp.dot(back_rows, out_full, preferred_element_type=jnp.float32)
    gain_two, gate_up_full, down_full = fetch_rows(norm_two, w_gate_up, w_down)
    normed_two, factor_two = norm_forward(middle, gain_two.astype(jnp.float32))
    normed_two_low = normed_two.astype(jnp.bfloat16)
    gate_up = jnp.dot(normed_two_low, gate_up_full, preferred_element_type=jnp.float32)
    hidden_units = gate_up.shape[1] // 2
    gate = gate_up[:, :hidden_units]
    upward = gate_up[:, hidden_units:]
    sigmoid = jax.nn.sigmoid(gate)
    activated = gate * sigmoid
    hidden = (activated * upward).astype(jnp.bfloat16)
    output = middle + jnp.dot(hidden, down_full, preferred_element_type=jnp.float32)
    cotangent = grad_out[0]
    grad_hidden = back_product(cotangent, down_full)
    grad_gate = grad_hidden * upward * sigmoid * (1.0 + gate * (1.0 - sigmoid))
    grad_upward = grad_hidden * activated
    grad_gate_up_low = jnp.concatenate([grad_gate, grad_upward], axis=1).astype(jnp.bfloat16)
    grad_normed_two = back_product(grad_gate_up_low, gate_up_full)
    middle_part, grad_gain_two = norm_backward(
        middle, factor_two, gain_two.astype(jnp.float32), grad_normed_two
    )
    grad_middle = cotangent.astype(jnp.float32) + middle_part
    grad_gate_up_term = weight_term(normed_two_low, grad_gate_up_low)
    grad_branch = grad_middle.astype(jnp.bfloat16)
    grad_out_term = weight_term(back_rows, grad_branch)
    grad_down_term = weight_term(hidden, cotangent)
    grad_down_sum, gain_two_sum = reduce_grads((grad_down_term, grad_gain_two))
    gate_up_sum, out_proj_sum = reduce_grads((grad_gate_up_term, grad_out_term))
    gain_one, qkv_full, out_full = fetch_rows(norm_one, w_qkv, w_out)
    grad_attended = back_product(grad_branch, out_full).astype(jnp.bfloat16)
    grad_heads = lax.all_to_all(
        grad_attended, "seq", split_axis=1, concat_axis=0, tiled=True
    ).reshape(length, heads, HEAD_DIM)
    query_parts = []
    grad_keys = jnp.zeros((length, heads, HEAD_DIM), jnp.float32)
    grad_values = jnp.zeros((length, heads, HEAD_DIM), jnp.float32)
    for index, start in enumerate(range(0, length, block)):
        stop = start + block
        query_block = query[start:stop]
        grad_block = grad_heads[start:stop]
        scores = block_scores(query_block, keys[:stop], start)
        probabilities = jnp.exp(scores - logsums[index])
        grad_probabilities = jnp.einsum(
            "qhd,khd->hqk", grad_block, values[:stop], preferred_element_type=jnp.float32
        )
        inner = jnp.sum(probabilities * grad_probabilities, axis=-1, keepdims=True)
        grad_scores = (probabilities * (grad_probabilities - inner)).astype(jnp.bfloat16)
        query_parts.append(
            jnp.einsum("hqk,khd->qhd", grad_scores, keys[:stop], preferred_element_type=jnp.float32)
            * SCALE
        )
        key_term = (
            jnp.einsum("hqk,qhd->khd", grad_scores, query_block, preferred_element_type=jnp.float32)
            * SCALE
        )
        value_term = jnp.einsum(
            "hqk,qhd->khd",
            probabilities.astype(jnp.bfloat16),
            grad_block,
            preferred_element_type=jnp.float32,
        )
        grad_keys = grad_keys.at[:stop].add(key_term)
        grad_values = grad_values.at[:stop].add(value_term)
    grad_query = unrotate(jnp.concatenate(query_parts, axis=0), cosine, sine)
    grad_keys = unrotate(grad_keys, cosine, sine)
    stacked = (
        jnp.stack([grad_query, grad_keys, grad_values], axis=1)
        .astype(jnp.bfloat16)
        .reshape(length, 3, local_width)
    )
    grad_mixed = lax.all_to_all(stacked, "seq", split_axis=0, concat_axis=2, tiled=True).reshape(
        tokens, 3 * width
    )
    grad_qkv_term = weight_term(normed_low, grad_mixed)
    grad_normed_one = back_product(grad_mixed, qkv_full)
    input_part, grad_gain_one = norm_backward(
        inputs, factor_one, gain_one.astype(jnp.float32), grad_normed_one
    )
    grad_inputs = grad_middle + input_part
    qkv_sum, gain_one_sum = reduce_grads((grad_qkv_term, grad_gain_one))
    return (
        output.astype(jnp.bfloat16)[None],
        grad_inputs[None],
        gain_one_sum,
        qkv_sum,
        out_proj_sum,
        gain_two_sum,
        gate_up_sum,
        grad_down_sum,
    )


def xor_pairs(size, offset):
    return [(i, i ^ offset) for i in range(size)]


def swap_cores(values, fsdp):
    return lax.ppermute(values, "fsdp", xor_pairs(fsdp, 1))


def gather_tokens(block, seq, fsdp):
    row = jnp.stack(
        [block] + [lax.ppermute(block, "seq", xor_pairs(seq, k)) for k in range(1, seq)]
    )
    return jnp.stack([row, swap_cores(row, fsdp)])


def reduce_tokens(partial, seq, fsdp):
    other = swap_cores(partial[1], fsdp)
    row = (partial[0].astype(jnp.float32) + other.astype(jnp.float32)).astype(jnp.bfloat16)
    total = row[0].astype(jnp.float32)
    for k in range(1, seq):
        total = total + lax.ppermute(row[k], "seq", xor_pairs(seq, k)).astype(jnp.float32)
    return total


def rows_groups(fsdp):
    return [[i for i in range(core, fsdp, 2)] for core in range(2)]


def gather_rows(block, fsdp):
    return lax.all_gather(block, "fsdp", axis=0, tiled=True, axis_index_groups=rows_groups(fsdp))


def scatter_rows(term, fsdp):
    return lax.psum_scatter(
        term, "fsdp", scatter_dimension=0, tiled=True, axis_index_groups=rows_groups(fsdp)
    )


def lane_mask(rows):
    return lax.broadcasted_iota(jnp.int32, (rows, LANES), 1) < LANES // 2


def slice_wide(weight, gain, place, groups, chunk, seq):
    rows = weight.shape[0]

    def body(place_ref, weight_ref, gain_ref, out_ref):
        out_ref[0] = (weight_ref[...].astype(jnp.float32) * gain_ref[...]).astype(jnp.bfloat16)

    return pl.pallas_call(
        body,
        grid_spec=pltpu.PrefetchScalarGridSpec(
            num_scalar_prefetch=1,
            grid=(2, groups),
            in_specs=[
                pl.BlockSpec(
                    (rows, chunk), lambda j, k, p: (0, (k * 2 + (p[1] ^ j)) * seq + p[0])
                ),
                pl.BlockSpec((rows, 1), lambda j, k, p: (0, 0)),
            ],
            out_specs=pl.BlockSpec((1, rows, chunk), lambda j, k, p: (j, 0, k)),
        ),
        out_shape=jax.ShapeDtypeStruct((2, rows, groups * chunk), jnp.bfloat16),
        name="slice_wide",
    )(place, weight, gain)


def slice_heads(weight, gain, place, heads, seq):
    rows = weight.shape[0]
    part = weight.shape[1] // 3

    def body(place_ref, weight_ref, gain_ref, out_ref):
        own_seq, own_core = place_ref[0], place_ref[1]
        odd = (own_seq % 2) == 1
        low = lane_mask(rows)
        for core in range(2):
            for pair in range(heads // 2):
                tiles = []
                for head in (2 * pair, 2 * pair + 1):
                    start = (head * 2 + (own_core ^ core)) * (seq * HEAD_DIM) + (
                        own_seq // 2
                    ) * LANES
                    tile = weight_ref[:, pl.ds(pl.multiple_of(start, LANES), LANES)]
                    tiles.append(tile.astype(jnp.float32) * gain_ref[...])
                turned = [pltpu.roll(tile, LANES // 2, axis=1) for tile in tiles]
                first = jnp.where(odd, turned[0], tiles[0])
                second = jnp.where(odd, tiles[1], turned[1])
                out_ref[core, :, pair * LANES : (pair + 1) * LANES] = jnp.where(
                    low, first, second
                ).astype(jnp.bfloat16)

    return pl.pallas_call(
        body,
        grid_spec=pltpu.PrefetchScalarGridSpec(
            num_scalar_prefetch=1,
            grid=(3,),
            in_specs=[
                pl.BlockSpec((rows, part), lambda k, p: (0, k)),
                pl.BlockSpec((rows, 1), lambda k, p: (0, 0)),
            ],
            out_specs=pl.BlockSpec((2, rows, heads * HEAD_DIM), lambda k, p: (0, 0, k)),
        ),
        out_shape=jax.ShapeDtypeStruct((2, rows, 3 * heads * HEAD_DIM), jnp.bfloat16),
        name="slice_heads",
    )(place, weight, gain)


def fold(products):
    total = products[:, :LANES]
    for k in range(1, products.shape[1] // LANES):
        total = total + products[:, k * LANES : (k + 1) * LANES]
    return total


def merge_wide(pieces, weight, gain, place, groups, chunk):
    seq = len(pieces)
    rows = weight.shape[0]
    width = seq * chunk

    def body(place_ref, *refs):
        weight_ref, gain_ref = refs[seq : seq + 2]
        out_ref, sum_ref = refs[seq + 2 :]

        @pl.when((pl.program_id(0) == 0) & (pl.program_id(1) == 0))
        def _():
            sum_ref[...] = jnp.zeros_like(sum_ref)

        for r in range(seq):
            start = pl.multiple_of((place_ref[0] ^ r) * chunk, LANES)
            term = refs[r][0].astype(jnp.float32)
            out_ref[:, pl.ds(start, chunk)] = term * gain_ref[...]
            sum_ref[place_ref[0] ^ r] += fold(
                term * weight_ref[:, pl.ds(start, chunk)].astype(jnp.float32)
            )

    wide = pl.BlockSpec((rows, width), lambda j, k, p: (0, k * 2 + (p[1] ^ j)))
    return pl.pallas_call(
        body,
        grid_spec=pltpu.PrefetchScalarGridSpec(
            num_scalar_prefetch=1,
            grid=(2, groups),
            in_specs=[pl.BlockSpec((1, rows, chunk), lambda j, k, p: (j, 0, k))] * seq
            + [wide, pl.BlockSpec((rows, 1), lambda j, k, p: (0, 0))],
            out_specs=[wide, pl.BlockSpec((seq, rows, LANES), lambda j, k, p: (0, 0, 0))],
        ),
        out_shape=[
            jax.ShapeDtypeStruct(weight.shape, jnp.float32),
            jax.ShapeDtypeStruct((seq, rows, LANES), jnp.float32),
        ],
        name="merge_wide",
    )(place, *pieces, weight, gain)


def merge_heads(pieces, weight, gain, place, heads):
    seq = len(pieces)
    rows = weight.shape[0]
    part = weight.shape[1] // 3

    def body(place_ref, *refs):
        weight_ref, gain_ref = refs[seq : seq + 2]
        out_ref, sum_ref = refs[seq + 2 :]
        own_seq, own_core = place_ref[0], place_ref[1]
        odd = (own_seq % 2) == 1
        low = lane_mask(rows)

        @pl.when(pl.program_id(0) == 0)
        def _():
            sum_ref[...] = jnp.zeros_like(sum_ref)

        for core in range(2):
            for pair in range(heads // 2):
                for couple in range(seq // 2):
                    first, second = (
                        refs[2 * couple + k][core, :, pair * LANES : (pair + 1) * LANES].astype(
                            jnp.float32
                        )
                        for k in range(2)
                    )
                    turned_first = pltpu.roll(first, LANES // 2, axis=1)
                    turned_second = pltpu.roll(second, LANES // 2, axis=1)
                    for head, even_tile, odd_tile in (
                        (
                            2 * pair,
                            jnp.where(low, first, turned_second),
                            jnp.where(low, second, turned_first),
                        ),
                        (
                            2 * pair + 1,
                            jnp.where(low, turned_first, second),
                            jnp.where(low, turned_second, first),
                        ),
                    ):
                        tile = jnp.where(odd, odd_tile, even_tile)
                        start = (head * 2 + (own_core ^ core)) * (seq * HEAD_DIM) + (
                            (own_seq // 2) ^ couple
                        ) * LANES
                        columns = pl.ds(pl.multiple_of(start, LANES), LANES)
                        out_ref[:, columns] = tile * gain_ref[...]
                        sum_ref[(own_seq // 2) ^ couple] += tile * weight_ref[:, columns].astype(
                            jnp.float32
                        )

    wide = pl.BlockSpec((rows, part), lambda k, p: (0, k))
    return pl.pallas_call(
        body,
        grid_spec=pltpu.PrefetchScalarGridSpec(
            num_scalar_prefetch=1,
            grid=(3,),
            in_specs=[pl.BlockSpec((2, rows, heads * HEAD_DIM), lambda k, p: (0, 0, k))] * seq
            + [wide, pl.BlockSpec((rows, 1), lambda k, p: (0, 0))],
            out_specs=[wide, pl.BlockSpec((seq // 2, rows, LANES), lambda k, p: (0, 0, 0))],
        ),
        out_shape=[
            jax.ShapeDtypeStruct(weight.shape, jnp.float32),
            jax.ShapeDtypeStruct((seq // 2, rows, LANES), jnp.float32),
        ],
        name="merge_heads",
    )(place, *pieces, weight, gain)


def share_rows(piece, seq):
    return [piece] + [lax.ppermute(piece, "seq", xor_pairs(seq, k)) for k in range(1, seq)]


def place_rows(pieces, own_seq):
    rows, width = pieces[0].shape
    out = jnp.zeros((rows * len(pieces), width), jnp.float32)
    for k, piece in enumerate(pieces):
        out = lax.dynamic_update_slice(out, piece.astype(jnp.float32), ((own_seq ^ k) * rows, 0))
    return out


def both_halves(mine, other, own_core):
    return jnp.concatenate(
        [jnp.where(own_core == 0, mine, other), jnp.where(own_core == 0, other, mine)]
    )


def own_halves(rows, own_core, fsdp):
    half = rows.shape[0] // 2
    mine = lax.dynamic_slice_in_dim(rows, own_core * half, half)
    other = swap_cores(lax.dynamic_slice_in_dim(rows, (1 - own_core) * half, half), fsdp)
    return jnp.stack([mine, other])


def sliced_plan(
    seq, fsdp, hidden_in, norm_one, w_qkv, w_out, norm_two, w_gate_up, w_down, grad_out
):
    own_seq = lax.axis_index("seq")
    own_core = lax.axis_index("fsdp") % 2
    place = jnp.stack([own_seq, own_core]).astype(jnp.int32)
    chips = fsdp // 2
    inputs = hidden_in[0].astype(jnp.float32)
    cotangent = grad_out[0]
    tokens, width = inputs.shape
    length = tokens * seq
    hidden_units = w_down.shape[0] * fsdp
    chunk = hidden_units // (fsdp * seq)
    heads = width // HEAD_DIM // (2 * seq)
    gain_one = norm_one.astype(jnp.float32)[:, None]
    gain_two = norm_two.astype(jnp.float32)[:, None]

    qkv_parts = slice_heads(w_qkv, gain_one, place, heads, seq)
    qkv_chip = both_halves(qkv_parts[0], swap_cores(qkv_parts[1], fsdp), own_core)
    qkv = gather_rows(qkv_chip, fsdp)
    out_rows = w_out.shape[0] // seq
    out_proj = gather_rows(lax.dynamic_slice_in_dim(w_out, own_seq * out_rows, out_rows), fsdp)
    gate_up_parts = slice_wide(w_gate_up, gain_two, place, 2 * chips, chunk, seq)
    gate_up_chip = both_halves(gate_up_parts[0], swap_cores(gate_up_parts[1], fsdp), own_core)
    gate_up_w = gather_rows(gate_up_chip, fsdp)
    down = gather_rows(lax.dynamic_slice_in_dim(w_down, own_seq * chunk, chunk), fsdp)

    factor_one = lax.rsqrt(jnp.mean(inputs * inputs, axis=-1, keepdims=True) + EPSILON)
    normed = (inputs * factor_one).astype(jnp.bfloat16)
    group = 2 * seq * tokens
    normed_all = gather_tokens(normed, seq, fsdp).reshape(group, width)
    mixed = jnp.dot(normed_all, qkv, preferred_element_type=jnp.float32).astype(jnp.bfloat16)
    mixed = mixed.reshape(2, length, 3, heads, HEAD_DIM)
    block_starts = (own_seq ^ jnp.arange(seq)) * tokens
    positions = (block_starts[:, None] + jnp.arange(tokens)[None]).reshape(length)
    half = HEAD_DIM // 2
    freqs = THETA ** (-(jnp.arange(half, dtype=jnp.float32) * 2.0) / HEAD_DIM)
    angles = positions.astype(jnp.float32)[:, None] * freqs[None, :]
    angles = jnp.concatenate([angles, angles], axis=1)
    cosine, sine = jnp.cos(angles)[:, None, :], jnp.sin(angles)[:, None, :]
    query = rotate(mixed[:, :, 0].astype(jnp.float32), cosine, sine).astype(jnp.bfloat16)
    keys = rotate(mixed[:, :, 1].astype(jnp.float32), cosine, sine).astype(jnp.bfloat16)
    values = mixed[:, :, 2]
    visible = positions[None, :] <= positions[:, None]
    scores = (
        jnp.einsum("bqhd,bkhd->bhqk", query, keys, preferred_element_type=jnp.float32) * SCALE
    )
    scores = jnp.where(visible, scores, -1e30)
    highest = jnp.max(scores, axis=-1, keepdims=True)
    weights = jnp.exp(scores - highest)
    total = jnp.sum(weights, axis=-1, keepdims=True)
    probabilities = weights / total
    attended = jnp.einsum(
        "bhqk,bkhd->bqhd",
        probabilities.astype(jnp.bfloat16),
        values,
        preferred_element_type=jnp.float32,
    ).astype(jnp.bfloat16)
    attended = attended.reshape(group, heads * HEAD_DIM)
    branch = jnp.dot(attended, out_proj, preferred_element_type=jnp.float32).astype(jnp.bfloat16)
    middle = inputs + reduce_tokens(branch.reshape(2, seq, tokens, width), seq, fsdp)

    factor_two = lax.rsqrt(jnp.mean(middle * middle, axis=-1, keepdims=True) + EPSILON)
    normed_two = (middle * factor_two).astype(jnp.bfloat16)
    cotangent_all = gather_tokens(cotangent, seq, fsdp).reshape(group, width)
    normed_two_all = gather_tokens(normed_two, seq, fsdp).reshape(group, width)
    gate_up = jnp.dot(normed_two_all, gate_up_w, preferred_element_type=jnp.float32)
    units = gate_up.shape[1] // 2
    gate, upward = gate_up[:, :units], gate_up[:, units:]
    sigmoid = jax.nn.sigmoid(gate)
    activated = gate * sigmoid
    hidden = (activated * upward).astype(jnp.bfloat16)
    grad_down_rows = scatter_rows(outer_sum(hidden, cotangent_all).astype(jnp.bfloat16), fsdp)
    grad_hidden = back_product(cotangent_all, down)
    grad_gate = grad_hidden * upward * sigmoid * (1.0 + gate * (1.0 - sigmoid))
    grad_upward = grad_hidden * activated
    grad_low = jnp.concatenate([grad_gate, grad_upward], axis=1).astype(jnp.bfloat16)
    back = back_product(grad_low, gate_up_w).astype(jnp.bfloat16)
    scaled_two = reduce_tokens(back.reshape(2, seq, tokens, width), seq, fsdp)
    grad_gate_up_rows = scatter_rows(outer_sum(normed_two_all, grad_low).astype(jnp.bfloat16), fsdp)
    grad_middle = (
        cotangent.astype(jnp.float32)
        + factor_two * scaled_two
        - middle * factor_two**3 * jnp.mean(scaled_two * middle, axis=-1, keepdims=True)
    )
    grad_branch = gather_tokens(grad_middle.astype(jnp.bfloat16), seq, fsdp).reshape(group, width)
    forward = jnp.dot(hidden, down, preferred_element_type=jnp.float32).astype(jnp.bfloat16)
    output = middle + reduce_tokens(forward.reshape(2, seq, tokens, width), seq, fsdp)

    grad_out_rows = scatter_rows(outer_sum(attended, grad_branch).astype(jnp.bfloat16), fsdp)
    grad_heads = back_product(grad_branch, out_proj).astype(jnp.bfloat16)
    grad_heads = grad_heads.reshape(2, length, heads, HEAD_DIM)
    grad_probabilities = jnp.einsum(
        "bqhd,bkhd->bhqk", grad_heads, values, preferred_element_type=jnp.float32
    )
    inner = jnp.sum(probabilities * grad_probabilities, axis=-1, keepdims=True)
    grad_scores = (probabilities * (grad_probabilities - inner)).astype(jnp.bfloat16)
    grad_query = (
        jnp.einsum("bhqk,bkhd->bqhd", grad_scores, keys, preferred_element_type=jnp.float32) * SCALE
    )
    grad_keys = (
        jnp.einsum("bhqk,bqhd->bkhd", grad_scores, query, preferred_element_type=jnp.float32)
        * SCALE
    )
    grad_values = jnp.einsum(
        "bhqk,bqhd->bkhd",
        probabilities.astype(jnp.bfloat16),
        grad_heads,
        preferred_element_type=jnp.float32,
    )
    grad_mixed = jnp.stack(
        [unrotate(grad_query, cosine, sine), unrotate(grad_keys, cosine, sine), grad_values], axis=2
    )
    grad_mixed = grad_mixed.astype(jnp.bfloat16).reshape(group, 3 * heads * HEAD_DIM)
    grad_qkv_rows = scatter_rows(outer_sum(normed_all, grad_mixed).astype(jnp.bfloat16), fsdp)
    back = back_product(grad_mixed, qkv).astype(jnp.bfloat16)
    scaled_one = reduce_tokens(back.reshape(2, seq, tokens, width), seq, fsdp)
    grad_inputs = (
        grad_middle
        + factor_one * scaled_one
        - inputs * factor_one**3 * jnp.mean(scaled_one * inputs, axis=-1, keepdims=True)
    )

    grad_down = place_rows(share_rows(grad_down_rows, seq), own_seq)
    grad_out_proj = place_rows(share_rows(grad_out_rows, seq), own_seq)
    grad_gate_up, gain_two_sums = merge_wide(
        share_rows(own_halves(grad_gate_up_rows, own_core, fsdp), seq),
        w_gate_up,
        gain_two,
        place,
        2 * chips,
        chunk,
    )
    grad_qkv, gain_one_sums = merge_heads(
        share_rows(own_halves(grad_qkv_rows, own_core, fsdp), seq), w_qkv, gain_one, place, heads
    )
    return (
        output.astype(jnp.bfloat16)[None],
        grad_inputs[None],
        jnp.sum(gain_one_sums, axis=(0, 2)),
        grad_qkv,
        grad_out_proj,
        jnp.sum(gain_two_sums, axis=(0, 2)),
        grad_gate_up,
        grad_down,
    )


def solution(mesh):
    seq, fsdp = mesh.shape["seq"], mesh.shape["fsdp"]

    def on_device(hidden_in, norm_one, w_qkv, w_out, norm_two, w_gate_up, w_down, grad_out):
        arrays = (hidden_in, norm_one, w_qkv, w_out, norm_two, w_gate_up, w_down, grad_out)
        if (
            w_out.shape[0] == seq * HEAD_DIM
            and (fsdp // 2) % 2 == 0
            and seq & (seq - 1) == 0
            and (w_down.shape[0] // seq) % LANES == 0
        ):
            return sliced_plan(seq, fsdp, *arrays)
        return gathered_plan(*arrays)

    placed = (
        P("fsdp", "seq", None),
        P("fsdp"),
        P("fsdp", None),
        P("fsdp", None),
        P("fsdp"),
        P("fsdp", None),
        P("fsdp", None),
        P("fsdp", "seq", None),
    )
    return jax.shard_map(
        on_device,
        mesh=mesh,
        in_specs=placed,
        out_specs=(
            P("fsdp", "seq", None),
            P("fsdp", "seq", None),
            P("fsdp"),
            P("fsdp", None),
            P("fsdp", None),
            P("fsdp"),
            P("fsdp", None),
            P("fsdp", None),
        ),
        check_vma=False,
    )
```

```python
import functools

import jax
import jax.numpy as jnp
from jax import lax
from jax.experimental import pallas as pl
from jax.experimental.pallas import tpu as pltpu
from jax.sharding import PartitionSpec as P

HEAD_DIM = 64


EPSILON = 1e-05
THETA = 130000.0
SCALE = 0.125
LANES = 128


def outer_sum(left, right):
    return lax.dot_general(
        left, right, (((0,), (0,)), ((), ())), preferred_element_type=jnp.float32
    )


def back_product(grad, weight):
    return lax.dot_general(
        grad, weight, (((1,), (1,)), ((), ())), preferred_element_type=jnp.float32
    )


def rope_tables(length):
    half = HEAD_DIM // 2
    freqs = THETA ** (-(jnp.arange(half, dtype=jnp.float32) * 2.0) / HEAD_DIM)
    angles = jnp.arange(length, dtype=jnp.float32)[:, None] * freqs[None, :]
    angles = jnp.concatenate([angles, angles], axis=1)
    return (jnp.cos(angles)[:, None, :], jnp.sin(angles)[:, None, :])


def rotate(values, cosine, sine):
    half = values.shape[-1] // 2
    turned = jnp.concatenate([-values[..., half:], values[..., :half]], axis=-1)
    return values * cosine + turned * sine


def unrotate(grads, cosine, sine):
    half = grads.shape[-1] // 2
    scaled = grads * sine
    turned = jnp.concatenate([scaled[..., half:], -scaled[..., :half]], axis=-1)
    return grads * cosine + turned


def norm_forward(values, gain):
    factor = lax.rsqrt(jnp.mean(values * values, axis=-1, keepdims=True) + EPSILON)
    return (values * factor * gain, factor)


def norm_backward(values, factor, gain, grad):
    grad_gain = jnp.sum(grad * values * factor, axis=0)
    scaled = grad * gain
    grad_values = factor * scaled - values * factor**3 * jnp.mean(
        scaled * values, axis=-1, keepdims=True
    )
    return (grad_values, grad_gain)


def fetch_rows(gain, first, second):
    return (
        lax.all_gather(gain, "fsdp", axis=0, tiled=True),
        lax.all_gather(first, "fsdp", axis=0, tiled=True),
        lax.all_gather(second, "fsdp", axis=0, tiled=True),
    )


def weight_term(left, right):
    return outer_sum(left, right)


def reduce_grads(terms):
    partial_sums = (
        lax.psum_scatter(
            terms[0].astype(jnp.bfloat16), "fsdp", scatter_dimension=0, tiled=True
        ).astype(jnp.float32),
        lax.psum_scatter(
            terms[1].astype(jnp.bfloat16), "fsdp", scatter_dimension=0, tiled=True
        ).astype(jnp.float32),
    )
    return (
        lax.psum(partial_sums[0].astype(jnp.bfloat16), "seq").astype(jnp.float32),
        lax.psum(partial_sums[1].astype(jnp.bfloat16), "seq").astype(jnp.float32),
    )


def block_scores(query_block, key_rows, offset):
    scores = (
        jnp.einsum("qhd,khd->hqk", query_block, key_rows, preferred_element_type=jnp.float32)
        * SCALE
    )
    rows = offset + jnp.arange(query_block.shape[0])[:, None]
    columns = jnp.arange(key_rows.shape[0])[None, :]
    return jnp.where((columns <= rows)[None], scores, -1e30)


def gathered_plan(hidden_in, norm_one, w_qkv, w_out, norm_two, w_gate_up, w_down, grad_out):
    inputs = hidden_in[0].astype(jnp.float32)
    tokens = inputs.shape[0]
    width = inputs.shape[1]
    gain_one, qkv_full, out_full = fetch_rows(norm_one, w_qkv, w_out)
    normed, factor_one = norm_forward(inputs, gain_one.astype(jnp.float32))
    normed_low = normed.astype(jnp.bfloat16)
    mixed = jnp.dot(normed_low, qkv_full, preferred_element_type=jnp.float32).astype(jnp.bfloat16)
    regrouped = lax.all_to_all(
        mixed.reshape(tokens, 3, width), "seq", split_axis=2, concat_axis=0, tiled=True
    )
    length = regrouped.shape[0]
    local_width = regrouped.shape[2]
    heads = local_width // HEAD_DIM
    regrouped = regrouped.reshape(length, 3, heads, HEAD_DIM)
    cosine, sine = rope_tables(length)
    query = rotate(regrouped[:, 0].astype(jnp.float32), cosine, sine).astype(jnp.bfloat16)
    keys = rotate(regrouped[:, 1].astype(jnp.float32), cosine, sine).astype(jnp.bfloat16)
    values = regrouped[:, 2]
    block = min(512, length)
    attended_parts = []
    logsums = []
    for start in range(0, length, block):
        stop = start + block
        scores = block_scores(query[start:stop], keys[:stop], start)
        highest = jnp.max(scores, axis=-1, keepdims=True)
        weights = jnp.exp(scores - highest)
        total = jnp.sum(weights, axis=-1, keepdims=True)
        probabilities = (weights / total).astype(jnp.bfloat16)
        logsums.append(highest + jnp.log(total))
        attended_parts.append(
            jnp.einsum(
                "hqk,khd->qhd", probabilities, values[:stop], preferred_element_type=jnp.float32
            )
        )
    attended = (
        jnp.concatenate(attended_parts, axis=0).reshape(length, local_width).astype(jnp.bfloat16)
    )
    back_rows = lax.all_to_all(attended, "seq", split_axis=0, concat_axis=1, tiled=True)
    middle = inputs + jnp.dot(back_rows, out_full, preferred_element_type=jnp.float32)
    gain_two, gate_up_full, down_full = fetch_rows(norm_two, w_gate_up, w_down)
    normed_two, factor_two = norm_forward(middle, gain_two.astype(jnp.float32))
    normed_two_low = normed_two.astype(jnp.bfloat16)
    gate_up = jnp.dot(normed_two_low, gate_up_full, preferred_element_type=jnp.float32)
    hidden_units = gate_up.shape[1] // 2
    gate = gate_up[:, :hidden_units]
    upward = gate_up[:, hidden_units:]
    sigmoid = jax.nn.sigmoid(gate)
    activated = gate * sigmoid
    hidden = (activated * upward).astype(jnp.bfloat16)
    output = middle + jnp.dot(hidden, down_full, preferred_element_type=jnp.float32)
    cotangent = grad_out[0]
    grad_hidden = back_product(cotangent, down_full)
    grad_gate = grad_hidden * upward * sigmoid * (1.0 + gate * (1.0 - sigmoid))
    grad_upward = grad_hidden * activated
    grad_gate_up_low = jnp.concatenate([grad_gate, grad_upward], axis=1).astype(jnp.bfloat16)
    grad_normed_two = back_product(grad_gate_up_low, gate_up_full)
    middle_part, grad_gain_two = norm_backward(
        middle, factor_two, gain_two.astype(jnp.float32), grad_normed_two
    )
    grad_middle = cotangent.astype(jnp.float32) + middle_part
    grad_gate_up_term = weight_term(normed_two_low, grad_gate_up_low)
    grad_branch = grad_middle.astype(jnp.bfloat16)
    grad_out_term = weight_term(back_rows, grad_branch)
    grad_down_term = weight_term(hidden, cotangent)
    grad_down_sum, gain_two_sum = reduce_grads((grad_down_term, grad_gain_two))
    gate_up_sum, out_proj_sum = reduce_grads((grad_gate_up_term, grad_out_term))
    gain_one, qkv_full, out_full = fetch_rows(norm_one, w_qkv, w_out)
    grad_attended = back_product(grad_branch, out_full).astype(jnp.bfloat16)
    grad_heads = lax.all_to_all(
        grad_attended, "seq", split_axis=1, concat_axis=0, tiled=True
    ).reshape(length, heads, HEAD_DIM)
    query_parts = []
    grad_keys = jnp.zeros((length, heads, HEAD_DIM), jnp.float32)
    grad_values = jnp.zeros((length, heads, HEAD_DIM), jnp.float32)
    for index, start in enumerate(range(0, length, block)):
        stop = start + block
        query_block = query[start:stop]
        grad_block = grad_heads[start:stop]
        scores = block_scores(query_block, keys[:stop], start)
        probabilities = jnp.exp(scores - logsums[index])
        grad_probabilities = jnp.einsum(
            "qhd,khd->hqk", grad_block, values[:stop], preferred_element_type=jnp.float32
        )
        inner = jnp.sum(probabilities * grad_probabilities, axis=-1, keepdims=True)
        grad_scores = (probabilities * (grad_probabilities - inner)).astype(jnp.bfloat16)
        query_parts.append(
            jnp.einsum("hqk,khd->qhd", grad_scores, keys[:stop], preferred_element_type=jnp.float32)
            * SCALE
        )
        key_term = (
            jnp.einsum("hqk,qhd->khd", grad_scores, query_block, preferred_element_type=jnp.float32)
            * SCALE
        )
        value_term = jnp.einsum(
            "hqk,qhd->khd",
            probabilities.astype(jnp.bfloat16),
            grad_block,
            preferred_element_type=jnp.float32,
        )
        grad_keys = grad_keys.at[:stop].add(key_term)
        grad_values = grad_values.at[:stop].add(value_term)
    grad_query = unrotate(jnp.concatenate(query_parts, axis=0), cosine, sine)
    grad_keys = unrotate(grad_keys, cosine, sine)
    stacked = (
        jnp.stack([grad_query, grad_keys, grad_values], axis=1)
        .astype(jnp.bfloat16)
        .reshape(length, 3, local_width)
    )
    grad_mixed = lax.all_to_all(stacked, "seq", split_axis=0, concat_axis=2, tiled=True).reshape(
        tokens, 3 * width
    )
    grad_qkv_term = weight_term(normed_low, grad_mixed)
    grad_normed_one = back_product(grad_mixed, qkv_full)
    input_part, grad_gain_one = norm_backward(
        inputs, factor_one, gain_one.astype(jnp.float32), grad_normed_one
    )
    grad_inputs = grad_middle + input_part
    qkv_sum, gain_one_sum = reduce_grads((grad_qkv_term, grad_gain_one))
    return (
        output.astype(jnp.bfloat16)[None],
        grad_inputs[None],
        gain_one_sum,
        qkv_sum,
        out_proj_sum,
        gain_two_sum,
        gate_up_sum,
        grad_down_sum,
    )


def xor_pairs(size, offset):
    return [(i, i ^ offset) for i in range(size)]


def swap_cores(values):
    return lax.ppermute(values, "fsdp", xor_pairs(8, 1))


def swap_rows(values, offset):
    return lax.ppermute(values, "fsdp", xor_pairs(8, 2 * offset))


def swap_seq(values, offset):
    return lax.ppermute(values, "seq", xor_pairs(4, offset))


def fence(*values):
    return lax.optimization_barrier(values)


def window(needed, work):
    outs = jax.eval_shape(work)
    return lax.cond(
        needed,
        work,
        lambda: jax.tree.map(lambda out: jnp.zeros(out.shape, out.dtype), outs),
    )


def halves(block):
    half = block.shape[0] // 2
    return block[:half], block[half:]


def gather_one(block):
    first, second = halves(block)
    return swap_seq(first, 1), swap_seq(second, 2), swap_rows(block, 2)


def gather_two(block, first_more, second_more, next_row):
    first, second = halves(block)
    first = jnp.concatenate([first, first_more])
    second = jnp.concatenate([second, second_more])
    next_first, next_second = halves(next_row)
    return (first, second, next_first, next_second), (
        swap_seq(first, 2),
        swap_seq(second, 1),
        swap_seq(next_first, 1),
        swap_seq(next_second, 2),
    )


def gather_three(held, arrived):
    first, second, next_first, next_second = held
    first_more, second_more, next_first_more, next_second_more = arrived
    own = jnp.concatenate([first, first_more, second, second_more])
    next_first = jnp.concatenate([next_first, next_first_more])
    next_second = jnp.concatenate([next_second, next_second_more])
    return (own, next_first, next_second), (
        swap_cores(own),
        swap_seq(next_first, 2),
        swap_seq(next_second, 1),
    )


def gather_four(held, arrived):
    own, next_first, next_second = held
    other, next_first_more, next_second_more = arrived
    next_own = jnp.concatenate([next_first, next_first_more, next_second, next_second_more])
    return (own, other, next_own), swap_cores(next_own)


def row_one(block):
    first, second = halves(block)
    return swap_seq(first, 1), swap_seq(second, 2)


def row_two(block, first_more, second_more):
    first, second = halves(block)
    first = jnp.concatenate([first, first_more])
    second = jnp.concatenate([second, second_more])
    return (first, second), (swap_seq(first, 2), swap_seq(second, 1))


def row_three(held, arrived):
    own = jnp.concatenate([held[0], arrived[0], held[1], arrived[1]])
    return own, swap_cores(own)


def send_quarters(partial):
    quarter = partial.shape[0] // 4
    return swap_seq(partial[quarter : 2 * quarter], 2), swap_seq(partial[3 * quarter :], 1)


def add_quarters(partial, first, second):
    quarter = partial.shape[0] // 4
    return (
        partial[:quarter].astype(jnp.float32) + first.astype(jnp.float32),
        partial[2 * quarter : 3 * quarter].astype(jnp.float32) + second.astype(jnp.float32),
    )


def send_eighths(first, second):
    half = first.shape[0] // 2
    return (
        swap_seq(first[half:].astype(jnp.bfloat16), 1),
        swap_seq(second[half:].astype(jnp.bfloat16), 2),
    )


def add_eighths(first, second, first_more, second_more):
    half = first.shape[0] // 2
    return jnp.concatenate(
        [
            first[:half] + first_more.astype(jnp.float32),
            second[:half] + second_more.astype(jnp.float32),
        ]
    )


def add(first, second):
    return (first.astype(jnp.float32) + second.astype(jnp.float32)).astype(jnp.bfloat16)


def share_one(first, second):
    return swap_seq(first, 1), swap_seq(second, 2)


def share_two(first, second, first_more, second_more):
    first = jnp.concatenate([first, first_more])
    second = jnp.concatenate([second, second_more])
    return (first, second), (swap_seq(first, 2), swap_seq(second, 1))


def shared(held, arrived):
    return held[0], arrived[0], held[1], arrived[1]


ROWS = [[0, 2, 4, 6], [1, 3, 5, 7]]
ROW_PAIRS = [[0, 2], [4, 6], [1, 3], [5, 7]]
ROW_ORDER = (0, 2, 1, 3)


def gather_rows(block, groups):
    return lax.all_gather(block, "fsdp", axis=0, tiled=True, axis_index_groups=groups)


def scatter_rows(term, groups):
    return lax.psum_scatter(
        term.astype(jnp.bfloat16),
        "fsdp",
        scatter_dimension=0,
        tiled=True,
        axis_index_groups=groups,
    )


def lane_mask(rows):
    return lax.broadcasted_iota(jnp.int32, (rows, LANES), 1) < LANES // 2


def mixed_row(k):
    return (k & 4) | ((k & 1) << 1) | ((k & 2) >> 1)


def slice_wide(weight, gain, place, groups, chunk):
    rows = weight.shape[0]

    def body(place_ref, own_ref, other_ref, gain_ref, *out_refs):
        for weight_ref, out_ref in zip((own_ref, other_ref), out_refs):
            for step in range(2):
                start = pl.multiple_of((place_ref[2] ^ step) * chunk, LANES)
                columns = weight_ref[:, pl.ds(start, chunk)].astype(jnp.float32)
                out_ref[step] = (columns * gain_ref[...]).astype(jnp.bfloat16)

    def columns_of(core):
        return pl.BlockSpec(
            (rows, 2 * chunk), lambda k, p: (0, (mixed_row(k) * 2 + (p[1] ^ core)) * 4 + p[0])
        )

    out = jax.ShapeDtypeStruct((2, rows, groups * chunk), jnp.bfloat16)
    return pl.pallas_call(
        body,
        grid_spec=pltpu.PrefetchScalarGridSpec(
            num_scalar_prefetch=1,
            grid=(groups,),
            in_specs=[columns_of(0), columns_of(1), pl.BlockSpec((rows, 1), lambda k, p: (0, 0))],
            out_specs=[pl.BlockSpec((2, rows, chunk), lambda k, p: (0, 0, k))] * 2,
        ),
        out_shape=[out, out],
        name="slice_wide",
    )(place, weight, weight, gain)


def slice_heads(weight, gain, place, heads):
    rows = weight.shape[0]
    part = weight.shape[1] // 3

    def body(place_ref, weight_ref, gain_ref, *out_refs):
        own_seq, own_core = place_ref[0], place_ref[1]
        odd = (own_seq % 2) == 1
        low = lane_mask(rows)
        for core in range(2):
            for pair in range(heads // 2):
                tiles = []
                for head in (2 * pair, 2 * pair + 1):
                    start = (head * 2 + (own_core ^ core)) * (4 * HEAD_DIM) + (
                        own_seq // 2
                    ) * LANES
                    tile = weight_ref[:, pl.ds(pl.multiple_of(start, LANES), LANES)]
                    tiles.append(tile.astype(jnp.float32) * gain_ref[...])
                turned = [pltpu.roll(tile, LANES // 2, axis=1) for tile in tiles]
                first = jnp.where(odd, turned[0], tiles[0])
                second = jnp.where(odd, tiles[1], turned[1])
                out_refs[core][:, pair * LANES : (pair + 1) * LANES] = jnp.where(
                    low, first, second
                ).astype(jnp.bfloat16)

    out = jax.ShapeDtypeStruct((rows, 3 * heads * HEAD_DIM), jnp.bfloat16)
    return pl.pallas_call(
        body,
        grid_spec=pltpu.PrefetchScalarGridSpec(
            num_scalar_prefetch=1,
            grid=(3,),
            in_specs=[
                pl.BlockSpec((rows, part), lambda k, p: (0, k)),
                pl.BlockSpec((rows, 1), lambda k, p: (0, 0)),
            ],
            out_specs=[pl.BlockSpec((rows, heads * HEAD_DIM), lambda k, p: (0, k))] * 2,
        ),
        out_shape=[out, out],
        name="slice_heads",
    )(place, weight, gain)


def fold(products):
    total = products[:, :LANES]
    for k in range(1, products.shape[1] // LANES):
        total = total + products[:, k * LANES : (k + 1) * LANES]
    return total


PIECES = (((0, 0), (0, 2), (1, 0), (1, 2)), ((2, 0), (3, 0), (2, 2), (3, 2)))


def merge_wide(pieces, weight, gain, place, groups, chunk):
    rows = weight.shape[0]
    width = 16 * chunk

    def body(place_ref, *refs):
        weight_ref, gain_ref = refs[4:6]
        out_ref, sum_ref = refs[6:]

        @pl.when(pl.program_id(0) == 0)
        def _():
            sum_ref[...] = jnp.zeros_like(sum_ref)

        for r in range(4):
            for k in range(4):
                block = ((place_ref[1] ^ (k // 2)) * 4 + (place_ref[0] ^ r)) * 2 + (
                    place_ref[2] ^ (k % 2)
                )
                columns = pl.ds(pl.multiple_of(block * chunk, LANES), chunk)
                term = refs[PIECES[k // 2][r][0]][PIECES[k // 2][r][1] + k % 2].astype(jnp.float32)
                out_ref[:, columns] = term * gain_ref[...]
                sum_ref[place_ref[0] ^ r] += fold(
                    term * weight_ref[:, columns].astype(jnp.float32)
                )

    wide = pl.BlockSpec((rows, width), lambda k, p: (0, mixed_row(k)))
    return pl.pallas_call(
        body,
        grid_spec=pltpu.PrefetchScalarGridSpec(
            num_scalar_prefetch=1,
            grid=(groups,),
            in_specs=[pl.BlockSpec((4, rows, chunk), lambda k, p: (0, 0, k))] * 4
            + [wide, pl.BlockSpec((rows, 1), lambda k, p: (0, 0))],
            out_specs=[wide, pl.BlockSpec((4, rows, LANES), lambda k, p: (0, 0, 0))],
        ),
        out_shape=[
            jax.ShapeDtypeStruct(weight.shape, jnp.float32),
            jax.ShapeDtypeStruct((4, rows, LANES), jnp.float32),
        ],
        compiler_params=pltpu.CompilerParams(vmem_limit_bytes=32 * 1024 * 1024),
        name="merge_wide",
    )(place, *pieces, weight, gain)


def merge_heads(pieces, weight, gain, place, heads):
    rows = weight.shape[0]
    part = weight.shape[1] // 3

    def body(place_ref, *refs):
        weight_ref, gain_ref = refs[4:6]
        out_ref, sum_ref = refs[6:]
        own_seq, own_core = place_ref[0], place_ref[1]
        odd = (own_seq % 2) == 1
        low = lane_mask(rows)

        @pl.when(pl.program_id(0) == 0)
        def _():
            sum_ref[...] = jnp.zeros_like(sum_ref)

        for core in range(2):
            for pair in range(heads // 2):
                for couple in range(2):
                    first, second = (
                        refs[at][block // 2, :, pair * LANES : (pair + 1) * LANES].astype(
                            jnp.float32
                        )
                        for at, block in PIECES[core][2 * couple : 2 * couple + 2]
                    )
                    turned_first = pltpu.roll(first, LANES // 2, axis=1)
                    turned_second = pltpu.roll(second, LANES // 2, axis=1)
                    for head, even_tile, odd_tile in (
                        (
                            2 * pair,
                            jnp.where(low, first, turned_second),
                            jnp.where(low, second, turned_first),
                        ),
                        (
                            2 * pair + 1,
                            jnp.where(low, turned_first, second),
                            jnp.where(low, turned_second, first),
                        ),
                    ):
                        tile = jnp.where(odd, odd_tile, even_tile)
                        start = (head * 2 + (own_core ^ core)) * (4 * HEAD_DIM) + (
                            (own_seq // 2) ^ couple
                        ) * LANES
                        columns = pl.ds(pl.multiple_of(start, LANES), LANES)
                        out_ref[:, columns] = tile * gain_ref[...]
                        sum_ref[(own_seq // 2) ^ couple] += tile * weight_ref[:, columns].astype(
                            jnp.float32
                        )

    wide = pl.BlockSpec((rows, part), lambda k, p: (0, k))
    return pl.pallas_call(
        body,
        grid_spec=pltpu.PrefetchScalarGridSpec(
            num_scalar_prefetch=1,
            grid=(3,),
            in_specs=[pl.BlockSpec((2, rows, heads * HEAD_DIM), lambda k, p: (0, 0, k))] * 4
            + [wide, pl.BlockSpec((rows, 1), lambda k, p: (0, 0))],
            out_specs=[wide, pl.BlockSpec((2, rows, LANES), lambda k, p: (0, 0, 0))],
        ),
        out_shape=[
            jax.ShapeDtypeStruct(weight.shape, jnp.float32),
            jax.ShapeDtypeStruct((2, rows, LANES), jnp.float32),
        ],
        name="merge_heads",
    )(place, *pieces, weight, gain)


def dot_rows(left, right):
    return lax.dot_general(
        left, right, (((1,), (1,)), ((), ())), preferred_element_type=jnp.float32
    )


def swap_head_halves(values):
    lanes = lax.broadcasted_iota(jnp.int32, values.shape, 1) % HEAD_DIM
    half = HEAD_DIM // 2
    return jnp.where(
        lanes < half,
        pltpu.roll(values, LANES - half, axis=1),
        pltpu.roll(values, half, axis=1),
    )


def softmax_of(query, keys, visible):
    scores = jnp.where(visible, dot_rows(query, keys) * SCALE, -1e30)
    weights = jnp.exp(scores - jnp.max(scores, axis=1, keepdims=True))
    return weights / jnp.sum(weights, axis=1, keepdims=True)


def attend(mixed, cosine, sine, rows_at, columns_at):
    length = cosine.shape[0]
    total, columns = mixed.shape
    part = columns // 3

    def body(mixed_ref, cosine_ref, sine_ref, rows_ref, columns_ref, out_ref, turned_ref):
        visible = columns_ref[...] <= rows_ref[...]
        low = lane_mask(length)
        for k in range(2 * part // LANES):
            lanes = slice(k * LANES, (k + 1) * LANES)
            heads = mixed_ref[:, lanes].astype(jnp.float32)
            turned_ref[:, lanes] = (
                heads * cosine_ref[...] + swap_head_halves(heads) * sine_ref[...]
            ).astype(jnp.bfloat16)
        for k in range(part // LANES):
            query = turned_ref[:, k * LANES : (k + 1) * LANES]
            keys = turned_ref[:, part + k * LANES : part + (k + 1) * LANES]
            values = mixed_ref[:, 2 * part + k * LANES : 2 * part + (k + 1) * LANES]
            zero = jnp.zeros_like(query)
            outs = []
            for own in (low, ~low):
                probabilities = softmax_of(jnp.where(own, query, zero), keys, visible)
                outs.append(
                    jnp.dot(
                        probabilities.astype(jnp.bfloat16),
                        values,
                        preferred_element_type=jnp.float32,
                    )
                )
            out_ref[:, k * LANES : (k + 1) * LANES] = jnp.where(low, outs[0], outs[1]).astype(
                jnp.bfloat16
            )

    def whole(shape):
        return pl.BlockSpec(shape, lambda i: (0, 0))

    return pl.pallas_call(
        body,
        grid=(total // length,),
        in_specs=[
            pl.BlockSpec((length, columns), lambda i: (i, 0)),
            whole((length, LANES)),
            whole((length, LANES)),
            whole((length, 1)),
            whole((1, length)),
        ],
        out_specs=[
            pl.BlockSpec((length, part), lambda i: (i, 0)),
            pl.BlockSpec((length, 2 * part), lambda i: (i, 0)),
        ],
        out_shape=[
            jax.ShapeDtypeStruct((total, part), jnp.bfloat16),
            jax.ShapeDtypeStruct((total, 2 * part), jnp.bfloat16),
        ],
        compiler_params=pltpu.CompilerParams(vmem_limit_bytes=40 * 1024 * 1024),
        cost_estimate=pl.CostEstimate(
            flops=8 * total * length * part,
            bytes_accessed=12 * total * part,
            transcendentals=total * length * part // HEAD_DIM,
        ),
        name="attend",
    )(mixed, cosine, sine, rows_at, columns_at)


def attend_back(turned, mixed, grad_heads, cosine, sine, rows_at, columns_at):
    length = cosine.shape[0]
    total, columns = mixed.shape
    part = columns // 3

    def body(
        turned_ref, values_ref, grad_ref, cosine_ref, sine_ref, rows_ref, columns_ref, out_ref
    ):
        visible = columns_ref[...] <= rows_ref[...]
        low = lane_mask(length)
        for k in range(part // LANES):
            lanes = slice(k * LANES, (k + 1) * LANES)
            query = turned_ref[:, lanes]
            keys = turned_ref[:, part + k * LANES : part + (k + 1) * LANES]
            values = values_ref[:, lanes]
            grad = grad_ref[:, lanes]
            zero = jnp.zeros_like(query)
            grads = []
            for own in (low, ~low):
                probabilities = softmax_of(jnp.where(own, query, zero), keys, visible)
                grad_probabilities = dot_rows(jnp.where(own, grad, zero), values)
                inner = jnp.sum(probabilities * grad_probabilities, axis=1, keepdims=True)
                grad_scores = (probabilities * (grad_probabilities - inner)).astype(jnp.bfloat16)
                grads.append(
                    (
                        jnp.dot(grad_scores, keys, preferred_element_type=jnp.float32) * SCALE,
                        outer_sum(grad_scores, query) * SCALE,
                        outer_sum(probabilities.astype(jnp.bfloat16), grad),
                    )
                )
            for which in range(3):
                heads = jnp.where(low, grads[0][which], grads[1][which])
                if which < 2:
                    heads = heads * cosine_ref[...] - swap_head_halves(heads) * sine_ref[...]
                start = which * part + k * LANES
                out_ref[:, start : start + LANES] = heads.astype(jnp.bfloat16)

    def whole(shape):
        return pl.BlockSpec(shape, lambda i: (0, 0))

    return pl.pallas_call(
        body,
        grid=(total // length,),
        in_specs=[
            pl.BlockSpec((length, 2 * part), lambda i: (i, 0)),
            pl.BlockSpec((length, part), lambda i: (i, 2)),
            pl.BlockSpec((length, part), lambda i: (i, 0)),
            whole((length, LANES)),
            whole((length, LANES)),
            whole((length, 1)),
            whole((1, length)),
        ],
        out_specs=pl.BlockSpec((length, columns), lambda i: (i, 0)),
        out_shape=jax.ShapeDtypeStruct((total, columns), jnp.bfloat16),
        compiler_params=pltpu.CompilerParams(vmem_limit_bytes=48 * 1024 * 1024),
        cost_estimate=pl.CostEstimate(
            flops=20 * total * length * part,
            bytes_accessed=16 * total * part,
            transcendentals=total * length * part // HEAD_DIM,
        ),
        name="attend_back",
    )(turned, mixed, grad_heads, cosine, sine, rows_at, columns_at)


def place_rows(pieces, own_seq):
    rows = pieces[0].shape[0] // 2
    width = pieces[0].shape[1]
    out = jnp.zeros((8 * rows, width), jnp.float32)
    for half in range(2):
        for k in range(4):
            at, block = PIECES[half][k]
            block = pieces[at][block // 2 * rows :][:rows].astype(jnp.float32)
            out = lax.dynamic_update_slice(out, block, (((own_seq ^ k) * 2 + half) * rows, 0))
    return out


def mix_blocks(values):
    blocks = jnp.split(values, 4, axis=1)
    return jnp.concatenate([blocks[k] for k in ROW_ORDER], axis=1)


def in_order(own, other, place):
    return jnp.concatenate([jnp.where(place == 0, own, other), jnp.where(place == 0, other, own)])


def sliced_plan(hidden_in, norm_one, w_qkv, w_out, norm_two, w_gate_up, w_down, grad_out):
    own_seq = lax.axis_index("seq")
    own_core = lax.axis_index("fsdp") % 2
    row = lax.axis_index("fsdp") // 2
    step = row // 2
    place = jnp.stack([own_seq, own_core, step]).astype(jnp.int32)
    inputs = hidden_in[0].astype(jnp.float32)
    cotangent = grad_out[0]
    tokens, width = inputs.shape
    length = tokens * 4
    chunk = w_down.shape[0] // 8
    chip_rows = width // 4
    gain_one = norm_one.astype(jnp.float32)[:, None]
    gain_two = norm_two.astype(jnp.float32)[:, None]

    needed = own_seq < 4
    heads = 4

    def project(rows, weight):
        return jnp.dot(rows, weight, preferred_element_type=jnp.float32).astype(jnp.bfloat16)

    def token_part(rows, k):
        return rows[k * length : (k + 1) * length]

    def backward(grad, weight):
        return [
            back_product(token_part(grad, k), weight).astype(jnp.bfloat16)
            for k in range(grad.shape[0] // length)
        ]

    def own_rows(pair, rows):
        return (
            lax.dynamic_slice_in_dim(pair, step * rows, rows),
            lax.dynamic_slice_in_dim(pair, (1 - step) * rows, rows),
        )

    def halves_of_chip(*chips):
        half_rows = chip_rows // 2
        mine = [lax.dynamic_slice_in_dim(c, own_core * half_rows, half_rows) for c in chips]
        other = [lax.dynamic_slice_in_dim(c, (1 - own_core) * half_rows, half_rows) for c in chips]
        return jnp.stack(mine), swap_cores(jnp.stack(other))

    factor_one = lax.rsqrt(jnp.mean(inputs * inputs, axis=-1, keepdims=True) + EPSILON)
    normed, qkv_own, qkv_other = fence(
        (inputs * factor_one).astype(jnp.bfloat16), *slice_heads(w_qkv, gain_one, place, heads)
    )
    normed, qkv_chip, w_out, w_down = fence(
        normed, in_order(qkv_own, swap_cores(qkv_other), own_core), w_out, w_down
    )
    qkv = gather_rows(qkv_chip, ROWS)
    out_proj = gather_rows(lax.dynamic_slice_in_dim(w_out, own_seq * HEAD_DIM, HEAD_DIM), ROWS)

    def gather_inputs():
        flight = fence(*row_one(normed))
        held, flight = row_two(normed, *flight)
        wide_own, wide_other = slice_wide(w_gate_up, gain_two, place, 8, chunk)
        *flight, wide_own, wide_other = fence(*flight, wide_own, wide_other)
        own, other = row_three(held, flight)
        other, *flight, wide_swapped = fence(other, *row_one(cotangent), swap_cores(wide_other))
        held, flight = row_two(cotangent, *flight)
        flight = fence(*flight)
        cotangent_own, cotangent_other = row_three(held, flight)
        return (
            jnp.concatenate([own, other]),
            [in_order(wide_own[k], wide_swapped[k], own_core) for k in range(2)],
            cotangent_own,
            *fence(cotangent_other),
        )

    normed_all, wide_chips, cotangent_own, cotangent_other = window(needed, gather_inputs)

    half_block = tokens // 2
    starts = jnp.concatenate(
        [
            (own_seq ^ jnp.array([0, 1, 2, 3])) * tokens,
            (own_seq ^ jnp.array([0, 2, 1, 3])) * tokens + half_block,
        ]
    )
    positions = (starts[:, None] + jnp.arange(half_block)[None]).reshape(length)
    half = HEAD_DIM // 2
    freqs = THETA ** (-(jnp.arange(half, dtype=jnp.float32) * 2.0) / HEAD_DIM)
    angles = positions.astype(jnp.float32)[:, None] * freqs[None, :]
    cosine = jnp.tile(jnp.cos(angles), (1, 4))
    sine = jnp.tile(jnp.concatenate([-jnp.sin(angles), jnp.sin(angles)], axis=1), (1, 2))
    tables = (cosine, sine, positions[:, None], positions[None, :])

    def norm_two_of(middle):
        factor = lax.rsqrt(jnp.mean(middle * middle, axis=-1, keepdims=True) + EPSILON)
        return mix_blocks((middle * factor).astype(jnp.bfloat16)), factor

    def attention():
        mixed = project(normed_all, qkv)
        return mixed, *attend(mixed, *tables)

    mixed, attended, turned = window(needed, attention)
    attended, out_proj, wide_send, cotangent_send, w_down = fence(
        attended, out_proj, wide_chips[1], cotangent, w_down
    )
    cotangent_next = swap_rows(cotangent_send, 2)
    wide_more = swap_rows(wide_send, 2)
    down_rows = [
        lax.dynamic_slice_in_dim(w_down, own_seq * 2 * chunk + (step ^ k) * chunk, chunk)
        for k in range(2)
    ]

    def attention_out():
        other = project(token_part(attended, 1), out_proj)
        own = project(token_part(attended, 0), out_proj)
        swapped, own = fence(swap_cores(other), own)
        own = add(own, swapped)
        flight = fence(*send_quarters(own))
        own = add_quarters(own, *flight)
        flight = fence(*send_eighths(*own))
        middle = inputs + add_eighths(*own, *flight)
        return middle, norm_two_of(middle)[0]

    middle, normed_two = window(needed, attention_out)
    wide_more, cotangent_next, normed_two = fence(wide_more, cotangent_next, normed_two)
    gate_up_w = gather_rows(in_order(wide_chips[0], wide_more, step), ROW_PAIRS)

    def gather_middle():
        *flight, first, second = fence(*gather_one(normed_two), *row_one(cotangent_next))
        cotangent_held, cotangent_flight = row_two(cotangent_next, first, second)
        held, flight = gather_two(normed_two, *flight)
        *flight, down_more = fence(*flight, swap_rows(down_rows[1], 2))
        held, flight = gather_three(held, flight)
        *flight, first, second = fence(*flight, *cotangent_flight)
        held, last = gather_four(held, flight)
        next_own, next_other = row_three(cotangent_held, (first, second))
        last, next_other = fence(last, next_other)
        return (
            jnp.concatenate([*held, last]),
            in_order(down_rows[0], down_more, step),
            next_own,
            next_other,
        )

    normed_two_all, down_pair, *cotangent_parts = window(needed, gather_middle)
    down = gather_rows(down_pair, ROW_PAIRS)

    _, factor_two = norm_two_of(middle)
    cotangent_all = jnp.concatenate([cotangent_own, cotangent_other, *cotangent_parts])
    gate_up = jnp.dot(normed_two_all, gate_up_w, preferred_element_type=jnp.float32)
    units = gate_up.shape[1] // 2
    gate, upward = gate_up[:, :units], gate_up[:, units:]
    sigmoid = jax.nn.sigmoid(gate)
    activated = gate * sigmoid
    hidden = (activated * upward).astype(jnp.bfloat16)
    hidden, cotangent_all = fence(hidden, cotangent_all)
    forward_far, forward_other = project(token_part(hidden, 2), down), project(
        token_part(hidden, 3), down
    )
    forward_far, forward_other = fence(forward_far, forward_other)
    grad_hidden = back_product(cotangent_all, down)
    grad_gate = grad_hidden * upward * sigmoid * (1.0 + gate * (1.0 - sigmoid))
    grad_upward = grad_hidden * activated
    grad_low = jnp.concatenate([grad_gate, grad_upward], axis=1).astype(jnp.bfloat16)
    grad_low, swapped = fence(grad_low, swap_cores(forward_other))
    forward_far = add(forward_far, swapped)
    forward_near, forward_other = project(token_part(hidden, 0), down), project(
        token_part(hidden, 1), down
    )

    def backward_part(grad, weight, k):
        return back_product(token_part(grad, k), weight).astype(jnp.bfloat16)

    far, far_other, forward_near, forward_other, *flight = fence(
        backward_part(grad_low, gate_up_w, 2),
        backward_part(grad_low, gate_up_w, 3),
        forward_near,
        forward_other,
        *send_quarters(forward_far),
    )
    forward_far = add_quarters(forward_far, *flight)
    grad_down_term = outer_sum(hidden, cotangent_all).astype(jnp.bfloat16)
    swapped, far, near, near_other, grad_down_term, forward_swapped, *flight = fence(
        swap_cores(far_other),
        far,
        backward_part(grad_low, gate_up_w, 0),
        backward_part(grad_low, gate_up_w, 1),
        grad_down_term,
        swap_cores(forward_other),
        *send_eighths(*forward_far),
    )
    far = add(far, swapped)
    forward_near = add(forward_near, forward_swapped)
    forward_far = add_eighths(*forward_far, *flight).astype(jnp.bfloat16)
    grad_down_pair = scatter_rows(grad_down_term, ROW_PAIRS)
    grad_gate_up_term = outer_sum(normed_two_all, grad_low).astype(jnp.bfloat16)
    *flight, swapped, grad_gate_up_term = fence(
        *send_quarters(far), swap_cores(near_other), grad_gate_up_term
    )
    far = add_quarters(far, *flight)
    near = add(near, swapped)
    grad_gate_up_pair = scatter_rows(grad_gate_up_term, ROW_PAIRS)

    def feed_forward_back():
        *flight, first, second = fence(*send_eighths(*far), *send_quarters(near))
        next_row = add_eighths(*far, *flight).astype(jnp.bfloat16)
        quarters = add_quarters(near, first, second)
        next_row, first, second, *flight = fence(
            swap_rows(next_row, 2), *send_eighths(*quarters), *send_quarters(forward_near)
        )
        scaled = mix_blocks(add_eighths(*quarters, first, second) + next_row.astype(jnp.float32))
        forward_quarters = add_quarters(forward_near, *flight)
        grad_middle = (
            cotangent.astype(jnp.float32)
            + factor_two * scaled
            - middle * factor_two**3 * jnp.mean(scaled * middle, axis=-1, keepdims=True)
        )
        block = grad_middle.astype(jnp.bfloat16)
        down_own, down_send = own_rows(grad_down_pair, chunk)
        *flight, first, second, forward_next = fence(
            *row_one(block), *send_eighths(*forward_quarters), swap_rows(forward_far, 2)
        )
        output = middle + forward_next.astype(jnp.float32)
        output = output + add_eighths(*forward_quarters, first, second)
        held, flight = row_two(block, *flight)
        *flight, down_more = fence(*flight, swap_rows(down_send, 2))
        own, other = row_three(held, flight)
        down_halves = halves(in_order(down_own, down_more, step))
        return jnp.concatenate([own, *fence(other)]), grad_middle, output, down_halves

    grad_branch, grad_middle, output, down_halves = window(needed, feed_forward_back)

    wide_own, wide_send = own_rows(grad_gate_up_pair, chip_rows)
    grad_branch, wide_send = fence(grad_branch, wide_send)
    wide_more = swap_rows(wide_send, 2)

    def attention_back():
        grad_heads = back_product(grad_branch, out_proj).astype(jnp.bfloat16)
        grad_mixed = attend_back(turned, mixed, grad_heads, *tables)
        grad_mixed, *flight = fence(grad_mixed, *share_one(*down_halves))
        held, flight = share_two(*down_halves, *flight)
        grad_qkv_term = outer_sum(normed_all, grad_mixed).astype(jnp.bfloat16)
        return grad_mixed, grad_qkv_term, shared(held, fence(*flight))

    grad_mixed, grad_qkv_term, down_pieces = window(needed, attention_back)
    grad_qkv_term, wide_more = fence(grad_qkv_term, wide_more)
    grad_qkv_rows = scatter_rows(grad_qkv_term, ROWS)
    grad_out_rows = scatter_rows(outer_sum(attended, grad_branch), ROWS)

    def inputs_back():
        back = backward(grad_mixed, qkv)
        mine, swapped = halves_of_chip(wide_own, wide_more)
        swapped, row_swapped, near = fence(swapped, swap_cores(back[1]), back[0])
        near = add(near, row_swapped)
        wide_halves = mine, swapped
        *row_flight, first, second = fence(*send_quarters(near), *share_one(*wide_halves))
        near = add_quarters(near, *row_flight)
        scaled = add_eighths(*near, *fence(*send_eighths(*near)))
        grad_inputs = (
            grad_middle
            + factor_one * scaled
            - inputs * factor_one**3 * jnp.mean(scaled * inputs, axis=-1, keepdims=True)
        )
        return grad_inputs, wide_halves, (first, second)

    grad_inputs, wide_halves, wide_flight = window(needed, inputs_back)

    wide_held, wide_flight = share_two(*wide_halves, *wide_flight)
    grad_qkv_rows, grad_inputs = fence(grad_qkv_rows, grad_inputs)
    qkv_halves = fence(*halves_of_chip(grad_qkv_rows))
    out_halves = halves(grad_out_rows)
    *qkv_flight, first, second = fence(*share_one(*qkv_halves), *share_one(*out_halves))
    qkv_held, qkv_flight = share_two(*qkv_halves, *qkv_flight)
    out_held, out_flight = share_two(*out_halves, first, second)
    grad_gate_up, gain_two_sums = merge_wide(
        shared(wide_held, wide_flight), w_gate_up, gain_two, place, 8, chunk
    )
    grad_qkv, gain_one_sums = merge_heads(
        shared(qkv_held, qkv_flight), w_qkv, gain_one, place, heads
    )
    return (
        output.astype(jnp.bfloat16)[None],
        grad_inputs[None],
        jnp.sum(gain_one_sums, axis=(0, 2)),
        grad_qkv,
        place_rows(shared(out_held, out_flight), own_seq),
        jnp.sum(gain_two_sums, axis=(0, 2)),
        grad_gate_up,
        place_rows(down_pieces, own_seq),
    )


def solution(mesh):
    seq, fsdp = mesh.shape["seq"], mesh.shape["fsdp"]

    def on_device(hidden_in, norm_one, w_qkv, w_out, norm_two, w_gate_up, w_down, grad_out):
        arrays = (hidden_in, norm_one, w_qkv, w_out, norm_two, w_gate_up, w_down, grad_out)
        if seq == 4 and fsdp == 8 and w_out.shape[0] == 4 * HEAD_DIM and w_down.shape[0] % 1024 == 0:
            return sliced_plan(*arrays)
        return gathered_plan(*arrays)

    placed = (
        P("fsdp", "seq", None),
        P("fsdp"),
        P("fsdp", None),
        P("fsdp", None),
        P("fsdp"),
        P("fsdp", None),
        P("fsdp", None),
        P("fsdp", "seq", None),
    )
    return jax.shard_map(
        on_device,
        mesh=mesh,
        in_specs=placed,
        out_specs=(
            P("fsdp", "seq", None),
            P("fsdp", "seq", None),
            P("fsdp"),
            P("fsdp", None),
            P("fsdp", None),
            P("fsdp"),
            P("fsdp", None),
            P("fsdp", None),
        ),
        check_vma=False,
    )
```

```python
import functools

import jax
import jax.numpy as jnp
from jax import lax
from jax.experimental import pallas as pl
from jax.experimental.pallas import tpu as pltpu
from jax.sharding import PartitionSpec as P

HEAD_DIM = 64


EPSILON = 1e-05
THETA = 130000.0
SCALE = 0.125
LANES = 128


def outer_sum(left, right):
    return lax.dot_general(
        left, right, (((0,), (0,)), ((), ())), preferred_element_type=jnp.float32
    )


def back_product(grad, weight):
    return lax.dot_general(
        grad, weight, (((1,), (1,)), ((), ())), preferred_element_type=jnp.float32
    )


def rope_tables(length):
    half = HEAD_DIM // 2
    freqs = THETA ** (-(jnp.arange(half, dtype=jnp.float32) * 2.0) / HEAD_DIM)
    angles = jnp.arange(length, dtype=jnp.float32)[:, None] * freqs[None, :]
    angles = jnp.concatenate([angles, angles], axis=1)
    return (jnp.cos(angles)[:, None, :], jnp.sin(angles)[:, None, :])


def rotate(values, cosine, sine):
    half = values.shape[-1] // 2
    turned = jnp.concatenate([-values[..., half:], values[..., :half]], axis=-1)
    return values * cosine + turned * sine


def unrotate(grads, cosine, sine):
    half = grads.shape[-1] // 2
    scaled = grads * sine
    turned = jnp.concatenate([scaled[..., half:], -scaled[..., :half]], axis=-1)
    return grads * cosine + turned


def norm_forward(values, gain):
    factor = lax.rsqrt(jnp.mean(values * values, axis=-1, keepdims=True) + EPSILON)
    return (values * factor * gain, factor)


def norm_backward(values, factor, gain, grad):
    grad_gain = jnp.sum(grad * values * factor, axis=0)
    scaled = grad * gain
    grad_values = factor * scaled - values * factor**3 * jnp.mean(
        scaled * values, axis=-1, keepdims=True
    )
    return (grad_values, grad_gain)


def fetch_rows(gain, first, second):
    return (
        lax.all_gather(gain, "fsdp", axis=0, tiled=True),
        lax.all_gather(first, "fsdp", axis=0, tiled=True),
        lax.all_gather(second, "fsdp", axis=0, tiled=True),
    )


def weight_term(left, right):
    return outer_sum(left, right)


def reduce_grads(terms):
    partial_sums = (
        lax.psum_scatter(
            terms[0].astype(jnp.bfloat16), "fsdp", scatter_dimension=0, tiled=True
        ).astype(jnp.float32),
        lax.psum_scatter(
            terms[1].astype(jnp.bfloat16), "fsdp", scatter_dimension=0, tiled=True
        ).astype(jnp.float32),
    )
    return (
        lax.psum(partial_sums[0].astype(jnp.bfloat16), "seq").astype(jnp.float32),
        lax.psum(partial_sums[1].astype(jnp.bfloat16), "seq").astype(jnp.float32),
    )


def block_scores(query_block, key_rows, offset):
    scores = (
        jnp.einsum("qhd,khd->hqk", query_block, key_rows, preferred_element_type=jnp.float32)
        * SCALE
    )
    rows = offset + jnp.arange(query_block.shape[0])[:, None]
    columns = jnp.arange(key_rows.shape[0])[None, :]
    return jnp.where((columns <= rows)[None], scores, -1e30)


def gathered_plan(hidden_in, norm_one, w_qkv, w_out, norm_two, w_gate_up, w_down, grad_out):
    inputs = hidden_in[0].astype(jnp.float32)
    tokens = inputs.shape[0]
    width = inputs.shape[1]
    gain_one, qkv_full, out_full = fetch_rows(norm_one, w_qkv, w_out)
    normed, factor_one = norm_forward(inputs, gain_one.astype(jnp.float32))
    normed_low = normed.astype(jnp.bfloat16)
    mixed = jnp.dot(normed_low, qkv_full, preferred_element_type=jnp.float32).astype(jnp.bfloat16)
    regrouped = lax.all_to_all(
        mixed.reshape(tokens, 3, width), "seq", split_axis=2, concat_axis=0, tiled=True
    )
    length = regrouped.shape[0]
    local_width = regrouped.shape[2]
    heads = local_width // HEAD_DIM
    regrouped = regrouped.reshape(length, 3, heads, HEAD_DIM)
    cosine, sine = rope_tables(length)
    query = rotate(regrouped[:, 0].astype(jnp.float32), cosine, sine).astype(jnp.bfloat16)
    keys = rotate(regrouped[:, 1].astype(jnp.float32), cosine, sine).astype(jnp.bfloat16)
    values = regrouped[:, 2]
    block = min(512, length)
    attended_parts = []
    logsums = []
    for start in range(0, length, block):
        stop = start + block
        scores = block_scores(query[start:stop], keys[:stop], start)
        highest = jnp.max(scores, axis=-1, keepdims=True)
        weights = jnp.exp(scores - highest)
        total = jnp.sum(weights, axis=-1, keepdims=True)
        probabilities = (weights / total).astype(jnp.bfloat16)
        logsums.append(highest + jnp.log(total))
        attended_parts.append(
            jnp.einsum(
                "hqk,khd->qhd", probabilities, values[:stop], preferred_element_type=jnp.float32
            )
        )
    attended = (
        jnp.concatenate(attended_parts, axis=0).reshape(length, local_width).astype(jnp.bfloat16)
    )
    back_rows = lax.all_to_all(attended, "seq", split_axis=0, concat_axis=1, tiled=True)
    middle = inputs + jnp.dot(back_rows, out_full, preferred_element_type=jnp.float32)
    gain_two, gate_up_full, down_full = fetch_rows(norm_two, w_gate_up, w_down)
    normed_two, factor_two = norm_forward(middle, gain_two.astype(jnp.float32))
    normed_two_low = normed_two.astype(jnp.bfloat16)
    gate_up = jnp.dot(normed_two_low, gate_up_full, preferred_element_type=jnp.float32)
    hidden_units = gate_up.shape[1] // 2
    gate = gate_up[:, :hidden_units]
    upward = gate_up[:, hidden_units:]
    sigmoid = jax.nn.sigmoid(gate)
    activated = gate * sigmoid
    hidden = (activated * upward).astype(jnp.bfloat16)
    output = middle + jnp.dot(hidden, down_full, preferred_element_type=jnp.float32)
    cotangent = grad_out[0]
    grad_hidden = back_product(cotangent, down_full)
    grad_gate = grad_hidden * upward * sigmoid * (1.0 + gate * (1.0 - sigmoid))
    grad_upward = grad_hidden * activated
    grad_gate_up_low = jnp.concatenate([grad_gate, grad_upward], axis=1).astype(jnp.bfloat16)
    grad_normed_two = back_product(grad_gate_up_low, gate_up_full)
    middle_part, grad_gain_two = norm_backward(
        middle, factor_two, gain_two.astype(jnp.float32), grad_normed_two
    )
    grad_middle = cotangent.astype(jnp.float32) + middle_part
    grad_gate_up_term = weight_term(normed_two_low, grad_gate_up_low)
    grad_branch = grad_middle.astype(jnp.bfloat16)
    grad_out_term = weight_term(back_rows, grad_branch)
    grad_down_term = weight_term(hidden, cotangent)
    grad_down_sum, gain_two_sum = reduce_grads((grad_down_term, grad_gain_two))
    gate_up_sum, out_proj_sum = reduce_grads((grad_gate_up_term, grad_out_term))
    gain_one, qkv_full, out_full = fetch_rows(norm_one, w_qkv, w_out)
    grad_attended = back_product(grad_branch, out_full).astype(jnp.bfloat16)
    grad_heads = lax.all_to_all(
        grad_attended, "seq", split_axis=1, concat_axis=0, tiled=True
    ).reshape(length, heads, HEAD_DIM)
    query_parts = []
    grad_keys = jnp.zeros((length, heads, HEAD_DIM), jnp.float32)
    grad_values = jnp.zeros((length, heads, HEAD_DIM), jnp.float32)
    for index, start in enumerate(range(0, length, block)):
        stop = start + block
        query_block = query[start:stop]
        grad_block = grad_heads[start:stop]
        scores = block_scores(query_block, keys[:stop], start)
        probabilities = jnp.exp(scores - logsums[index])
        grad_probabilities = jnp.einsum(
            "qhd,khd->hqk", grad_block, values[:stop], preferred_element_type=jnp.float32
        )
        inner = jnp.sum(probabilities * grad_probabilities, axis=-1, keepdims=True)
        grad_scores = (probabilities * (grad_probabilities - inner)).astype(jnp.bfloat16)
        query_parts.append(
            jnp.einsum("hqk,khd->qhd", grad_scores, keys[:stop], preferred_element_type=jnp.float32)
            * SCALE
        )
        key_term = (
            jnp.einsum("hqk,qhd->khd", grad_scores, query_block, preferred_element_type=jnp.float32)
            * SCALE
        )
        value_term = jnp.einsum(
            "hqk,qhd->khd",
            probabilities.astype(jnp.bfloat16),
            grad_block,
            preferred_element_type=jnp.float32,
        )
        grad_keys = grad_keys.at[:stop].add(key_term)
        grad_values = grad_values.at[:stop].add(value_term)
    grad_query = unrotate(jnp.concatenate(query_parts, axis=0), cosine, sine)
    grad_keys = unrotate(grad_keys, cosine, sine)
    stacked = (
        jnp.stack([grad_query, grad_keys, grad_values], axis=1)
        .astype(jnp.bfloat16)
        .reshape(length, 3, local_width)
    )
    grad_mixed = lax.all_to_all(stacked, "seq", split_axis=0, concat_axis=2, tiled=True).reshape(
        tokens, 3 * width
    )
    grad_qkv_term = weight_term(normed_low, grad_mixed)
    grad_normed_one = back_product(grad_mixed, qkv_full)
    input_part, grad_gain_one = norm_backward(
        inputs, factor_one, gain_one.astype(jnp.float32), grad_normed_one
    )
    grad_inputs = grad_middle + input_part
    qkv_sum, gain_one_sum = reduce_grads((grad_qkv_term, grad_gain_one))
    return (
        output.astype(jnp.bfloat16)[None],
        grad_inputs[None],
        gain_one_sum,
        qkv_sum,
        out_proj_sum,
        gain_two_sum,
        gate_up_sum,
        grad_down_sum,
    )


def xor_pairs(size, offset):
    return [(i, i ^ offset) for i in range(size)]


def swap_cores(values):
    return lax.ppermute(values, "fsdp", xor_pairs(8, 1))


def swap_rows(values, offset):
    return lax.ppermute(values, "fsdp", xor_pairs(8, 2 * offset))


def swap_seq(values, offset):
    return lax.ppermute(values, "seq", xor_pairs(4, offset))


def fence(*values):
    return lax.optimization_barrier(values)


def window(needed, work):
    outs = jax.eval_shape(work)
    return lax.cond(
        needed,
        work,
        lambda: jax.tree.map(lambda out: jnp.zeros(out.shape, out.dtype), outs),
    )


def halves(block):
    half = block.shape[0] // 2
    return block[:half], block[half:]


def gather_one(block):
    first, second = halves(block)
    return swap_seq(first, 1), swap_seq(second, 2), swap_rows(block, 2)


def gather_two(block, first_more, second_more, next_row):
    first, second = halves(block)
    first = jnp.concatenate([first, first_more])
    second = jnp.concatenate([second, second_more])
    next_first, next_second = halves(next_row)
    return (first, second, next_first, next_second), (
        swap_seq(first, 2),
        swap_seq(second, 1),
        swap_seq(next_first, 1),
        swap_seq(next_second, 2),
    )


def gather_three(held, arrived):
    first, second, next_first, next_second = held
    first_more, second_more, next_first_more, next_second_more = arrived
    own = jnp.concatenate([first, first_more, second, second_more])
    next_first = jnp.concatenate([next_first, next_first_more])
    next_second = jnp.concatenate([next_second, next_second_more])
    return (own, next_first, next_second), (
        swap_cores(own),
        swap_seq(next_first, 2),
        swap_seq(next_second, 1),
    )


def gather_four(held, arrived):
    own, next_first, next_second = held
    other, next_first_more, next_second_more = arrived
    next_own = jnp.concatenate([next_first, next_first_more, next_second, next_second_more])
    return (own, other, next_own), swap_cores(next_own)


def row_one(block):
    first, second = halves(block)
    return swap_seq(first, 1), swap_seq(second, 2)


def row_two(block, first_more, second_more):
    first, second = halves(block)
    first = jnp.concatenate([first, first_more])
    second = jnp.concatenate([second, second_more])
    return (first, second), (swap_seq(first, 2), swap_seq(second, 1))


def row_three(held, arrived):
    own = jnp.concatenate([held[0], arrived[0], held[1], arrived[1]])
    return own, swap_cores(own)


def send_quarters(partial):
    quarter = partial.shape[0] // 4
    return swap_seq(partial[quarter : 2 * quarter], 2), swap_seq(partial[3 * quarter :], 1)


def add_quarters(partial, first, second):
    quarter = partial.shape[0] // 4
    return (
        partial[:quarter].astype(jnp.float32) + first.astype(jnp.float32),
        partial[2 * quarter : 3 * quarter].astype(jnp.float32) + second.astype(jnp.float32),
    )


def send_eighths(first, second):
    half = first.shape[0] // 2
    return (
        swap_seq(first[half:].astype(jnp.bfloat16), 1),
        swap_seq(second[half:].astype(jnp.bfloat16), 2),
    )


def add_eighths(first, second, first_more, second_more):
    half = first.shape[0] // 2
    return jnp.concatenate(
        [
            first[:half] + first_more.astype(jnp.float32),
            second[:half] + second_more.astype(jnp.float32),
        ]
    )


def add(first, second):
    return (first.astype(jnp.float32) + second.astype(jnp.float32)).astype(jnp.bfloat16)


def share_one(first, second):
    return swap_seq(first, 1), swap_seq(second, 2)


def share_two(first, second, first_more, second_more):
    first = jnp.concatenate([first, first_more])
    second = jnp.concatenate([second, second_more])
    return (first, second), (swap_seq(first, 2), swap_seq(second, 1))


def shared(held, arrived):
    return held[0], arrived[0], held[1], arrived[1]


ROWS = [[0, 2, 4, 6], [1, 3, 5, 7]]
ROW_PAIRS = [[0, 2], [4, 6], [1, 3], [5, 7]]
ROW_ORDER = (0, 2, 1, 3)


def gather_rows(block, groups):
    return lax.all_gather(block, "fsdp", axis=0, tiled=True, axis_index_groups=groups)


def scatter_rows(term, groups):
    return lax.psum_scatter(
        term.astype(jnp.bfloat16),
        "fsdp",
        scatter_dimension=0,
        tiled=True,
        axis_index_groups=groups,
    )


def lane_mask(rows):
    return lax.broadcasted_iota(jnp.int32, (rows, LANES), 1) < LANES // 2


def mixed_row(k):
    return (k & 4) | ((k & 1) << 1) | ((k & 2) >> 1)


def slice_wide(weight, gain, place, groups, chunk):
    rows = weight.shape[0]

    def body(place_ref, own_ref, other_ref, gain_ref, *out_refs):
        for weight_ref, out_ref in zip((own_ref, other_ref), out_refs):
            for step in range(2):
                start = pl.multiple_of((place_ref[2] ^ step) * chunk, LANES)
                columns = weight_ref[:, pl.ds(start, chunk)].astype(jnp.float32)
                out_ref[step] = (columns * gain_ref[...]).astype(jnp.bfloat16)

    def columns_of(core):
        return pl.BlockSpec(
            (rows, 2 * chunk), lambda k, p: (0, (mixed_row(k) * 2 + (p[1] ^ core)) * 4 + p[0])
        )

    out = jax.ShapeDtypeStruct((2, rows, groups * chunk), jnp.bfloat16)
    return pl.pallas_call(
        body,
        grid_spec=pltpu.PrefetchScalarGridSpec(
            num_scalar_prefetch=1,
            grid=(groups,),
            in_specs=[columns_of(0), columns_of(1), pl.BlockSpec((rows, 1), lambda k, p: (0, 0))],
            out_specs=[pl.BlockSpec((2, rows, chunk), lambda k, p: (0, 0, k))] * 2,
        ),
        out_shape=[out, out],
        name="slice_wide",
    )(place, weight, weight, gain)


def slice_heads(weight, gain, place, heads):
    rows = weight.shape[0]
    part = weight.shape[1] // 3

    def body(place_ref, weight_ref, gain_ref, *out_refs):
        own_seq, own_core = place_ref[0], place_ref[1]
        odd = (own_seq % 2) == 1
        low = lane_mask(rows)
        for core in range(2):
            for pair in range(heads // 2):
                tiles = []
                for head in (2 * pair, 2 * pair + 1):
                    start = (head * 2 + (own_core ^ core)) * (4 * HEAD_DIM) + (
                        own_seq // 2
                    ) * LANES
                    tile = weight_ref[:, pl.ds(pl.multiple_of(start, LANES), LANES)]
                    tiles.append(tile.astype(jnp.float32) * gain_ref[...])
                turned = [pltpu.roll(tile, LANES // 2, axis=1) for tile in tiles]
                first = jnp.where(odd, turned[0], tiles[0])
                second = jnp.where(odd, tiles[1], turned[1])
                out_refs[core][:, pair * LANES : (pair + 1) * LANES] = jnp.where(
                    low, first, second
                ).astype(jnp.bfloat16)

    out = jax.ShapeDtypeStruct((rows, 3 * heads * HEAD_DIM), jnp.bfloat16)
    return pl.pallas_call(
        body,
        grid_spec=pltpu.PrefetchScalarGridSpec(
            num_scalar_prefetch=1,
            grid=(3,),
            in_specs=[
                pl.BlockSpec((rows, part), lambda k, p: (0, k)),
                pl.BlockSpec((rows, 1), lambda k, p: (0, 0)),
            ],
            out_specs=[pl.BlockSpec((rows, heads * HEAD_DIM), lambda k, p: (0, k))] * 2,
        ),
        out_shape=[out, out],
        name="slice_heads",
    )(place, weight, gain)


def fold(products):
    total = products[:, :LANES]
    for k in range(1, products.shape[1] // LANES):
        total = total + products[:, k * LANES : (k + 1) * LANES]
    return total


PIECES = (((0, 0), (0, 2), (1, 0), (1, 2)), ((2, 0), (3, 0), (2, 2), (3, 2)))


def merge_wide(pieces, weight, gain, place, groups, chunk):
    rows = weight.shape[0]
    width = 16 * chunk

    def body(place_ref, *refs):
        weight_ref, gain_ref = refs[4:6]
        out_ref, sum_ref = refs[6:]

        @pl.when(pl.program_id(0) == 0)
        def _():
            sum_ref[...] = jnp.zeros_like(sum_ref)

        for r in range(4):
            for k in range(4):
                block = ((place_ref[1] ^ (k // 2)) * 4 + (place_ref[0] ^ r)) * 2 + (
                    place_ref[2] ^ (k % 2)
                )
                columns = pl.ds(pl.multiple_of(block * chunk, LANES), chunk)
                term = refs[PIECES[k // 2][r][0]][PIECES[k // 2][r][1] + k % 2].astype(jnp.float32)
                out_ref[:, columns] = term * gain_ref[...]
                sum_ref[place_ref[0] ^ r] += fold(
                    term * weight_ref[:, columns].astype(jnp.float32)
                )

    wide = pl.BlockSpec((rows, width), lambda k, p: (0, mixed_row(k)))
    return pl.pallas_call(
        body,
        grid_spec=pltpu.PrefetchScalarGridSpec(
            num_scalar_prefetch=1,
            grid=(groups,),
            in_specs=[pl.BlockSpec((4, rows, chunk), lambda k, p: (0, 0, k))] * 4
            + [wide, pl.BlockSpec((rows, 1), lambda k, p: (0, 0))],
            out_specs=[wide, pl.BlockSpec((4, rows, LANES), lambda k, p: (0, 0, 0))],
        ),
        out_shape=[
            jax.ShapeDtypeStruct(weight.shape, jnp.float32),
            jax.ShapeDtypeStruct((4, rows, LANES), jnp.float32),
        ],
        compiler_params=pltpu.CompilerParams(vmem_limit_bytes=32 * 1024 * 1024),
        name="merge_wide",
    )(place, *pieces, weight, gain)


def merge_heads(pieces, weight, gain, place, heads):
    rows = weight.shape[0]
    part = weight.shape[1] // 3

    def body(place_ref, *refs):
        weight_ref, gain_ref = refs[4:6]
        out_ref, sum_ref = refs[6:]
        own_seq, own_core = place_ref[0], place_ref[1]
        odd = (own_seq % 2) == 1
        low = lane_mask(rows)

        @pl.when(pl.program_id(0) == 0)
        def _():
            sum_ref[...] = jnp.zeros_like(sum_ref)

        for core in range(2):
            for pair in range(heads // 2):
                for couple in range(2):
                    first, second = (
                        refs[at][block // 2, :, pair * LANES : (pair + 1) * LANES].astype(
                            jnp.float32
                        )
                        for at, block in PIECES[core][2 * couple : 2 * couple + 2]
                    )
                    turned_first = pltpu.roll(first, LANES // 2, axis=1)
                    turned_second = pltpu.roll(second, LANES // 2, axis=1)
                    for head, even_tile, odd_tile in (
                        (
                            2 * pair,
                            jnp.where(low, first, turned_second),
                            jnp.where(low, second, turned_first),
                        ),
                        (
                            2 * pair + 1,
                            jnp.where(low, turned_first, second),
                            jnp.where(low, turned_second, first),
                        ),
                    ):
                        tile = jnp.where(odd, odd_tile, even_tile)
                        start = (head * 2 + (own_core ^ core)) * (4 * HEAD_DIM) + (
                            (own_seq // 2) ^ couple
                        ) * LANES
                        columns = pl.ds(pl.multiple_of(start, LANES), LANES)
                        out_ref[:, columns] = tile * gain_ref[...]
                        sum_ref[(own_seq // 2) ^ couple] += tile * weight_ref[:, columns].astype(
                            jnp.float32
                        )

    wide = pl.BlockSpec((rows, part), lambda k, p: (0, k))
    return pl.pallas_call(
        body,
        grid_spec=pltpu.PrefetchScalarGridSpec(
            num_scalar_prefetch=1,
            grid=(3,),
            in_specs=[pl.BlockSpec((2, rows, heads * HEAD_DIM), lambda k, p: (0, 0, k))] * 4
            + [wide, pl.BlockSpec((rows, 1), lambda k, p: (0, 0))],
            out_specs=[wide, pl.BlockSpec((2, rows, LANES), lambda k, p: (0, 0, 0))],
        ),
        out_shape=[
            jax.ShapeDtypeStruct(weight.shape, jnp.float32),
            jax.ShapeDtypeStruct((2, rows, LANES), jnp.float32),
        ],
        name="merge_heads",
    )(place, *pieces, weight, gain)


def dot_rows(left, right):
    return lax.dot_general(
        left, right, (((1,), (1,)), ((), ())), preferred_element_type=jnp.float32
    )


def swap_head_halves(values):
    lanes = lax.broadcasted_iota(jnp.int32, values.shape, 1) % HEAD_DIM
    half = HEAD_DIM // 2
    return jnp.where(
        lanes < half,
        pltpu.roll(values, LANES - half, axis=1),
        pltpu.roll(values, half, axis=1),
    )


def softmax_of(query, keys, visible):
    scores = jnp.where(visible, dot_rows(query, keys) * SCALE, -1e30)
    weights = jnp.exp(scores - jnp.max(scores, axis=1, keepdims=True))
    return weights / jnp.sum(weights, axis=1, keepdims=True)


def attend(mixed, cosine, sine, rows_at, columns_at):
    length = cosine.shape[0]
    total, columns = mixed.shape
    part = columns // 3

    def body(mixed_ref, cosine_ref, sine_ref, rows_ref, columns_ref, out_ref, turned_ref):
        visible = columns_ref[...] <= rows_ref[...]
        low = lane_mask(length)
        for k in range(2 * part // LANES):
            lanes = slice(k * LANES, (k + 1) * LANES)
            heads = mixed_ref[:, lanes].astype(jnp.float32)
            turned_ref[:, lanes] = (
                heads * cosine_ref[...] + swap_head_halves(heads) * sine_ref[...]
            ).astype(jnp.bfloat16)
        for k in range(part // LANES):
            query = turned_ref[:, k * LANES : (k + 1) * LANES]
            keys = turned_ref[:, part + k * LANES : part + (k + 1) * LANES]
            values = mixed_ref[:, 2 * part + k * LANES : 2 * part + (k + 1) * LANES]
            zero = jnp.zeros_like(query)
            outs = []
            for own in (low, ~low):
                probabilities = softmax_of(jnp.where(own, query, zero), keys, visible)
                outs.append(
                    jnp.dot(
                        probabilities.astype(jnp.bfloat16),
                        values,
                        preferred_element_type=jnp.float32,
                    )
                )
            out_ref[:, k * LANES : (k + 1) * LANES] = jnp.where(low, outs[0], outs[1]).astype(
                jnp.bfloat16
            )

    def whole(shape):
        return pl.BlockSpec(shape, lambda i: (0, 0))

    return pl.pallas_call(
        body,
        grid=(total // length,),
        in_specs=[
            pl.BlockSpec((length, columns), lambda i: (i, 0)),
            whole((length, LANES)),
            whole((length, LANES)),
            whole((length, 1)),
            whole((1, length)),
        ],
        out_specs=[
            pl.BlockSpec((length, part), lambda i: (i, 0)),
            pl.BlockSpec((length, 2 * part), lambda i: (i, 0)),
        ],
        out_shape=[
            jax.ShapeDtypeStruct((total, part), jnp.bfloat16),
            jax.ShapeDtypeStruct((total, 2 * part), jnp.bfloat16),
        ],
        compiler_params=pltpu.CompilerParams(vmem_limit_bytes=40 * 1024 * 1024),
        cost_estimate=pl.CostEstimate(
            flops=8 * total * length * part,
            bytes_accessed=12 * total * part,
            transcendentals=total * length * part // HEAD_DIM,
        ),
        name="attend",
    )(mixed, cosine, sine, rows_at, columns_at)


def attend_back(turned, mixed, grad_heads, cosine, sine, rows_at, columns_at):
    length = cosine.shape[0]
    total, columns = mixed.shape
    part = columns // 3

    def body(
        turned_ref, values_ref, grad_ref, cosine_ref, sine_ref, rows_ref, columns_ref, out_ref
    ):
        visible = columns_ref[...] <= rows_ref[...]
        low = lane_mask(length)
        for k in range(part // LANES):
            lanes = slice(k * LANES, (k + 1) * LANES)
            query = turned_ref[:, lanes]
            keys = turned_ref[:, part + k * LANES : part + (k + 1) * LANES]
            values = values_ref[:, lanes]
            grad = grad_ref[:, lanes]
            zero = jnp.zeros_like(query)
            grads = []
            for own in (low, ~low):
                probabilities = softmax_of(jnp.where(own, query, zero), keys, visible)
                grad_probabilities = dot_rows(jnp.where(own, grad, zero), values)
                inner = jnp.sum(probabilities * grad_probabilities, axis=1, keepdims=True)
                grad_scores = (probabilities * (grad_probabilities - inner)).astype(jnp.bfloat16)
                grads.append(
                    (
                        jnp.dot(grad_scores, keys, preferred_element_type=jnp.float32) * SCALE,
                        outer_sum(grad_scores, query) * SCALE,
                        outer_sum(probabilities.astype(jnp.bfloat16), grad),
                    )
                )
            for which in range(3):
                heads = jnp.where(low, grads[0][which], grads[1][which])
                if which < 2:
                    heads = heads * cosine_ref[...] - swap_head_halves(heads) * sine_ref[...]
                start = which * part + k * LANES
                out_ref[:, start : start + LANES] = heads.astype(jnp.bfloat16)

    def whole(shape):
        return pl.BlockSpec(shape, lambda i: (0, 0))

    return pl.pallas_call(
        body,
        grid=(total // length,),
        in_specs=[
            pl.BlockSpec((length, 2 * part), lambda i: (i, 0)),
            pl.BlockSpec((length, part), lambda i: (i, 2)),
            pl.BlockSpec((length, part), lambda i: (i, 0)),
            whole((length, LANES)),
            whole((length, LANES)),
            whole((length, 1)),
            whole((1, length)),
        ],
        out_specs=pl.BlockSpec((length, columns), lambda i: (i, 0)),
        out_shape=jax.ShapeDtypeStruct((total, columns), jnp.bfloat16),
        compiler_params=pltpu.CompilerParams(vmem_limit_bytes=48 * 1024 * 1024),
        cost_estimate=pl.CostEstimate(
            flops=20 * total * length * part,
            bytes_accessed=16 * total * part,
            transcendentals=total * length * part // HEAD_DIM,
        ),
        name="attend_back",
    )(turned, mixed, grad_heads, cosine, sine, rows_at, columns_at)


def place_rows(pieces, place):
    rows = pieces[0].shape[0] // 2
    width = pieces[0].shape[1]

    def body(place_ref, *refs):
        for half in range(2):
            for k in range(4):
                at, block = PIECES[half][k]

                @pl.when(pl.program_id(0) == half * 4 + k)
                def _(at=at, start=block // 2 * rows):
                    refs[4][...] = refs[at][start : start + rows, :].astype(jnp.float32)

    return pl.pallas_call(
        body,
        grid_spec=pltpu.PrefetchScalarGridSpec(
            num_scalar_prefetch=1,
            grid=(8,),
            in_specs=[pl.BlockSpec((2 * rows, width), lambda i, p: (0, 0))] * 4,
            out_specs=pl.BlockSpec((rows, width), lambda i, p: ((p[0] ^ (i % 4)) * 2 + i // 4, 0)),
        ),
        out_shape=jax.ShapeDtypeStruct((8 * rows, width), jnp.float32),
        compiler_params=pltpu.CompilerParams(vmem_limit_bytes=32 * 1024 * 1024),
        name="place_rows",
    )(place, *pieces)


def mix_blocks(values):
    blocks = jnp.split(values, 4, axis=1)
    return jnp.concatenate([blocks[k] for k in ROW_ORDER], axis=1)


def in_order(own, other, place):
    return jnp.concatenate([jnp.where(place == 0, own, other), jnp.where(place == 0, other, own)])


def sliced_plan(hidden_in, norm_one, w_qkv, w_out, norm_two, w_gate_up, w_down, grad_out):
    own_seq = lax.axis_index("seq")
    own_core = lax.axis_index("fsdp") % 2
    row = lax.axis_index("fsdp") // 2
    step = row // 2
    place = jnp.stack([own_seq, own_core, step]).astype(jnp.int32)
    inputs = hidden_in[0].astype(jnp.float32)
    cotangent = grad_out[0]
    tokens, width = inputs.shape
    length = tokens * 4
    chunk = w_down.shape[0] // 8
    chip_rows = width // 4
    gain_one = norm_one.astype(jnp.float32)[:, None]
    gain_two = norm_two.astype(jnp.float32)[:, None]

    needed = own_seq < 4
    heads = 4

    def project(rows, weight):
        return jnp.dot(rows, weight, preferred_element_type=jnp.float32).astype(jnp.bfloat16)

    def token_part(rows, k):
        return rows[k * length : (k + 1) * length]

    def backward(grad, weight):
        return [
            back_product(token_part(grad, k), weight).astype(jnp.bfloat16)
            for k in range(grad.shape[0] // length)
        ]

    def own_rows(pair, rows):
        return (
            lax.dynamic_slice_in_dim(pair, step * rows, rows),
            lax.dynamic_slice_in_dim(pair, (1 - step) * rows, rows),
        )

    def halves_of_chip(*chips):
        half_rows = chip_rows // 2

        def of_core(core):
            return jnp.stack(
                [
                    lax.dynamic_slice_in_dim(rows, start + core * half_rows, half_rows)
                    for rows, start in chips
                ]
            )

        return of_core(own_core), swap_cores(of_core(1 - own_core))

    factor_one = lax.rsqrt(jnp.mean(inputs * inputs, axis=-1, keepdims=True) + EPSILON)
    normed, qkv_own, qkv_other = fence(
        (inputs * factor_one).astype(jnp.bfloat16), *slice_heads(w_qkv, gain_one, place, heads)
    )
    normed, qkv_chip, w_out, w_down = fence(
        normed, in_order(qkv_own, swap_cores(qkv_other), own_core), w_out, w_down
    )
    qkv = gather_rows(qkv_chip, ROWS)
    out_proj = gather_rows(lax.dynamic_slice_in_dim(w_out, own_seq * HEAD_DIM, HEAD_DIM), ROWS)

    def gather_inputs():
        flight = fence(*row_one(normed))
        held, flight = row_two(normed, *flight)
        wide_own, wide_other = slice_wide(w_gate_up, gain_two, place, 8, chunk)
        *flight, wide_own, wide_other = fence(*flight, wide_own, wide_other)
        own, other = row_three(held, flight)
        other, *flight, wide_swapped = fence(other, *row_one(cotangent), swap_cores(wide_other))
        held, flight = row_two(cotangent, *flight)
        flight = fence(*flight)
        cotangent_own, cotangent_other = row_three(held, flight)
        return (
            jnp.concatenate([own, other]),
            [in_order(wide_own[k], wide_swapped[k], own_core) for k in range(2)],
            cotangent_own,
            *fence(cotangent_other),
        )

    normed_all, wide_chips, cotangent_own, cotangent_other = window(needed, gather_inputs)

    half_block = tokens // 2
    starts = jnp.concatenate(
        [
            (own_seq ^ jnp.array([0, 1, 2, 3])) * tokens,
            (own_seq ^ jnp.array([0, 2, 1, 3])) * tokens + half_block,
        ]
    )
    positions = (starts[:, None] + jnp.arange(half_block)[None]).reshape(length)
    half = HEAD_DIM // 2
    freqs = THETA ** (-(jnp.arange(half, dtype=jnp.float32) * 2.0) / HEAD_DIM)
    angles = positions.astype(jnp.float32)[:, None] * freqs[None, :]
    cosine = jnp.tile(jnp.cos(angles), (1, 4))
    sine = jnp.tile(jnp.concatenate([-jnp.sin(angles), jnp.sin(angles)], axis=1), (1, 2))
    tables = (cosine, sine, positions[:, None], positions[None, :])

    def norm_two_of(middle):
        factor = lax.rsqrt(jnp.mean(middle * middle, axis=-1, keepdims=True) + EPSILON)
        return mix_blocks((middle * factor).astype(jnp.bfloat16)), factor

    def attention():
        mixed = project(normed_all, qkv)
        return mixed, *attend(mixed, *tables)

    mixed, attended, turned = window(needed, attention)
    attended, out_proj, wide_send, w_down = fence(attended, out_proj, wide_chips[1], w_down)
    wide_more = swap_rows(wide_send, 2)
    down_rows = [
        lax.dynamic_slice_in_dim(w_down, own_seq * 2 * chunk + (step ^ k) * chunk, chunk)
        for k in range(2)
    ]

    def attention_out():
        other = project(token_part(attended, 1), out_proj)
        own = project(token_part(attended, 0), out_proj)
        swapped, own = fence(swap_cores(other), own)
        own = add(own, swapped)
        flight = fence(*send_quarters(own))
        own = add_quarters(own, *flight)
        flight = fence(*send_eighths(*own))
        middle = inputs + add_eighths(*own, *flight)
        return middle, norm_two_of(middle)[0]

    def row_gather(block):
        held, flight = row_two(block, *fence(*row_one(block)))
        own, other = row_three(held, fence(*flight))
        return own, *fence(other)

    middle, normed_two = window(needed, attention_out)
    normed_two_next = swap_rows(normed_two, 2)
    normed_two_row = window(needed, lambda: row_gather(normed_two))
    wide_more, normed_two_next, down_send, cotangent_send, *normed_two_row = fence(
        wide_more, normed_two_next, down_rows[1], cotangent, *normed_two_row
    )
    gate_up_w = gather_rows(in_order(wide_chips[0], wide_more, step), ROW_PAIRS)
    cotangent_next = swap_rows(cotangent_send, 2)
    down_more = swap_rows(down_send, 2)
    normed_two_all = window(
        needed, lambda: jnp.concatenate([*normed_two_row, *row_gather(normed_two_next)])
    )
    normed_two_all, cotangent_next = fence(normed_two_all, cotangent_next)
    cotangent_all = window(
        needed,
        lambda: jnp.concatenate([cotangent_own, cotangent_other, *row_gather(cotangent_next)]),
    )
    down_more, cotangent_all = fence(down_more, cotangent_all)
    down = gather_rows(in_order(down_rows[0], down_more, step), ROW_PAIRS)

    _, factor_two = norm_two_of(middle)
    gate_up = jnp.dot(normed_two_all, gate_up_w, preferred_element_type=jnp.float32)
    units = gate_up.shape[1] // 2
    gate, upward = gate_up[:, :units], gate_up[:, units:]
    sigmoid = jax.nn.sigmoid(gate)
    activated = gate * sigmoid
    hidden = (activated * upward).astype(jnp.bfloat16)
    grad_down_term = outer_sum(hidden, cotangent_all).astype(jnp.bfloat16)
    grad_down_pair = scatter_rows(grad_down_term, ROW_PAIRS)
    cotangent_all, grad_down_term = fence(cotangent_all, grad_down_term)
    grad_hidden = back_product(cotangent_all, down)
    grad_gate = grad_hidden * upward * sigmoid * (1.0 + gate * (1.0 - sigmoid))
    grad_upward = grad_hidden * activated
    grad_low = jnp.concatenate([grad_gate, grad_upward], axis=1).astype(jnp.bfloat16)

    def backward_part(grad, weight, k):
        return back_product(token_part(grad, k), weight).astype(jnp.bfloat16)

    far, far_other = fence(
        backward_part(grad_low, gate_up_w, 2), backward_part(grad_low, gate_up_w, 3)
    )
    grad_gate_up_term = outer_sum(normed_two_all, grad_low).astype(jnp.bfloat16)
    swapped, far, grad_gate_up_term, grad_low, grad_down_pair, hidden = fence(
        swap_cores(far_other), far, grad_gate_up_term, grad_low, grad_down_pair, hidden
    )
    grad_gate_up_pair = scatter_rows(grad_gate_up_term, ROW_PAIRS)
    far = add(far, swapped)
    *flight, near, near_other, forward_far, forward_other = fence(
        *send_quarters(far),
        backward_part(grad_low, gate_up_w, 0),
        backward_part(grad_low, gate_up_w, 1),
        project(token_part(hidden, 2), down),
        project(token_part(hidden, 3), down),
    )
    far = add_quarters(far, *flight)

    def feed_forward_back():
        *flight, swapped, forward_swapped = fence(
            *send_eighths(*far), swap_cores(near_other), swap_cores(forward_other)
        )
        next_row = add_eighths(*far, *flight).astype(jnp.bfloat16)
        near_sum = add(near, swapped)
        forward_sum = add(forward_far, forward_swapped)
        next_row, first, second, *flight = fence(
            swap_rows(next_row, 2), *send_quarters(near_sum), *send_quarters(forward_sum)
        )
        quarters = add_quarters(near_sum, first, second)
        forward_quarters = add_quarters(forward_sum, *flight)
        first, second, *flight = fence(
            *send_eighths(*quarters), *send_eighths(*forward_quarters)
        )
        scaled = mix_blocks(add_eighths(*quarters, first, second) + next_row.astype(jnp.float32))
        grad_middle = (
            cotangent.astype(jnp.float32)
            + factor_two * scaled
            - middle * factor_two**3 * jnp.mean(scaled * middle, axis=-1, keepdims=True)
        )
        return grad_middle, add_eighths(*forward_quarters, *flight).astype(jnp.bfloat16)

    grad_middle, forward_far = window(needed, feed_forward_back)
    wide_send = lax.dynamic_slice_in_dim(grad_gate_up_pair, (1 - step) * chip_rows, chip_rows)
    grad_middle, wide_send = fence(grad_middle, wide_send)
    wide_more = swap_rows(wide_send, 2)

    def gather_branch():
        block = grad_middle.astype(jnp.bfloat16)
        forward = [project(token_part(hidden, k), down) for k in range(2)]
        *flight, swapped = fence(*row_one(block), swap_cores(forward[1]))
        held, flight = row_two(block, *flight)
        flight = fence(*flight)
        own, other = row_three(held, flight)
        forward_sum = add(forward[0], swapped)
        other, *flight = fence(other, *send_quarters(forward_sum))
        return jnp.concatenate([own, other]), add_quarters(forward_sum, *flight)

    grad_branch, forward_near = window(needed, gather_branch)

    down_own, down_send = own_rows(grad_down_pair, chunk)
    grad_branch, wide_more, down_send = fence(grad_branch, wide_more, down_send)

    def attention_back():
        grad_heads = back_product(grad_branch, out_proj).astype(jnp.bfloat16)
        grad_heads, *wide_halves = fence(
            grad_heads, *halves_of_chip((grad_gate_up_pair, step * chip_rows), (wide_more, 0))
        )
        flight = share_one(*wide_halves)
        down_more = swap_rows(down_send, 2)
        grad_mixed = attend_back(turned, mixed, grad_heads, *tables)
        grad_mixed, *near = fence(grad_mixed, *forward_near)
        grad_qkv_term = outer_sum(normed_all, grad_mixed).astype(jnp.bfloat16)
        arrived = fence(grad_qkv_term, down_more, *send_eighths(*near), *flight)
        return grad_mixed, wide_halves, arrived

    grad_mixed, wide_halves, arrived = window(needed, attention_back)
    grad_qkv_term, down_more, forward_first, forward_second, *wide_flight = arrived
    grad_qkv_rows = scatter_rows(grad_qkv_term, ROWS)
    wide_held, wide_flight = share_two(*wide_halves, *wide_flight)

    def inputs_back():
        back = backward(grad_mixed, qkv)
        swapped, near = fence(swap_cores(back[1]), back[0])
        near = add(near, swapped)
        near = add_quarters(near, *fence(*send_quarters(near)))
        scaled = add_eighths(*near, *fence(*send_eighths(*near)))
        return (
            grad_middle
            + factor_one * scaled
            - inputs * factor_one**3 * jnp.mean(scaled * inputs, axis=-1, keepdims=True)
        )

    grad_inputs = window(needed, inputs_back)

    grad_qkv_rows, grad_inputs, attended, forward_far, w_gate_up, down_own, down_more = fence(
        grad_qkv_rows, grad_inputs, attended, forward_far, w_gate_up, down_own, down_more
    )
    down_halves = halves(in_order(down_own, down_more, step))
    qkv_mine, qkv_swapped = halves_of_chip((grad_qkv_rows, 0))
    qkv_swapped, *down_halves = fence(qkv_swapped, *down_halves)
    qkv_halves = qkv_mine, qkv_swapped
    flight = *share_one(*qkv_halves), *share_one(*down_halves)
    grad_out_rows = scatter_rows(outer_sum(attended, grad_branch), ROWS)
    forward_next = swap_rows(forward_far, 2)
    grad_gate_up, gain_two_sums = merge_wide(
        shared(wide_held, wide_flight), w_gate_up, gain_two, place, 8, chunk
    )
    grad_gate_up, gain_two_sums, *flight = fence(grad_gate_up, gain_two_sums, *flight)
    qkv_held, qkv_flight = share_two(*qkv_halves, *flight[:2])
    down_held, down_flight = share_two(*down_halves, *flight[2:])
    grad_out_rows, *qkv_flight = fence(grad_out_rows, *qkv_flight)
    out_halves = halves(grad_out_rows)
    grad_qkv, gain_one_sums = merge_heads(
        shared(qkv_held, qkv_flight), w_qkv, gain_one, place, heads
    )
    grad_qkv, gain_one_sums, forward_next, *flight = fence(
        grad_qkv, gain_one_sums, forward_next, *down_flight, *share_one(*out_halves)
    )
    out_held, out_flight = share_two(*out_halves, *flight[2:])
    output = middle + forward_next.astype(jnp.float32)
    output = output + add_eighths(*forward_near, forward_first, forward_second)
    grad_down = place_rows(shared(down_held, flight[:2]), place)
    grad_down, output, *out_flight = fence(grad_down, output, *out_flight)
    return (
        output.astype(jnp.bfloat16)[None],
        grad_inputs[None],
        jnp.sum(gain_one_sums, axis=(0, 2)),
        grad_qkv,
        place_rows(shared(out_held, out_flight), place),
        jnp.sum(gain_two_sums, axis=(0, 2)),
        grad_gate_up,
        grad_down,
    )


def solution(mesh):
    seq, fsdp = mesh.shape["seq"], mesh.shape["fsdp"]

    def on_device(hidden_in, norm_one, w_qkv, w_out, norm_two, w_gate_up, w_down, grad_out):
        arrays = (hidden_in, norm_one, w_qkv, w_out, norm_two, w_gate_up, w_down, grad_out)
        if seq == 4 and fsdp == 8 and w_out.shape[0] == 4 * HEAD_DIM and w_down.shape[0] % 1024 == 0:
            return sliced_plan(*arrays)
        return gathered_plan(*arrays)

    placed = (
        P("fsdp", "seq", None),
        P("fsdp"),
        P("fsdp", None),
        P("fsdp", None),
        P("fsdp"),
        P("fsdp", None),
        P("fsdp", None),
        P("fsdp", "seq", None),
    )
    return jax.shard_map(
        on_device,
        mesh=mesh,
        in_specs=placed,
        out_specs=(
            P("fsdp", "seq", None),
            P("fsdp", "seq", None),
            P("fsdp"),
            P("fsdp", None),
            P("fsdp", None),
            P("fsdp"),
            P("fsdp", None),
            P("fsdp", None),
        ),
        check_vma=False,
    )
```

```python
import functools

import jax
import jax.numpy as jnp
from jax import lax
from jax.experimental import pallas as pl
from jax.experimental.pallas import tpu as pltpu
from jax.sharding import PartitionSpec as P

HEAD_DIM = 64


EPSILON = 1e-05
THETA = 130000.0
SCALE = 0.125
LANES = 128


def outer_sum(left, right):
    return lax.dot_general(
        left, right, (((0,), (0,)), ((), ())), preferred_element_type=jnp.float32
    )


def back_product(grad, weight):
    return lax.dot_general(
        grad, weight, (((1,), (1,)), ((), ())), preferred_element_type=jnp.float32
    )


def rope_tables(length):
    half = HEAD_DIM // 2
    freqs = THETA ** (-(jnp.arange(half, dtype=jnp.float32) * 2.0) / HEAD_DIM)
    angles = jnp.arange(length, dtype=jnp.float32)[:, None] * freqs[None, :]
    angles = jnp.concatenate([angles, angles], axis=1)
    return (jnp.cos(angles)[:, None, :], jnp.sin(angles)[:, None, :])


def rotate(values, cosine, sine):
    half = values.shape[-1] // 2
    turned = jnp.concatenate([-values[..., half:], values[..., :half]], axis=-1)
    return values * cosine + turned * sine


def unrotate(grads, cosine, sine):
    half = grads.shape[-1] // 2
    scaled = grads * sine
    turned = jnp.concatenate([scaled[..., half:], -scaled[..., :half]], axis=-1)
    return grads * cosine + turned


def norm_forward(values, gain):
    factor = lax.rsqrt(jnp.mean(values * values, axis=-1, keepdims=True) + EPSILON)
    return (values * factor * gain, factor)


def norm_backward(values, factor, gain, grad):
    grad_gain = jnp.sum(grad * values * factor, axis=0)
    scaled = grad * gain
    grad_values = factor * scaled - values * factor**3 * jnp.mean(
        scaled * values, axis=-1, keepdims=True
    )
    return (grad_values, grad_gain)


def fetch_rows(gain, first, second):
    return (
        lax.all_gather(gain, "fsdp", axis=0, tiled=True),
        lax.all_gather(first, "fsdp", axis=0, tiled=True),
        lax.all_gather(second, "fsdp", axis=0, tiled=True),
    )


def weight_term(left, right):
    return outer_sum(left, right)


def reduce_grads(terms):
    partial_sums = (
        lax.psum_scatter(
            terms[0].astype(jnp.bfloat16), "fsdp", scatter_dimension=0, tiled=True
        ).astype(jnp.float32),
        lax.psum_scatter(
            terms[1].astype(jnp.bfloat16), "fsdp", scatter_dimension=0, tiled=True
        ).astype(jnp.float32),
    )
    return (
        lax.psum(partial_sums[0].astype(jnp.bfloat16), "seq").astype(jnp.float32),
        lax.psum(partial_sums[1].astype(jnp.bfloat16), "seq").astype(jnp.float32),
    )


def block_scores(query_block, key_rows, offset):
    scores = (
        jnp.einsum("qhd,khd->hqk", query_block, key_rows, preferred_element_type=jnp.float32)
        * SCALE
    )
    rows = offset + jnp.arange(query_block.shape[0])[:, None]
    columns = jnp.arange(key_rows.shape[0])[None, :]
    return jnp.where((columns <= rows)[None], scores, -1e30)


def gathered_plan(hidden_in, norm_one, w_qkv, w_out, norm_two, w_gate_up, w_down, grad_out):
    inputs = hidden_in[0].astype(jnp.float32)
    tokens = inputs.shape[0]
    width = inputs.shape[1]
    gain_one, qkv_full, out_full = fetch_rows(norm_one, w_qkv, w_out)
    normed, factor_one = norm_forward(inputs, gain_one.astype(jnp.float32))
    normed_low = normed.astype(jnp.bfloat16)
    mixed = jnp.dot(normed_low, qkv_full, preferred_element_type=jnp.float32).astype(jnp.bfloat16)
    regrouped = lax.all_to_all(
        mixed.reshape(tokens, 3, width), "seq", split_axis=2, concat_axis=0, tiled=True
    )
    length = regrouped.shape[0]
    local_width = regrouped.shape[2]
    heads = local_width // HEAD_DIM
    regrouped = regrouped.reshape(length, 3, heads, HEAD_DIM)
    cosine, sine = rope_tables(length)
    query = rotate(regrouped[:, 0].astype(jnp.float32), cosine, sine).astype(jnp.bfloat16)
    keys = rotate(regrouped[:, 1].astype(jnp.float32), cosine, sine).astype(jnp.bfloat16)
    values = regrouped[:, 2]
    block = min(512, length)
    attended_parts = []
    logsums = []
    for start in range(0, length, block):
        stop = start + block
        scores = block_scores(query[start:stop], keys[:stop], start)
        highest = jnp.max(scores, axis=-1, keepdims=True)
        weights = jnp.exp(scores - highest)
        total = jnp.sum(weights, axis=-1, keepdims=True)
        probabilities = (weights / total).astype(jnp.bfloat16)
        logsums.append(highest + jnp.log(total))
        attended_parts.append(
            jnp.einsum(
                "hqk,khd->qhd", probabilities, values[:stop], preferred_element_type=jnp.float32
            )
        )
    attended = (
        jnp.concatenate(attended_parts, axis=0).reshape(length, local_width).astype(jnp.bfloat16)
    )
    back_rows = lax.all_to_all(attended, "seq", split_axis=0, concat_axis=1, tiled=True)
    middle = inputs + jnp.dot(back_rows, out_full, preferred_element_type=jnp.float32)
    gain_two, gate_up_full, down_full = fetch_rows(norm_two, w_gate_up, w_down)
    normed_two, factor_two = norm_forward(middle, gain_two.astype(jnp.float32))
    normed_two_low = normed_two.astype(jnp.bfloat16)
    gate_up = jnp.dot(normed_two_low, gate_up_full, preferred_element_type=jnp.float32)
    hidden_units = gate_up.shape[1] // 2
    gate = gate_up[:, :hidden_units]
    upward = gate_up[:, hidden_units:]
    sigmoid = jax.nn.sigmoid(gate)
    activated = gate * sigmoid
    hidden = (activated * upward).astype(jnp.bfloat16)
    output = middle + jnp.dot(hidden, down_full, preferred_element_type=jnp.float32)
    cotangent = grad_out[0]
    grad_hidden = back_product(cotangent, down_full)
    grad_gate = grad_hidden * upward * sigmoid * (1.0 + gate * (1.0 - sigmoid))
    grad_upward = grad_hidden * activated
    grad_gate_up_low = jnp.concatenate([grad_gate, grad_upward], axis=1).astype(jnp.bfloat16)
    grad_normed_two = back_product(grad_gate_up_low, gate_up_full)
    middle_part, grad_gain_two = norm_backward(
        middle, factor_two, gain_two.astype(jnp.float32), grad_normed_two
    )
    grad_middle = cotangent.astype(jnp.float32) + middle_part
    grad_gate_up_term = weight_term(normed_two_low, grad_gate_up_low)
    grad_branch = grad_middle.astype(jnp.bfloat16)
    grad_out_term = weight_term(back_rows, grad_branch)
    grad_down_term = weight_term(hidden, cotangent)
    grad_down_sum, gain_two_sum = reduce_grads((grad_down_term, grad_gain_two))
    gate_up_sum, out_proj_sum = reduce_grads((grad_gate_up_term, grad_out_term))
    gain_one, qkv_full, out_full = fetch_rows(norm_one, w_qkv, w_out)
    grad_attended = back_product(grad_branch, out_full).astype(jnp.bfloat16)
    grad_heads = lax.all_to_all(
        grad_attended, "seq", split_axis=1, concat_axis=0, tiled=True
    ).reshape(length, heads, HEAD_DIM)
    query_parts = []
    grad_keys = jnp.zeros((length, heads, HEAD_DIM), jnp.float32)
    grad_values = jnp.zeros((length, heads, HEAD_DIM), jnp.float32)
    for index, start in enumerate(range(0, length, block)):
        stop = start + block
        query_block = query[start:stop]
        grad_block = grad_heads[start:stop]
        scores = block_scores(query_block, keys[:stop], start)
        probabilities = jnp.exp(scores - logsums[index])
        grad_probabilities = jnp.einsum(
            "qhd,khd->hqk", grad_block, values[:stop], preferred_element_type=jnp.float32
        )
        inner = jnp.sum(probabilities * grad_probabilities, axis=-1, keepdims=True)
        grad_scores = (probabilities * (grad_probabilities - inner)).astype(jnp.bfloat16)
        query_parts.append(
            jnp.einsum("hqk,khd->qhd", grad_scores, keys[:stop], preferred_element_type=jnp.float32)
            * SCALE
        )
        key_term = (
            jnp.einsum("hqk,qhd->khd", grad_scores, query_block, preferred_element_type=jnp.float32)
            * SCALE
        )
        value_term = jnp.einsum(
            "hqk,qhd->khd",
            probabilities.astype(jnp.bfloat16),
            grad_block,
            preferred_element_type=jnp.float32,
        )
        grad_keys = grad_keys.at[:stop].add(key_term)
        grad_values = grad_values.at[:stop].add(value_term)
    grad_query = unrotate(jnp.concatenate(query_parts, axis=0), cosine, sine)
    grad_keys = unrotate(grad_keys, cosine, sine)
    stacked = (
        jnp.stack([grad_query, grad_keys, grad_values], axis=1)
        .astype(jnp.bfloat16)
        .reshape(length, 3, local_width)
    )
    grad_mixed = lax.all_to_all(stacked, "seq", split_axis=0, concat_axis=2, tiled=True).reshape(
        tokens, 3 * width
    )
    grad_qkv_term = weight_term(normed_low, grad_mixed)
    grad_normed_one = back_product(grad_mixed, qkv_full)
    input_part, grad_gain_one = norm_backward(
        inputs, factor_one, gain_one.astype(jnp.float32), grad_normed_one
    )
    grad_inputs = grad_middle + input_part
    qkv_sum, gain_one_sum = reduce_grads((grad_qkv_term, grad_gain_one))
    return (
        output.astype(jnp.bfloat16)[None],
        grad_inputs[None],
        gain_one_sum,
        qkv_sum,
        out_proj_sum,
        gain_two_sum,
        gate_up_sum,
        grad_down_sum,
    )


def xor_pairs(size, offset):
    return [(i, i ^ offset) for i in range(size)]


def swap_cores(values):
    return lax.ppermute(values, "fsdp", xor_pairs(8, 1))


def swap_rows(values, offset):
    return lax.ppermute(values, "fsdp", xor_pairs(8, 2 * offset))


def swap_seq(values, offset):
    return lax.ppermute(values, "seq", xor_pairs(4, offset))


def fence(*values):
    return lax.optimization_barrier(values)


def window(needed, work):
    outs = jax.eval_shape(work)
    return lax.cond(
        needed,
        work,
        lambda: jax.tree.map(lambda out: jnp.zeros(out.shape, out.dtype), outs),
    )


def halves(block):
    half = block.shape[0] // 2
    return block[:half], block[half:]


def gather_one(block):
    first, second = halves(block)
    return swap_seq(first, 1), swap_seq(second, 2), swap_rows(block, 2)


def gather_two(block, first_more, second_more, next_row):
    first, second = halves(block)
    first = jnp.concatenate([first, first_more])
    second = jnp.concatenate([second, second_more])
    next_first, next_second = halves(next_row)
    return (first, second, next_first, next_second), (
        swap_seq(first, 2),
        swap_seq(second, 1),
        swap_seq(next_first, 1),
        swap_seq(next_second, 2),
    )


def gather_three(held, arrived):
    first, second, next_first, next_second = held
    first_more, second_more, next_first_more, next_second_more = arrived
    own = jnp.concatenate([first, first_more, second, second_more])
    next_first = jnp.concatenate([next_first, next_first_more])
    next_second = jnp.concatenate([next_second, next_second_more])
    return (own, next_first, next_second), (
        swap_cores(own),
        swap_seq(next_first, 2),
        swap_seq(next_second, 1),
    )


def gather_four(held, arrived):
    own, next_first, next_second = held
    other, next_first_more, next_second_more = arrived
    next_own = jnp.concatenate([next_first, next_first_more, next_second, next_second_more])
    return (own, other, next_own), swap_cores(next_own)


def row_one(block):
    first, second = halves(block)
    return swap_seq(first, 1), swap_seq(second, 2)


def row_two(block, first_more, second_more):
    first, second = halves(block)
    first = jnp.concatenate([first, first_more])
    second = jnp.concatenate([second, second_more])
    return (first, second), (swap_seq(first, 2), swap_seq(second, 1))


def row_three(held, arrived):
    own = jnp.concatenate([held[0], arrived[0], held[1], arrived[1]])
    return own, swap_cores(own)


def send_quarters(partial):
    quarter = partial.shape[0] // 4
    return swap_seq(partial[quarter : 2 * quarter], 2), swap_seq(partial[3 * quarter :], 1)


def add_quarters(partial, first, second):
    quarter = partial.shape[0] // 4
    return (
        partial[:quarter].astype(jnp.float32) + first.astype(jnp.float32),
        partial[2 * quarter : 3 * quarter].astype(jnp.float32) + second.astype(jnp.float32),
    )


def send_eighths(first, second):
    half = first.shape[0] // 2
    return (
        swap_seq(first[half:].astype(jnp.bfloat16), 1),
        swap_seq(second[half:].astype(jnp.bfloat16), 2),
    )


def add_eighths(first, second, first_more, second_more):
    half = first.shape[0] // 2
    return jnp.concatenate(
        [
            first[:half] + first_more.astype(jnp.float32),
            second[:half] + second_more.astype(jnp.float32),
        ]
    )


def add(first, second):
    return (first.astype(jnp.float32) + second.astype(jnp.float32)).astype(jnp.bfloat16)


def share_one(first, second):
    return swap_seq(first, 1), swap_seq(second, 2)


def share_two(first, second, first_more, second_more):
    first = jnp.concatenate([first, first_more])
    second = jnp.concatenate([second, second_more])
    return (first, second), (swap_seq(first, 2), swap_seq(second, 1))


def shared(held, arrived):
    return held[0], arrived[0], held[1], arrived[1]


ROWS = [[0, 2, 4, 6], [1, 3, 5, 7]]
ROW_PAIRS = [[0, 2], [4, 6], [1, 3], [5, 7]]
ROW_ORDER = (0, 2, 1, 3)


def gather_rows(block, groups):
    return lax.all_gather(block, "fsdp", axis=0, tiled=True, axis_index_groups=groups)


def scatter_rows(term, groups):
    return lax.psum_scatter(
        term.astype(jnp.bfloat16),
        "fsdp",
        scatter_dimension=0,
        tiled=True,
        axis_index_groups=groups,
    )


def lane_mask(rows):
    return lax.broadcasted_iota(jnp.int32, (rows, LANES), 1) < LANES // 2


def mixed_row(k):
    return (k & 4) | ((k & 1) << 1) | ((k & 2) >> 1)


def slice_wide(weight, gain, place, groups, chunk):
    rows = weight.shape[0]

    def body(place_ref, own_ref, other_ref, gain_ref, *out_refs):
        for weight_ref, out_ref in zip((own_ref, other_ref), out_refs):
            for step in range(2):
                start = pl.multiple_of((place_ref[2] ^ step) * chunk, LANES)
                columns = weight_ref[:, pl.ds(start, chunk)].astype(jnp.float32)
                out_ref[step] = (columns * gain_ref[...]).astype(jnp.bfloat16)

    def columns_of(core):
        return pl.BlockSpec(
            (rows, 2 * chunk), lambda k, p: (0, (mixed_row(k) * 2 + (p[1] ^ core)) * 4 + p[0])
        )

    out = jax.ShapeDtypeStruct((2, rows, groups * chunk), jnp.bfloat16)
    return pl.pallas_call(
        body,
        grid_spec=pltpu.PrefetchScalarGridSpec(
            num_scalar_prefetch=1,
            grid=(groups,),
            in_specs=[columns_of(0), columns_of(1), pl.BlockSpec((rows, 1), lambda k, p: (0, 0))],
            out_specs=[pl.BlockSpec((2, rows, chunk), lambda k, p: (0, 0, k))] * 2,
        ),
        out_shape=[out, out],
        name="slice_wide",
    )(place, weight, weight, gain)


def slice_heads(weight, gain, place, heads):
    rows = weight.shape[0]
    part = weight.shape[1] // 3

    def body(place_ref, weight_ref, gain_ref, *out_refs):
        own_seq, own_core = place_ref[0], place_ref[1]
        odd = (own_seq % 2) == 1
        low = lane_mask(rows)
        for core in range(2):
            for pair in range(heads // 2):
                tiles = []
                for head in (2 * pair, 2 * pair + 1):
                    start = (head * 2 + (own_core ^ core)) * (4 * HEAD_DIM) + (
                        own_seq // 2
                    ) * LANES
                    tile = weight_ref[:, pl.ds(pl.multiple_of(start, LANES), LANES)]
                    tiles.append(tile.astype(jnp.float32) * gain_ref[...])
                turned = [pltpu.roll(tile, LANES // 2, axis=1) for tile in tiles]
                first = jnp.where(odd, turned[0], tiles[0])
                second = jnp.where(odd, tiles[1], turned[1])
                out_refs[core][:, pair * LANES : (pair + 1) * LANES] = jnp.where(
                    low, first, second
                ).astype(jnp.bfloat16)

    out = jax.ShapeDtypeStruct((rows, 3 * heads * HEAD_DIM), jnp.bfloat16)
    return pl.pallas_call(
        body,
        grid_spec=pltpu.PrefetchScalarGridSpec(
            num_scalar_prefetch=1,
            grid=(3,),
            in_specs=[
                pl.BlockSpec((rows, part), lambda k, p: (0, k)),
                pl.BlockSpec((rows, 1), lambda k, p: (0, 0)),
            ],
            out_specs=[pl.BlockSpec((rows, heads * HEAD_DIM), lambda k, p: (0, k))] * 2,
        ),
        out_shape=[out, out],
        name="slice_heads",
    )(place, weight, gain)


def fold(products):
    total = products[:, :LANES]
    for k in range(1, products.shape[1] // LANES):
        total = total + products[:, k * LANES : (k + 1) * LANES]
    return total


PIECES = (((0, 0), (0, 2), (1, 0), (1, 2)), ((2, 0), (3, 0), (2, 2), (3, 2)))


def merge_wide(pieces, weight, gain, place, groups, chunk):
    rows = weight.shape[0]
    width = 16 * chunk

    def body(place_ref, *refs):
        weight_ref, gain_ref = refs[4:6]
        out_ref, sum_ref = refs[6:]

        @pl.when(pl.program_id(0) == 0)
        def _():
            sum_ref[...] = jnp.zeros_like(sum_ref)

        for r in range(4):
            for k in range(4):
                block = ((place_ref[1] ^ (k // 2)) * 4 + (place_ref[0] ^ r)) * 2 + (
                    place_ref[2] ^ (k % 2)
                )
                columns = pl.ds(pl.multiple_of(block * chunk, LANES), chunk)
                term = refs[PIECES[k // 2][r][0]][PIECES[k // 2][r][1] + k % 2].astype(jnp.float32)
                out_ref[:, columns] = term * gain_ref[...]
                sum_ref[place_ref[0] ^ r] += fold(
                    term * weight_ref[:, columns].astype(jnp.float32)
                )

    wide = pl.BlockSpec((rows, width), lambda k, p: (0, mixed_row(k)))
    return pl.pallas_call(
        body,
        grid_spec=pltpu.PrefetchScalarGridSpec(
            num_scalar_prefetch=1,
            grid=(groups,),
            in_specs=[pl.BlockSpec((4, rows, chunk), lambda k, p: (0, 0, k))] * 4
            + [wide, pl.BlockSpec((rows, 1), lambda k, p: (0, 0))],
            out_specs=[wide, pl.BlockSpec((4, rows, LANES), lambda k, p: (0, 0, 0))],
        ),
        out_shape=[
            jax.ShapeDtypeStruct(weight.shape, jnp.float32),
            jax.ShapeDtypeStruct((4, rows, LANES), jnp.float32),
        ],
        compiler_params=pltpu.CompilerParams(vmem_limit_bytes=32 * 1024 * 1024),
        name="merge_wide",
    )(place, *pieces, weight, gain)


def merge_heads(pieces, weight, gain, place, heads):
    rows = weight.shape[0]
    part = weight.shape[1] // 3

    def body(place_ref, *refs):
        weight_ref, gain_ref = refs[4:6]
        out_ref, sum_ref = refs[6:]
        own_seq, own_core = place_ref[0], place_ref[1]
        odd = (own_seq % 2) == 1
        low = lane_mask(rows)

        @pl.when(pl.program_id(0) == 0)
        def _():
            sum_ref[...] = jnp.zeros_like(sum_ref)

        for core in range(2):
            for pair in range(heads // 2):
                for couple in range(2):
                    first, second = (
                        refs[at][block // 2, :, pair * LANES : (pair + 1) * LANES].astype(
                            jnp.float32
                        )
                        for at, block in PIECES[core][2 * couple : 2 * couple + 2]
                    )
                    turned_first = pltpu.roll(first, LANES // 2, axis=1)
                    turned_second = pltpu.roll(second, LANES // 2, axis=1)
                    for head, even_tile, odd_tile in (
                        (
                            2 * pair,
                            jnp.where(low, first, turned_second),
                            jnp.where(low, second, turned_first),
                        ),
                        (
                            2 * pair + 1,
                            jnp.where(low, turned_first, second),
                            jnp.where(low, turned_second, first),
                        ),
                    ):
                        tile = jnp.where(odd, odd_tile, even_tile)
                        start = (head * 2 + (own_core ^ core)) * (4 * HEAD_DIM) + (
                            (own_seq // 2) ^ couple
                        ) * LANES
                        columns = pl.ds(pl.multiple_of(start, LANES), LANES)
                        out_ref[:, columns] = tile * gain_ref[...]
                        sum_ref[(own_seq // 2) ^ couple] += tile * weight_ref[:, columns].astype(
                            jnp.float32
                        )

    wide = pl.BlockSpec((rows, part), lambda k, p: (0, k))
    return pl.pallas_call(
        body,
        grid_spec=pltpu.PrefetchScalarGridSpec(
            num_scalar_prefetch=1,
            grid=(3,),
            in_specs=[pl.BlockSpec((2, rows, heads * HEAD_DIM), lambda k, p: (0, 0, k))] * 4
            + [wide, pl.BlockSpec((rows, 1), lambda k, p: (0, 0))],
            out_specs=[wide, pl.BlockSpec((2, rows, LANES), lambda k, p: (0, 0, 0))],
        ),
        out_shape=[
            jax.ShapeDtypeStruct(weight.shape, jnp.float32),
            jax.ShapeDtypeStruct((2, rows, LANES), jnp.float32),
        ],
        name="merge_heads",
    )(place, *pieces, weight, gain)


def dot_rows(left, right):
    return lax.dot_general(
        left, right, (((1,), (1,)), ((), ())), preferred_element_type=jnp.float32
    )


def swap_head_halves(values):
    lanes = lax.broadcasted_iota(jnp.int32, values.shape, 1) % HEAD_DIM
    half = HEAD_DIM // 2
    return jnp.where(
        lanes < half,
        pltpu.roll(values, LANES - half, axis=1),
        pltpu.roll(values, half, axis=1),
    )


def softmax_of(query, keys, visible):
    scores = jnp.where(visible, dot_rows(query, keys) * SCALE, -1e30)
    weights = jnp.exp(scores - jnp.max(scores, axis=1, keepdims=True))
    return weights / jnp.sum(weights, axis=1, keepdims=True)


def attend(mixed, cosine, sine, rows_at, columns_at):
    length = cosine.shape[0]
    total, columns = mixed.shape
    part = columns // 3

    def body(mixed_ref, cosine_ref, sine_ref, rows_ref, columns_ref, out_ref, turned_ref):
        visible = columns_ref[...] <= rows_ref[...]
        low = lane_mask(length)
        for k in range(2 * part // LANES):
            lanes = slice(k * LANES, (k + 1) * LANES)
            heads = mixed_ref[:, lanes].astype(jnp.float32)
            turned_ref[:, lanes] = (
                heads * cosine_ref[...] + swap_head_halves(heads) * sine_ref[...]
            ).astype(jnp.bfloat16)
        for k in range(part // LANES):
            query = turned_ref[:, k * LANES : (k + 1) * LANES]
            keys = turned_ref[:, part + k * LANES : part + (k + 1) * LANES]
            values = mixed_ref[:, 2 * part + k * LANES : 2 * part + (k + 1) * LANES]
            zero = jnp.zeros_like(query)
            outs = []
            for own in (low, ~low):
                probabilities = softmax_of(jnp.where(own, query, zero), keys, visible)
                outs.append(
                    jnp.dot(
                        probabilities.astype(jnp.bfloat16),
                        values,
                        preferred_element_type=jnp.float32,
                    )
                )
            out_ref[:, k * LANES : (k + 1) * LANES] = jnp.where(low, outs[0], outs[1]).astype(
                jnp.bfloat16
            )

    def whole(shape):
        return pl.BlockSpec(shape, lambda i: (0, 0))

    return pl.pallas_call(
        body,
        grid=(total // length,),
        in_specs=[
            pl.BlockSpec((length, columns), lambda i: (i, 0)),
            whole((length, LANES)),
            whole((length, LANES)),
            whole((length, 1)),
            whole((1, length)),
        ],
        out_specs=[
            pl.BlockSpec((length, part), lambda i: (i, 0)),
            pl.BlockSpec((length, 2 * part), lambda i: (i, 0)),
        ],
        out_shape=[
            jax.ShapeDtypeStruct((total, part), jnp.bfloat16),
            jax.ShapeDtypeStruct((total, 2 * part), jnp.bfloat16),
        ],
        compiler_params=pltpu.CompilerParams(vmem_limit_bytes=40 * 1024 * 1024),
        cost_estimate=pl.CostEstimate(
            flops=8 * total * length * part,
            bytes_accessed=12 * total * part,
            transcendentals=total * length * part // HEAD_DIM,
        ),
        name="attend",
    )(mixed, cosine, sine, rows_at, columns_at)


def attend_back(turned, mixed, grad_heads, cosine, sine, rows_at, columns_at):
    length = cosine.shape[0]
    total, columns = mixed.shape
    part = columns // 3

    def body(
        turned_ref, values_ref, grad_ref, cosine_ref, sine_ref, rows_ref, columns_ref, out_ref
    ):
        visible = columns_ref[...] <= rows_ref[...]
        low = lane_mask(length)
        for k in range(part // LANES):
            lanes = slice(k * LANES, (k + 1) * LANES)
            query = turned_ref[:, lanes]
            keys = turned_ref[:, part + k * LANES : part + (k + 1) * LANES]
            values = values_ref[:, lanes]
            grad = grad_ref[:, lanes]
            zero = jnp.zeros_like(query)
            grads = []
            for own in (low, ~low):
                probabilities = softmax_of(jnp.where(own, query, zero), keys, visible)
                grad_probabilities = dot_rows(jnp.where(own, grad, zero), values)
                inner = jnp.sum(probabilities * grad_probabilities, axis=1, keepdims=True)
                grad_scores = (probabilities * (grad_probabilities - inner)).astype(jnp.bfloat16)
                grads.append(
                    (
                        jnp.dot(grad_scores, keys, preferred_element_type=jnp.float32) * SCALE,
                        outer_sum(grad_scores, query) * SCALE,
                        outer_sum(probabilities.astype(jnp.bfloat16), grad),
                    )
                )
            for which in range(3):
                heads = jnp.where(low, grads[0][which], grads[1][which])
                if which < 2:
                    heads = heads * cosine_ref[...] - swap_head_halves(heads) * sine_ref[...]
                start = which * part + k * LANES
                out_ref[:, start : start + LANES] = heads.astype(jnp.bfloat16)

    def whole(shape):
        return pl.BlockSpec(shape, lambda i: (0, 0))

    return pl.pallas_call(
        body,
        grid=(total // length,),
        in_specs=[
            pl.BlockSpec((length, 2 * part), lambda i: (i, 0)),
            pl.BlockSpec((length, part), lambda i: (i, 2)),
            pl.BlockSpec((length, part), lambda i: (i, 0)),
            whole((length, LANES)),
            whole((length, LANES)),
            whole((length, 1)),
            whole((1, length)),
        ],
        out_specs=pl.BlockSpec((length, columns), lambda i: (i, 0)),
        out_shape=jax.ShapeDtypeStruct((total, columns), jnp.bfloat16),
        compiler_params=pltpu.CompilerParams(vmem_limit_bytes=48 * 1024 * 1024),
        cost_estimate=pl.CostEstimate(
            flops=20 * total * length * part,
            bytes_accessed=16 * total * part,
            transcendentals=total * length * part // HEAD_DIM,
        ),
        name="attend_back",
    )(turned, mixed, grad_heads, cosine, sine, rows_at, columns_at)


def place_rows(pieces, place):
    rows = pieces[0].shape[0] // 2
    width = pieces[0].shape[1]

    def body(place_ref, *refs):
        for half in range(2):
            for k in range(4):
                at, block = PIECES[half][k]

                @pl.when(pl.program_id(0) == half * 4 + k)
                def _(at=at, start=block // 2 * rows):
                    refs[4][...] = refs[at][start : start + rows, :].astype(jnp.float32)

    return pl.pallas_call(
        body,
        grid_spec=pltpu.PrefetchScalarGridSpec(
            num_scalar_prefetch=1,
            grid=(8,),
            in_specs=[pl.BlockSpec((2 * rows, width), lambda i, p: (0, 0))] * 4,
            out_specs=pl.BlockSpec((rows, width), lambda i, p: ((p[0] ^ (i % 4)) * 2 + i // 4, 0)),
        ),
        out_shape=jax.ShapeDtypeStruct((8 * rows, width), jnp.float32),
        compiler_params=pltpu.CompilerParams(vmem_limit_bytes=32 * 1024 * 1024),
        name="place_rows",
    )(place, *pieces)


def mix_blocks(values):
    blocks = jnp.split(values, 4, axis=1)
    return jnp.concatenate([blocks[k] for k in ROW_ORDER], axis=1)


def in_order(own, other, place):
    return jnp.concatenate([jnp.where(place == 0, own, other), jnp.where(place == 0, other, own)])


def sliced_plan(hidden_in, norm_one, w_qkv, w_out, norm_two, w_gate_up, w_down, grad_out):
    own_seq = lax.axis_index("seq")
    own_core = lax.axis_index("fsdp") % 2
    row = lax.axis_index("fsdp") // 2
    step = row // 2
    place = jnp.stack([own_seq, own_core, step]).astype(jnp.int32)
    inputs = hidden_in[0].astype(jnp.float32)
    cotangent = grad_out[0]
    tokens, width = inputs.shape
    length = tokens * 4
    chunk = w_down.shape[0] // 8
    chip_rows = width // 4
    gain_one = norm_one.astype(jnp.float32)[:, None]
    gain_two = norm_two.astype(jnp.float32)[:, None]

    needed = own_seq < 4
    heads = 4

    def project(rows, weight):
        return jnp.dot(rows, weight, preferred_element_type=jnp.float32).astype(jnp.bfloat16)

    def token_part(rows, k):
        return rows[k * length : (k + 1) * length]

    def backward(grad, weight):
        return [
            back_product(token_part(grad, k), weight).astype(jnp.bfloat16)
            for k in range(grad.shape[0] // length)
        ]

    def own_rows(pair, rows):
        return (
            lax.dynamic_slice_in_dim(pair, step * rows, rows),
            lax.dynamic_slice_in_dim(pair, (1 - step) * rows, rows),
        )

    def halves_of_chip(*chips):
        half_rows = chip_rows // 2

        def of_core(core):
            return jnp.stack(
                [
                    lax.dynamic_slice_in_dim(rows, start + core * half_rows, half_rows)
                    for rows, start in chips
                ]
            )

        return of_core(own_core), swap_cores(of_core(1 - own_core))

    factor_one = lax.rsqrt(jnp.mean(inputs * inputs, axis=-1, keepdims=True) + EPSILON)
    normed, qkv_own, qkv_other = fence(
        (inputs * factor_one).astype(jnp.bfloat16), *slice_heads(w_qkv, gain_one, place, heads)
    )
    normed, qkv_chip, w_out, w_down = fence(
        normed, in_order(qkv_own, swap_cores(qkv_other), own_core), w_out, w_down
    )
    qkv = gather_rows(qkv_chip, ROWS)
    out_proj = gather_rows(lax.dynamic_slice_in_dim(w_out, own_seq * HEAD_DIM, HEAD_DIM), ROWS)

    def gather_inputs():
        flight = fence(*row_one(normed))
        held, flight = row_two(normed, *flight)
        wide_own, wide_other = slice_wide(w_gate_up, gain_two, place, 8, chunk)
        *flight, wide_own, wide_other = fence(*flight, wide_own, wide_other)
        own, other = row_three(held, flight)
        other, *flight, wide_swapped = fence(other, *row_one(cotangent), swap_cores(wide_other))
        held, flight = row_two(cotangent, *flight)
        flight = fence(*flight)
        cotangent_own, cotangent_other = row_three(held, flight)
        return (
            jnp.concatenate([own, other]),
            [in_order(wide_own[k], wide_swapped[k], own_core) for k in range(2)],
            cotangent_own,
            *fence(cotangent_other),
        )

    normed_all, wide_chips, cotangent_own, cotangent_other = window(needed, gather_inputs)

    half_block = tokens // 2
    starts = jnp.concatenate(
        [
            (own_seq ^ jnp.array([0, 1, 2, 3])) * tokens,
            (own_seq ^ jnp.array([0, 2, 1, 3])) * tokens + half_block,
        ]
    )
    positions = (starts[:, None] + jnp.arange(half_block)[None]).reshape(length)
    half = HEAD_DIM // 2
    freqs = THETA ** (-(jnp.arange(half, dtype=jnp.float32) * 2.0) / HEAD_DIM)
    angles = positions.astype(jnp.float32)[:, None] * freqs[None, :]
    cosine = jnp.tile(jnp.cos(angles), (1, 4))
    sine = jnp.tile(jnp.concatenate([-jnp.sin(angles), jnp.sin(angles)], axis=1), (1, 2))
    tables = (cosine, sine, positions[:, None], positions[None, :])

    def norm_two_of(middle):
        factor = lax.rsqrt(jnp.mean(middle * middle, axis=-1, keepdims=True) + EPSILON)
        return mix_blocks((middle * factor).astype(jnp.bfloat16)), factor

    def attention():
        mixed = project(normed_all, qkv)
        return mixed, *attend(mixed, *tables)

    mixed, attended, turned = window(needed, attention)
    attended, out_proj, wide_send, w_down = fence(attended, out_proj, wide_chips[1], w_down)
    wide_more = swap_rows(wide_send, 2)
    down_rows = [
        lax.dynamic_slice_in_dim(w_down, own_seq * 2 * chunk + (step ^ k) * chunk, chunk)
        for k in range(2)
    ]

    def attention_out():
        other = project(token_part(attended, 1), out_proj)
        own = project(token_part(attended, 0), out_proj)
        swapped, own = fence(swap_cores(other), own)
        own = add(own, swapped)
        flight = fence(*send_quarters(own))
        own = add_quarters(own, *flight)
        flight = fence(*send_eighths(*own))
        middle = inputs + add_eighths(*own, *flight)
        return middle, norm_two_of(middle)[0]

    def row_gather(block):
        held, flight = row_two(block, *fence(*row_one(block)))
        own, other = row_three(held, fence(*flight))
        return own, *fence(other)

    middle, normed_two = window(needed, attention_out)
    normed_two_next = swap_rows(normed_two, 2)
    normed_two_row = window(needed, lambda: row_gather(normed_two))
    wide_more, normed_two_next, down_send, cotangent_send, *normed_two_row = fence(
        wide_more, normed_two_next, down_rows[1], cotangent, *normed_two_row
    )
    gate_up_w = gather_rows(in_order(wide_chips[0], wide_more, step), ROW_PAIRS)
    cotangent_next = swap_rows(cotangent_send, 2)
    down_more = swap_rows(down_send, 2)
    normed_two_all = window(
        needed, lambda: jnp.concatenate([*normed_two_row, *row_gather(normed_two_next)])
    )
    normed_two_all, cotangent_next = fence(normed_two_all, cotangent_next)
    cotangent_all = window(
        needed,
        lambda: jnp.concatenate([cotangent_own, cotangent_other, *row_gather(cotangent_next)]),
    )
    down_more, cotangent_all = fence(down_more, cotangent_all)
    down = gather_rows(in_order(down_rows[0], down_more, step), ROW_PAIRS)

    _, factor_two = norm_two_of(middle)
    gate_up = jnp.dot(normed_two_all, gate_up_w, preferred_element_type=jnp.float32)
    units = gate_up.shape[1] // 2
    gate, upward = gate_up[:, :units], gate_up[:, units:]
    sigmoid = jax.nn.sigmoid(gate)
    activated = gate * sigmoid
    hidden = (activated * upward).astype(jnp.bfloat16)
    grad_down_term = outer_sum(hidden, cotangent_all).astype(jnp.bfloat16)
    grad_down_pair = scatter_rows(grad_down_term, ROW_PAIRS)
    cotangent_all, grad_down_term = fence(cotangent_all, grad_down_term)
    grad_hidden = back_product(cotangent_all, down)
    grad_gate = grad_hidden * upward * sigmoid * (1.0 + gate * (1.0 - sigmoid))
    grad_upward = grad_hidden * activated
    grad_low = jnp.concatenate([grad_gate, grad_upward], axis=1).astype(jnp.bfloat16)

    def backward_part(grad, weight, k):
        return back_product(token_part(grad, k), weight).astype(jnp.bfloat16)

    far, far_other = fence(
        backward_part(grad_low, gate_up_w, 2), backward_part(grad_low, gate_up_w, 3)
    )
    grad_gate_up_term = outer_sum(normed_two_all, grad_low).astype(jnp.bfloat16)
    swapped, far, grad_gate_up_term, grad_low, grad_down_pair, hidden = fence(
        swap_cores(far_other), far, grad_gate_up_term, grad_low, grad_down_pair, hidden
    )
    grad_gate_up_pair = scatter_rows(grad_gate_up_term, ROW_PAIRS)
    far = add(far, swapped)
    *flight, near, near_other, forward_near, near_forward_other, forward_far, forward_other = fence(
        *send_quarters(far),
        backward_part(grad_low, gate_up_w, 0),
        backward_part(grad_low, gate_up_w, 1),
        *(project(token_part(hidden, k), down) for k in range(4)),
    )
    far = add_quarters(far, *flight)

    def feed_forward_back():
        *flight, swapped, forward_swapped = fence(
            *send_eighths(*far), swap_cores(near_other), swap_cores(forward_other)
        )
        next_row = add_eighths(*far, *flight).astype(jnp.bfloat16)
        near_sum = add(near, swapped)
        forward_sum = add(forward_far, forward_swapped)
        next_row, first, second, *flight = fence(
            swap_rows(next_row, 2), *send_quarters(near_sum), *send_quarters(forward_sum)
        )
        quarters = add_quarters(near_sum, first, second)
        forward_quarters = add_quarters(forward_sum, *flight)
        first, second, *flight = fence(
            *send_eighths(*quarters), *send_eighths(*forward_quarters)
        )
        scaled = mix_blocks(add_eighths(*quarters, first, second) + next_row.astype(jnp.float32))
        grad_middle = (
            cotangent.astype(jnp.float32)
            + factor_two * scaled
            - middle * factor_two**3 * jnp.mean(scaled * middle, axis=-1, keepdims=True)
        )
        return grad_middle, add_eighths(*forward_quarters, *flight).astype(jnp.bfloat16)

    grad_middle, forward_far = window(needed, feed_forward_back)
    wide_send = lax.dynamic_slice_in_dim(grad_gate_up_pair, (1 - step) * chip_rows, chip_rows)
    grad_middle, wide_send = fence(grad_middle, wide_send)
    wide_more = swap_rows(wide_send, 2)

    def gather_branch():
        block = grad_middle.astype(jnp.bfloat16)
        *flight, swapped = fence(*row_one(block), swap_cores(near_forward_other))
        held, flight = row_two(block, *flight)
        flight = fence(*flight)
        own, other = row_three(held, flight)
        forward_sum = add(forward_near, swapped)
        other, *flight = fence(other, *send_quarters(forward_sum))
        return jnp.concatenate([own, other]), add_quarters(forward_sum, *flight)

    grad_branch, forward_quarters = window(needed, gather_branch)

    down_own, down_send = own_rows(grad_down_pair, chunk)
    grad_branch, wide_more, down_send = fence(grad_branch, wide_more, down_send)

    def attention_back():
        grad_heads = back_product(grad_branch, out_proj).astype(jnp.bfloat16)
        grad_heads, *wide_halves = fence(
            grad_heads, *halves_of_chip((grad_gate_up_pair, step * chip_rows), (wide_more, 0))
        )
        flight = share_one(*wide_halves)
        down_more = swap_rows(down_send, 2)
        grad_mixed = attend_back(turned, mixed, grad_heads, *tables)
        grad_mixed, *near = fence(grad_mixed, *forward_quarters)
        grad_qkv_term = outer_sum(normed_all, grad_mixed).astype(jnp.bfloat16)
        arrived = fence(grad_qkv_term, down_more, *send_eighths(*near), *flight)
        return grad_mixed, wide_halves, arrived

    grad_mixed, wide_halves, arrived = window(needed, attention_back)
    grad_qkv_term, down_more, forward_first, forward_second, *wide_flight = arrived
    grad_qkv_rows = scatter_rows(grad_qkv_term, ROWS)
    wide_held, wide_flight = share_two(*wide_halves, *wide_flight)

    def inputs_back():
        back = backward(grad_mixed, qkv)
        swapped, near = fence(swap_cores(back[1]), back[0])
        near = add(near, swapped)
        near = add_quarters(near, *fence(*send_quarters(near)))
        scaled = add_eighths(*near, *fence(*send_eighths(*near)))
        return (
            grad_middle
            + factor_one * scaled
            - inputs * factor_one**3 * jnp.mean(scaled * inputs, axis=-1, keepdims=True)
        )

    grad_inputs = window(needed, inputs_back)

    grad_qkv_rows, grad_inputs, attended, forward_far, w_gate_up, down_own, down_more = fence(
        grad_qkv_rows, grad_inputs, attended, forward_far, w_gate_up, down_own, down_more
    )
    down_halves = halves(in_order(down_own, down_more, step))
    qkv_mine, qkv_swapped = halves_of_chip((grad_qkv_rows, 0))
    qkv_swapped, w_gate_up, attended, *down_halves = fence(
        qkv_swapped, w_gate_up, attended, *down_halves
    )
    qkv_halves = qkv_mine, qkv_swapped
    flight = *share_one(*qkv_halves), *share_one(*down_halves)
    grad_out_rows = scatter_rows(outer_sum(attended, grad_branch), ROWS)
    forward_next = swap_rows(forward_far, 2)
    grad_gate_up, gain_two_sums = merge_wide(
        shared(wide_held, wide_flight), w_gate_up, gain_two, place, 8, chunk
    )
    grad_gate_up, gain_two_sums, *flight = fence(grad_gate_up, gain_two_sums, *flight)
    qkv_held, qkv_flight = share_two(*qkv_halves, *flight[:2])
    down_held, down_flight = share_two(*down_halves, *flight[2:])
    grad_out_rows, *qkv_flight = fence(grad_out_rows, *qkv_flight)
    out_halves = halves(grad_out_rows)
    grad_qkv, gain_one_sums = merge_heads(
        shared(qkv_held, qkv_flight), w_qkv, gain_one, place, heads
    )
    grad_qkv, gain_one_sums, forward_next, *flight = fence(
        grad_qkv, gain_one_sums, forward_next, *down_flight, *share_one(*out_halves)
    )
    out_held, out_flight = share_two(*out_halves, *flight[2:])
    output = middle + forward_next.astype(jnp.float32)
    output = output + add_eighths(*forward_quarters, forward_first, forward_second)
    grad_down = place_rows(shared(down_held, flight[:2]), place)
    grad_down, output, *out_flight = fence(grad_down, output, *out_flight)
    return (
        output.astype(jnp.bfloat16)[None],
        grad_inputs[None],
        jnp.sum(gain_one_sums, axis=(0, 2)),
        grad_qkv,
        place_rows(shared(out_held, out_flight), place),
        jnp.sum(gain_two_sums, axis=(0, 2)),
        grad_gate_up,
        grad_down,
    )


def solution(mesh):
    seq, fsdp = mesh.shape["seq"], mesh.shape["fsdp"]

    def on_device(hidden_in, norm_one, w_qkv, w_out, norm_two, w_gate_up, w_down, grad_out):
        arrays = (hidden_in, norm_one, w_qkv, w_out, norm_two, w_gate_up, w_down, grad_out)
        if seq == 4 and fsdp == 8 and w_out.shape[0] == 4 * HEAD_DIM and w_down.shape[0] % 1024 == 0:
            return sliced_plan(*arrays)
        return gathered_plan(*arrays)

    placed = (
        P("fsdp", "seq", None),
        P("fsdp"),
        P("fsdp", None),
        P("fsdp", None),
        P("fsdp"),
        P("fsdp", None),
        P("fsdp", None),
        P("fsdp", "seq", None),
    )
    return jax.shard_map(
        on_device,
        mesh=mesh,
        in_specs=placed,
        out_specs=(
            P("fsdp", "seq", None),
            P("fsdp", "seq", None),
            P("fsdp"),
            P("fsdp", None),
            P("fsdp", None),
            P("fsdp"),
            P("fsdp", None),
            P("fsdp", None),
        ),
        check_vma=False,
    )
```

```python
import functools

import jax
import jax.numpy as jnp
from jax import lax
from jax.experimental import pallas as pl
from jax.experimental.pallas import tpu as pltpu
from jax.sharding import PartitionSpec as P

HEAD_DIM = 64


EPSILON = 1e-05
THETA = 130000.0
SCALE = 0.125
LANES = 128


def outer_sum(left, right):
    return lax.dot_general(
        left, right, (((0,), (0,)), ((), ())), preferred_element_type=jnp.float32
    )


def back_product(grad, weight):
    return lax.dot_general(
        grad, weight, (((1,), (1,)), ((), ())), preferred_element_type=jnp.float32
    )


def rope_tables(length):
    half = HEAD_DIM // 2
    freqs = THETA ** (-(jnp.arange(half, dtype=jnp.float32) * 2.0) / HEAD_DIM)
    angles = jnp.arange(length, dtype=jnp.float32)[:, None] * freqs[None, :]
    angles = jnp.concatenate([angles, angles], axis=1)
    return (jnp.cos(angles)[:, None, :], jnp.sin(angles)[:, None, :])


def rotate(values, cosine, sine):
    half = values.shape[-1] // 2
    turned = jnp.concatenate([-values[..., half:], values[..., :half]], axis=-1)
    return values * cosine + turned * sine


def unrotate(grads, cosine, sine):
    half = grads.shape[-1] // 2
    scaled = grads * sine
    turned = jnp.concatenate([scaled[..., half:], -scaled[..., :half]], axis=-1)
    return grads * cosine + turned


def norm_forward(values, gain):
    factor = lax.rsqrt(jnp.mean(values * values, axis=-1, keepdims=True) + EPSILON)
    return (values * factor * gain, factor)


def norm_backward(values, factor, gain, grad):
    grad_gain = jnp.sum(grad * values * factor, axis=0)
    scaled = grad * gain
    grad_values = factor * scaled - values * factor**3 * jnp.mean(
        scaled * values, axis=-1, keepdims=True
    )
    return (grad_values, grad_gain)


def fetch_rows(gain, first, second):
    return (
        lax.all_gather(gain, "fsdp", axis=0, tiled=True),
        lax.all_gather(first, "fsdp", axis=0, tiled=True),
        lax.all_gather(second, "fsdp", axis=0, tiled=True),
    )


def weight_term(left, right):
    return outer_sum(left, right)


def reduce_grads(terms):
    partial_sums = (
        lax.psum_scatter(
            terms[0].astype(jnp.bfloat16), "fsdp", scatter_dimension=0, tiled=True
        ).astype(jnp.float32),
        lax.psum_scatter(
            terms[1].astype(jnp.bfloat16), "fsdp", scatter_dimension=0, tiled=True
        ).astype(jnp.float32),
    )
    return (
        lax.psum(partial_sums[0].astype(jnp.bfloat16), "seq").astype(jnp.float32),
        lax.psum(partial_sums[1].astype(jnp.bfloat16), "seq").astype(jnp.float32),
    )


def block_scores(query_block, key_rows, offset):
    scores = (
        jnp.einsum("qhd,khd->hqk", query_block, key_rows, preferred_element_type=jnp.float32)
        * SCALE
    )
    rows = offset + jnp.arange(query_block.shape[0])[:, None]
    columns = jnp.arange(key_rows.shape[0])[None, :]
    return jnp.where((columns <= rows)[None], scores, -1e30)


def gathered_plan(hidden_in, norm_one, w_qkv, w_out, norm_two, w_gate_up, w_down, grad_out):
    inputs = hidden_in[0].astype(jnp.float32)
    tokens = inputs.shape[0]
    width = inputs.shape[1]
    gain_one, qkv_full, out_full = fetch_rows(norm_one, w_qkv, w_out)
    normed, factor_one = norm_forward(inputs, gain_one.astype(jnp.float32))
    normed_low = normed.astype(jnp.bfloat16)
    mixed = jnp.dot(normed_low, qkv_full, preferred_element_type=jnp.float32).astype(jnp.bfloat16)
    regrouped = lax.all_to_all(
        mixed.reshape(tokens, 3, width), "seq", split_axis=2, concat_axis=0, tiled=True
    )
    length = regrouped.shape[0]
    local_width = regrouped.shape[2]
    heads = local_width // HEAD_DIM
    regrouped = regrouped.reshape(length, 3, heads, HEAD_DIM)
    cosine, sine = rope_tables(length)
    query = rotate(regrouped[:, 0].astype(jnp.float32), cosine, sine).astype(jnp.bfloat16)
    keys = rotate(regrouped[:, 1].astype(jnp.float32), cosine, sine).astype(jnp.bfloat16)
    values = regrouped[:, 2]
    block = min(512, length)
    attended_parts = []
    logsums = []
    for start in range(0, length, block):
        stop = start + block
        scores = block_scores(query[start:stop], keys[:stop], start)
        highest = jnp.max(scores, axis=-1, keepdims=True)
        weights = jnp.exp(scores - highest)
        total = jnp.sum(weights, axis=-1, keepdims=True)
        probabilities = (weights / total).astype(jnp.bfloat16)
        logsums.append(highest + jnp.log(total))
        attended_parts.append(
            jnp.einsum(
                "hqk,khd->qhd", probabilities, values[:stop], preferred_element_type=jnp.float32
            )
        )
    attended = (
        jnp.concatenate(attended_parts, axis=0).reshape(length, local_width).astype(jnp.bfloat16)
    )
    back_rows = lax.all_to_all(attended, "seq", split_axis=0, concat_axis=1, tiled=True)
    middle = inputs + jnp.dot(back_rows, out_full, preferred_element_type=jnp.float32)
    gain_two, gate_up_full, down_full = fetch_rows(norm_two, w_gate_up, w_down)
    normed_two, factor_two = norm_forward(middle, gain_two.astype(jnp.float32))
    normed_two_low = normed_two.astype(jnp.bfloat16)
    gate_up = jnp.dot(normed_two_low, gate_up_full, preferred_element_type=jnp.float32)
    hidden_units = gate_up.shape[1] // 2
    gate = gate_up[:, :hidden_units]
    upward = gate_up[:, hidden_units:]
    sigmoid = jax.nn.sigmoid(gate)
    activated = gate * sigmoid
    hidden = (activated * upward).astype(jnp.bfloat16)
    output = middle + jnp.dot(hidden, down_full, preferred_element_type=jnp.float32)
    cotangent = grad_out[0]
    grad_hidden = back_product(cotangent, down_full)
    grad_gate = grad_hidden * upward * sigmoid * (1.0 + gate * (1.0 - sigmoid))
    grad_upward = grad_hidden * activated
    grad_gate_up_low = jnp.concatenate([grad_gate, grad_upward], axis=1).astype(jnp.bfloat16)
    grad_normed_two = back_product(grad_gate_up_low, gate_up_full)
    middle_part, grad_gain_two = norm_backward(
        middle, factor_two, gain_two.astype(jnp.float32), grad_normed_two
    )
    grad_middle = cotangent.astype(jnp.float32) + middle_part
    grad_gate_up_term = weight_term(normed_two_low, grad_gate_up_low)
    grad_branch = grad_middle.astype(jnp.bfloat16)
    grad_out_term = weight_term(back_rows, grad_branch)
    grad_down_term = weight_term(hidden, cotangent)
    grad_down_sum, gain_two_sum = reduce_grads((grad_down_term, grad_gain_two))
    gate_up_sum, out_proj_sum = reduce_grads((grad_gate_up_term, grad_out_term))
    gain_one, qkv_full, out_full = fetch_rows(norm_one, w_qkv, w_out)
    grad_attended = back_product(grad_branch, out_full).astype(jnp.bfloat16)
    grad_heads = lax.all_to_all(
        grad_attended, "seq", split_axis=1, concat_axis=0, tiled=True
    ).reshape(length, heads, HEAD_DIM)
    query_parts = []
    grad_keys = jnp.zeros((length, heads, HEAD_DIM), jnp.float32)
    grad_values = jnp.zeros((length, heads, HEAD_DIM), jnp.float32)
    for index, start in enumerate(range(0, length, block)):
        stop = start + block
        query_block = query[start:stop]
        grad_block = grad_heads[start:stop]
        scores = block_scores(query_block, keys[:stop], start)
        probabilities = jnp.exp(scores - logsums[index])
        grad_probabilities = jnp.einsum(
            "qhd,khd->hqk", grad_block, values[:stop], preferred_element_type=jnp.float32
        )
        inner = jnp.sum(probabilities * grad_probabilities, axis=-1, keepdims=True)
        grad_scores = (probabilities * (grad_probabilities - inner)).astype(jnp.bfloat16)
        query_parts.append(
            jnp.einsum("hqk,khd->qhd", grad_scores, keys[:stop], preferred_element_type=jnp.float32)
            * SCALE
        )
        key_term = (
            jnp.einsum("hqk,qhd->khd", grad_scores, query_block, preferred_element_type=jnp.float32)
            * SCALE
        )
        value_term = jnp.einsum(
            "hqk,qhd->khd",
            probabilities.astype(jnp.bfloat16),
            grad_block,
            preferred_element_type=jnp.float32,
        )
        grad_keys = grad_keys.at[:stop].add(key_term)
        grad_values = grad_values.at[:stop].add(value_term)
    grad_query = unrotate(jnp.concatenate(query_parts, axis=0), cosine, sine)
    grad_keys = unrotate(grad_keys, cosine, sine)
    stacked = (
        jnp.stack([grad_query, grad_keys, grad_values], axis=1)
        .astype(jnp.bfloat16)
        .reshape(length, 3, local_width)
    )
    grad_mixed = lax.all_to_all(stacked, "seq", split_axis=0, concat_axis=2, tiled=True).reshape(
        tokens, 3 * width
    )
    grad_qkv_term = weight_term(normed_low, grad_mixed)
    grad_normed_one = back_product(grad_mixed, qkv_full)
    input_part, grad_gain_one = norm_backward(
        inputs, factor_one, gain_one.astype(jnp.float32), grad_normed_one
    )
    grad_inputs = grad_middle + input_part
    qkv_sum, gain_one_sum = reduce_grads((grad_qkv_term, grad_gain_one))
    return (
        output.astype(jnp.bfloat16)[None],
        grad_inputs[None],
        gain_one_sum,
        qkv_sum,
        out_proj_sum,
        gain_two_sum,
        gate_up_sum,
        grad_down_sum,
    )


def xor_pairs(size, offset):
    return [(i, i ^ offset) for i in range(size)]


def swap_cores(values):
    return lax.ppermute(values, "fsdp", xor_pairs(8, 1))


def swap_rows(values, offset):
    return lax.ppermute(values, "fsdp", xor_pairs(8, 2 * offset))


def swap_seq(values, offset):
    return lax.ppermute(values, "seq", xor_pairs(4, offset))


def fence(*values):
    return lax.optimization_barrier(values)


def window(needed, work):
    outs = jax.eval_shape(work)
    return lax.cond(
        needed,
        work,
        lambda: jax.tree.map(lambda out: jnp.zeros(out.shape, out.dtype), outs),
    )


def halves(block):
    half = block.shape[0] // 2
    return block[:half], block[half:]


def gather_one(block):
    first, second = halves(block)
    return swap_seq(first, 1), swap_seq(second, 2), swap_rows(block, 2)


def gather_two(block, first_more, second_more, next_row):
    first, second = halves(block)
    first = jnp.concatenate([first, first_more])
    second = jnp.concatenate([second, second_more])
    next_first, next_second = halves(next_row)
    return (first, second, next_first, next_second), (
        swap_seq(first, 2),
        swap_seq(second, 1),
        swap_seq(next_first, 1),
        swap_seq(next_second, 2),
    )


def gather_three(held, arrived):
    first, second, next_first, next_second = held
    first_more, second_more, next_first_more, next_second_more = arrived
    own = jnp.concatenate([first, first_more, second, second_more])
    next_first = jnp.concatenate([next_first, next_first_more])
    next_second = jnp.concatenate([next_second, next_second_more])
    return (own, next_first, next_second), (
        swap_cores(own),
        swap_seq(next_first, 2),
        swap_seq(next_second, 1),
    )


def gather_four(held, arrived):
    own, next_first, next_second = held
    other, next_first_more, next_second_more = arrived
    next_own = jnp.concatenate([next_first, next_first_more, next_second, next_second_more])
    return (own, other, next_own), swap_cores(next_own)


def row_one(block):
    first, second = halves(block)
    return swap_seq(first, 1), swap_seq(second, 2)


def row_two(block, first_more, second_more):
    first, second = halves(block)
    first = jnp.concatenate([first, first_more])
    second = jnp.concatenate([second, second_more])
    return (first, second), (swap_seq(first, 2), swap_seq(second, 1))


def row_three(held, arrived):
    own = jnp.concatenate([held[0], arrived[0], held[1], arrived[1]])
    return own, swap_cores(own)


def send_quarters(partial):
    quarter = partial.shape[0] // 4
    return swap_seq(partial[quarter : 2 * quarter], 2), swap_seq(partial[3 * quarter :], 1)


def add_quarters(partial, first, second):
    quarter = partial.shape[0] // 4
    return (
        partial[:quarter].astype(jnp.float32) + first.astype(jnp.float32),
        partial[2 * quarter : 3 * quarter].astype(jnp.float32) + second.astype(jnp.float32),
    )


def send_eighths(first, second):
    half = first.shape[0] // 2
    return (
        swap_seq(first[half:].astype(jnp.bfloat16), 1),
        swap_seq(second[half:].astype(jnp.bfloat16), 2),
    )


def add_eighths(first, second, first_more, second_more):
    half = first.shape[0] // 2
    return jnp.concatenate(
        [
            first[:half] + first_more.astype(jnp.float32),
            second[:half] + second_more.astype(jnp.float32),
        ]
    )


def add(first, second):
    return (first.astype(jnp.float32) + second.astype(jnp.float32)).astype(jnp.bfloat16)


def share_one(first, second):
    return swap_seq(first, 1), swap_seq(second, 2)


def share_two(first, second, first_more, second_more):
    first = jnp.concatenate([first, first_more])
    second = jnp.concatenate([second, second_more])
    return (first, second), (swap_seq(first, 2), swap_seq(second, 1))


def shared(held, arrived):
    return held[0], arrived[0], held[1], arrived[1]


ROWS = [[0, 2, 4, 6], [1, 3, 5, 7]]
ROW_PAIRS = [[0, 2], [4, 6], [1, 3], [5, 7]]
ROW_ORDER = (0, 2, 1, 3)


def gather_rows(block, groups):
    return lax.all_gather(block, "fsdp", axis=0, tiled=True, axis_index_groups=groups)


def scatter_rows(term, groups):
    return lax.psum_scatter(
        term.astype(jnp.bfloat16),
        "fsdp",
        scatter_dimension=0,
        tiled=True,
        axis_index_groups=groups,
    )


def lane_mask(rows):
    return lax.broadcasted_iota(jnp.int32, (rows, LANES), 1) < LANES // 2


def mixed_row(k):
    return (k & 4) | ((k & 1) << 1) | ((k & 2) >> 1)


def slice_wide(weight, gain, place, groups, chunk):
    rows = weight.shape[0]

    def body(place_ref, own_ref, other_ref, gain_ref, *out_refs):
        for weight_ref, out_ref in zip((own_ref, other_ref), out_refs):
            for step in range(2):
                start = pl.multiple_of((place_ref[2] ^ step) * chunk, LANES)
                columns = weight_ref[:, pl.ds(start, chunk)].astype(jnp.float32)
                out_ref[step] = (columns * gain_ref[...]).astype(jnp.bfloat16)

    def columns_of(core):
        return pl.BlockSpec(
            (rows, 2 * chunk), lambda k, p: (0, (mixed_row(k) * 2 + (p[1] ^ core)) * 4 + p[0])
        )

    out = jax.ShapeDtypeStruct((2, rows, groups * chunk), jnp.bfloat16)
    return pl.pallas_call(
        body,
        grid_spec=pltpu.PrefetchScalarGridSpec(
            num_scalar_prefetch=1,
            grid=(groups,),
            in_specs=[columns_of(0), columns_of(1), pl.BlockSpec((rows, 1), lambda k, p: (0, 0))],
            out_specs=[pl.BlockSpec((2, rows, chunk), lambda k, p: (0, 0, k))] * 2,
        ),
        out_shape=[out, out],
        name="slice_wide",
    )(place, weight, weight, gain)


def slice_heads(weight, gain, place, heads):
    rows = weight.shape[0]
    part = weight.shape[1] // 3

    def body(place_ref, weight_ref, gain_ref, *out_refs):
        own_seq, own_core = place_ref[0], place_ref[1]
        odd = (own_seq % 2) == 1
        low = lane_mask(rows)
        for core in range(2):
            for pair in range(heads // 2):
                tiles = []
                for head in (2 * pair, 2 * pair + 1):
                    start = (head * 2 + (own_core ^ core)) * (4 * HEAD_DIM) + (
                        own_seq // 2
                    ) * LANES
                    tile = weight_ref[:, pl.ds(pl.multiple_of(start, LANES), LANES)]
                    tiles.append(tile.astype(jnp.float32) * gain_ref[...])
                turned = [pltpu.roll(tile, LANES // 2, axis=1) for tile in tiles]
                first = jnp.where(odd, turned[0], tiles[0])
                second = jnp.where(odd, tiles[1], turned[1])
                out_refs[core][:, pair * LANES : (pair + 1) * LANES] = jnp.where(
                    low, first, second
                ).astype(jnp.bfloat16)

    out = jax.ShapeDtypeStruct((rows, 3 * heads * HEAD_DIM), jnp.bfloat16)
    return pl.pallas_call(
        body,
        grid_spec=pltpu.PrefetchScalarGridSpec(
            num_scalar_prefetch=1,
            grid=(3,),
            in_specs=[
                pl.BlockSpec((rows, part), lambda k, p: (0, k)),
                pl.BlockSpec((rows, 1), lambda k, p: (0, 0)),
            ],
            out_specs=[pl.BlockSpec((rows, heads * HEAD_DIM), lambda k, p: (0, k))] * 2,
        ),
        out_shape=[out, out],
        name="slice_heads",
    )(place, weight, gain)


def fold(products):
    total = products[:, :LANES]
    for k in range(1, products.shape[1] // LANES):
        total = total + products[:, k * LANES : (k + 1) * LANES]
    return total


PIECES = (((0, 0), (0, 2), (1, 0), (1, 2)), ((2, 0), (3, 0), (2, 2), (3, 2)))


def merge_wide(pieces, weight, gain, place, groups, chunk):
    rows = weight.shape[0]
    width = 16 * chunk

    def body(place_ref, *refs):
        weight_ref, gain_ref = refs[4:6]
        out_ref, sum_ref = refs[6:]

        @pl.when(pl.program_id(0) == 0)
        def _():
            sum_ref[...] = jnp.zeros_like(sum_ref)

        for r in range(4):
            for k in range(4):
                block = ((place_ref[1] ^ (k // 2)) * 4 + (place_ref[0] ^ r)) * 2 + (
                    place_ref[2] ^ (k % 2)
                )
                columns = pl.ds(pl.multiple_of(block * chunk, LANES), chunk)
                term = refs[PIECES[k // 2][r][0]][PIECES[k // 2][r][1] + k % 2].astype(jnp.float32)
                out_ref[:, columns] = term * gain_ref[...]
                sum_ref[place_ref[0] ^ r] += fold(
                    term * weight_ref[:, columns].astype(jnp.float32)
                )

    wide = pl.BlockSpec((rows, width), lambda k, p: (0, mixed_row(k)))
    return pl.pallas_call(
        body,
        grid_spec=pltpu.PrefetchScalarGridSpec(
            num_scalar_prefetch=1,
            grid=(groups,),
            in_specs=[pl.BlockSpec((4, rows, chunk), lambda k, p: (0, 0, k))] * 4
            + [wide, pl.BlockSpec((rows, 1), lambda k, p: (0, 0))],
            out_specs=[wide, pl.BlockSpec((4, rows, LANES), lambda k, p: (0, 0, 0))],
        ),
        out_shape=[
            jax.ShapeDtypeStruct(weight.shape, jnp.float32),
            jax.ShapeDtypeStruct((4, rows, LANES), jnp.float32),
        ],
        compiler_params=pltpu.CompilerParams(vmem_limit_bytes=32 * 1024 * 1024),
        name="merge_wide",
    )(place, *pieces, weight, gain)


def merge_heads(pieces, weight, gain, place, heads):
    rows = weight.shape[0]
    part = weight.shape[1] // 3

    def body(place_ref, *refs):
        weight_ref, gain_ref = refs[4:6]
        out_ref, sum_ref = refs[6:]
        own_seq, own_core = place_ref[0], place_ref[1]
        odd = (own_seq % 2) == 1
        low = lane_mask(rows)

        @pl.when(pl.program_id(0) == 0)
        def _():
            sum_ref[...] = jnp.zeros_like(sum_ref)

        for core in range(2):
            for pair in range(heads // 2):
                for couple in range(2):
                    first, second = (
                        refs[at][block // 2, :, pair * LANES : (pair + 1) * LANES].astype(
                            jnp.float32
                        )
                        for at, block in PIECES[core][2 * couple : 2 * couple + 2]
                    )
                    turned_first = pltpu.roll(first, LANES // 2, axis=1)
                    turned_second = pltpu.roll(second, LANES // 2, axis=1)
                    for head, even_tile, odd_tile in (
                        (
                            2 * pair,
                            jnp.where(low, first, turned_second),
                            jnp.where(low, second, turned_first),
                        ),
                        (
                            2 * pair + 1,
                            jnp.where(low, turned_first, second),
                            jnp.where(low, turned_second, first),
                        ),
                    ):
                        tile = jnp.where(odd, odd_tile, even_tile)
                        start = (head * 2 + (own_core ^ core)) * (4 * HEAD_DIM) + (
                            (own_seq // 2) ^ couple
                        ) * LANES
                        columns = pl.ds(pl.multiple_of(start, LANES), LANES)
                        out_ref[:, columns] = tile * gain_ref[...]
                        sum_ref[(own_seq // 2) ^ couple] += tile * weight_ref[:, columns].astype(
                            jnp.float32
                        )

    wide = pl.BlockSpec((rows, part), lambda k, p: (0, k))
    return pl.pallas_call(
        body,
        grid_spec=pltpu.PrefetchScalarGridSpec(
            num_scalar_prefetch=1,
            grid=(3,),
            in_specs=[pl.BlockSpec((2, rows, heads * HEAD_DIM), lambda k, p: (0, 0, k))] * 4
            + [wide, pl.BlockSpec((rows, 1), lambda k, p: (0, 0))],
            out_specs=[wide, pl.BlockSpec((2, rows, LANES), lambda k, p: (0, 0, 0))],
        ),
        out_shape=[
            jax.ShapeDtypeStruct(weight.shape, jnp.float32),
            jax.ShapeDtypeStruct((2, rows, LANES), jnp.float32),
        ],
        name="merge_heads",
    )(place, *pieces, weight, gain)


def dot_rows(left, right):
    return lax.dot_general(
        left, right, (((1,), (1,)), ((), ())), preferred_element_type=jnp.float32
    )


def swap_head_halves(values):
    lanes = lax.broadcasted_iota(jnp.int32, values.shape, 1) % HEAD_DIM
    half = HEAD_DIM // 2
    return jnp.where(
        lanes < half,
        pltpu.roll(values, LANES - half, axis=1),
        pltpu.roll(values, half, axis=1),
    )


def softmax_of(query, keys, visible):
    scores = jnp.where(visible, dot_rows(query, keys) * SCALE, -1e30)
    weights = jnp.exp(scores - jnp.max(scores, axis=1, keepdims=True))
    return weights / jnp.sum(weights, axis=1, keepdims=True)


def attend(mixed, cosine, sine, rows_at, columns_at):
    length = cosine.shape[0]
    total, columns = mixed.shape
    part = columns // 3

    def body(mixed_ref, cosine_ref, sine_ref, rows_ref, columns_ref, out_ref, turned_ref):
        visible = columns_ref[...] <= rows_ref[...]
        low = lane_mask(length)
        for k in range(2 * part // LANES):
            lanes = slice(k * LANES, (k + 1) * LANES)
            heads = mixed_ref[:, lanes].astype(jnp.float32)
            turned_ref[:, lanes] = (
                heads * cosine_ref[...] + swap_head_halves(heads) * sine_ref[...]
            ).astype(jnp.bfloat16)
        for k in range(part // LANES):
            query = turned_ref[:, k * LANES : (k + 1) * LANES]
            keys = turned_ref[:, part + k * LANES : part + (k + 1) * LANES]
            values = mixed_ref[:, 2 * part + k * LANES : 2 * part + (k + 1) * LANES]
            zero = jnp.zeros_like(query)
            outs = []
            for own in (low, ~low):
                probabilities = softmax_of(jnp.where(own, query, zero), keys, visible)
                outs.append(
                    jnp.dot(
                        probabilities.astype(jnp.bfloat16),
                        values,
                        preferred_element_type=jnp.float32,
                    )
                )
            out_ref[:, k * LANES : (k + 1) * LANES] = jnp.where(low, outs[0], outs[1]).astype(
                jnp.bfloat16
            )

    def whole(shape):
        return pl.BlockSpec(shape, lambda i: (0, 0))

    return pl.pallas_call(
        body,
        grid=(total // length,),
        in_specs=[
            pl.BlockSpec((length, columns), lambda i: (i, 0)),
            whole((length, LANES)),
            whole((length, LANES)),
            whole((length, 1)),
            whole((1, length)),
        ],
        out_specs=[
            pl.BlockSpec((length, part), lambda i: (i, 0)),
            pl.BlockSpec((length, 2 * part), lambda i: (i, 0)),
        ],
        out_shape=[
            jax.ShapeDtypeStruct((total, part), jnp.bfloat16),
            jax.ShapeDtypeStruct((total, 2 * part), jnp.bfloat16),
        ],
        compiler_params=pltpu.CompilerParams(vmem_limit_bytes=40 * 1024 * 1024),
        cost_estimate=pl.CostEstimate(
            flops=8 * total * length * part,
            bytes_accessed=12 * total * part,
            transcendentals=total * length * part // HEAD_DIM,
        ),
        name="attend",
    )(mixed, cosine, sine, rows_at, columns_at)


def attend_back(turned, mixed, grad_heads, cosine, sine, rows_at, columns_at):
    length = cosine.shape[0]
    total, columns = mixed.shape
    part = columns // 3

    def body(
        turned_ref, values_ref, grad_ref, cosine_ref, sine_ref, rows_ref, columns_ref, out_ref
    ):
        visible = columns_ref[...] <= rows_ref[...]
        low = lane_mask(length)
        for k in range(part // LANES):
            lanes = slice(k * LANES, (k + 1) * LANES)
            query = turned_ref[:, lanes]
            keys = turned_ref[:, part + k * LANES : part + (k + 1) * LANES]
            values = values_ref[:, lanes]
            grad = grad_ref[:, lanes]
            zero = jnp.zeros_like(query)
            grads = []
            for own in (low, ~low):
                probabilities = softmax_of(jnp.where(own, query, zero), keys, visible)
                grad_probabilities = dot_rows(jnp.where(own, grad, zero), values)
                inner = jnp.sum(probabilities * grad_probabilities, axis=1, keepdims=True)
                grad_scores = (probabilities * (grad_probabilities - inner)).astype(jnp.bfloat16)
                grads.append(
                    (
                        jnp.dot(grad_scores, keys, preferred_element_type=jnp.float32) * SCALE,
                        outer_sum(grad_scores, query) * SCALE,
                        outer_sum(probabilities.astype(jnp.bfloat16), grad),
                    )
                )
            for which in range(3):
                heads = jnp.where(low, grads[0][which], grads[1][which])
                if which < 2:
                    heads = heads * cosine_ref[...] - swap_head_halves(heads) * sine_ref[...]
                start = which * part + k * LANES
                out_ref[:, start : start + LANES] = heads.astype(jnp.bfloat16)

    def whole(shape):
        return pl.BlockSpec(shape, lambda i: (0, 0))

    return pl.pallas_call(
        body,
        grid=(total // length,),
        in_specs=[
            pl.BlockSpec((length, 2 * part), lambda i: (i, 0)),
            pl.BlockSpec((length, part), lambda i: (i, 2)),
            pl.BlockSpec((length, part), lambda i: (i, 0)),
            whole((length, LANES)),
            whole((length, LANES)),
            whole((length, 1)),
            whole((1, length)),
        ],
        out_specs=pl.BlockSpec((length, columns), lambda i: (i, 0)),
        out_shape=jax.ShapeDtypeStruct((total, columns), jnp.bfloat16),
        compiler_params=pltpu.CompilerParams(vmem_limit_bytes=48 * 1024 * 1024),
        cost_estimate=pl.CostEstimate(
            flops=20 * total * length * part,
            bytes_accessed=16 * total * part,
            transcendentals=total * length * part // HEAD_DIM,
        ),
        name="attend_back",
    )(turned, mixed, grad_heads, cosine, sine, rows_at, columns_at)


def place_rows(pieces, place):
    rows = pieces[0].shape[0] // 2
    width = pieces[0].shape[1]

    def body(place_ref, *refs):
        for half in range(2):
            for k in range(4):
                at, block = PIECES[half][k]

                @pl.when(pl.program_id(0) == half * 4 + k)
                def _(at=at, start=block // 2 * rows):
                    refs[4][...] = refs[at][start : start + rows, :].astype(jnp.float32)

    return pl.pallas_call(
        body,
        grid_spec=pltpu.PrefetchScalarGridSpec(
            num_scalar_prefetch=1,
            grid=(8,),
            in_specs=[pl.BlockSpec((2 * rows, width), lambda i, p: (0, 0))] * 4,
            out_specs=pl.BlockSpec((rows, width), lambda i, p: ((p[0] ^ (i % 4)) * 2 + i // 4, 0)),
        ),
        out_shape=jax.ShapeDtypeStruct((8 * rows, width), jnp.float32),
        compiler_params=pltpu.CompilerParams(vmem_limit_bytes=32 * 1024 * 1024),
        name="place_rows",
    )(place, *pieces)


def mix_blocks(values):
    blocks = jnp.split(values, 4, axis=1)
    return jnp.concatenate([blocks[k] for k in ROW_ORDER], axis=1)


def in_order(own, other, place):
    return jnp.concatenate([jnp.where(place == 0, own, other), jnp.where(place == 0, other, own)])


def sliced_plan(hidden_in, norm_one, w_qkv, w_out, norm_two, w_gate_up, w_down, grad_out):
    own_seq = lax.axis_index("seq")
    own_core = lax.axis_index("fsdp") % 2
    row = lax.axis_index("fsdp") // 2
    step = row // 2
    place = jnp.stack([own_seq, own_core, step]).astype(jnp.int32)
    inputs = hidden_in[0].astype(jnp.float32)
    cotangent = grad_out[0]
    tokens, width = inputs.shape
    length = tokens * 4
    chunk = w_down.shape[0] // 8
    chip_rows = width // 4
    gain_one = norm_one.astype(jnp.float32)[:, None]
    gain_two = norm_two.astype(jnp.float32)[:, None]

    needed = own_seq < 4
    heads = 4

    def project(rows, weight):
        return jnp.dot(rows, weight, preferred_element_type=jnp.float32).astype(jnp.bfloat16)

    def token_part(rows, k):
        return rows[k * length : (k + 1) * length]

    def backward(grad, weight):
        return [
            back_product(token_part(grad, k), weight).astype(jnp.bfloat16)
            for k in range(grad.shape[0] // length)
        ]

    def own_rows(pair, rows):
        return (
            lax.dynamic_slice_in_dim(pair, step * rows, rows),
            lax.dynamic_slice_in_dim(pair, (1 - step) * rows, rows),
        )

    def halves_of_chip(*chips):
        half_rows = chip_rows // 2

        def of_core(core):
            return jnp.stack(
                [
                    lax.dynamic_slice_in_dim(rows, start + core * half_rows, half_rows)
                    for rows, start in chips
                ]
            )

        return of_core(own_core), swap_cores(of_core(1 - own_core))

    factor_one = lax.rsqrt(jnp.mean(inputs * inputs, axis=-1, keepdims=True) + EPSILON)
    normed = (inputs * factor_one).astype(jnp.bfloat16)
    qkv_own, qkv_other = slice_heads(w_qkv, gain_one, place, heads)
    normed, qkv_chip, w_out, w_down = fence(
        normed, in_order(qkv_own, swap_cores(qkv_other), own_core), w_out, w_down
    )
    qkv = gather_rows(qkv_chip, ROWS)
    out_proj = gather_rows(lax.dynamic_slice_in_dim(w_out, own_seq * HEAD_DIM, HEAD_DIM), ROWS)

    def gather_inputs():
        flight = fence(*row_one(normed))
        held, flight = row_two(normed, *flight)
        wide_own, wide_other = slice_wide(w_gate_up, gain_two, place, 8, chunk)
        *flight, wide_own, wide_other = fence(*flight, wide_own, wide_other)
        own, other = row_three(held, flight)
        other, *flight, wide_swapped = fence(other, *row_one(cotangent), swap_cores(wide_other))
        held, flight = row_two(cotangent, *flight)
        flight = fence(*flight)
        cotangent_own, cotangent_other = row_three(held, flight)
        return (
            jnp.concatenate([own, other]),
            [in_order(wide_own[k], wide_swapped[k], own_core) for k in range(2)],
            cotangent_own,
            *fence(cotangent_other),
        )

    normed_all, wide_chips, cotangent_own, cotangent_other = window(needed, gather_inputs)

    half_block = tokens // 2
    starts = jnp.concatenate(
        [
            (own_seq ^ jnp.array([0, 1, 2, 3])) * tokens,
            (own_seq ^ jnp.array([0, 2, 1, 3])) * tokens + half_block,
        ]
    )
    positions = (starts[:, None] + jnp.arange(half_block)[None]).reshape(length)
    half = HEAD_DIM // 2
    freqs = THETA ** (-(jnp.arange(half, dtype=jnp.float32) * 2.0) / HEAD_DIM)
    angles = positions.astype(jnp.float32)[:, None] * freqs[None, :]
    cosine = jnp.tile(jnp.cos(angles), (1, 4))
    sine = jnp.tile(jnp.concatenate([-jnp.sin(angles), jnp.sin(angles)], axis=1), (1, 2))
    tables = (cosine, sine, positions[:, None], positions[None, :])

    def norm_two_of(middle):
        factor = lax.rsqrt(jnp.mean(middle * middle, axis=-1, keepdims=True) + EPSILON)
        return mix_blocks((middle * factor).astype(jnp.bfloat16)), factor

    def attention():
        mixed = project(normed_all, qkv)
        return mixed, *attend(mixed, *tables)

    mixed, attended, turned = window(needed, attention)
    attended, out_proj, wide_send, w_down = fence(attended, out_proj, wide_chips[1], w_down)
    wide_more = swap_rows(wide_send, 2)
    down_rows = [
        lax.dynamic_slice_in_dim(w_down, own_seq * 2 * chunk + (step ^ k) * chunk, chunk)
        for k in range(2)
    ]

    def attention_out():
        other = project(token_part(attended, 1), out_proj)
        own = project(token_part(attended, 0), out_proj)
        swapped, own = fence(swap_cores(other), own)
        own = add(own, swapped)
        flight = fence(*send_quarters(own))
        own = add_quarters(own, *flight)
        flight = fence(*send_eighths(*own))
        middle = inputs + add_eighths(*own, *flight)
        return middle, norm_two_of(middle)[0]

    def row_gather(block):
        held, flight = row_two(block, *fence(*row_one(block)))
        own, other = row_three(held, fence(*flight))
        return own, *fence(other)

    middle, normed_two = window(needed, attention_out)
    normed_two_next = swap_rows(normed_two, 2)
    normed_two_row = window(needed, lambda: row_gather(normed_two))
    wide_more, normed_two_next, down_send, cotangent_send, *normed_two_row = fence(
        wide_more, normed_two_next, down_rows[1], cotangent, *normed_two_row
    )
    gate_up_w = gather_rows(in_order(wide_chips[0], wide_more, step), ROW_PAIRS)
    cotangent_next = swap_rows(cotangent_send, 2)
    down_more = swap_rows(down_send, 2)
    normed_two_all = window(
        needed, lambda: jnp.concatenate([*normed_two_row, *row_gather(normed_two_next)])
    )
    normed_two_all, cotangent_next = fence(normed_two_all, cotangent_next)
    cotangent_all = window(
        needed,
        lambda: jnp.concatenate([cotangent_own, cotangent_other, *row_gather(cotangent_next)]),
    )
    down_more, cotangent_all = fence(down_more, cotangent_all)
    down = gather_rows(in_order(down_rows[0], down_more, step), ROW_PAIRS)

    _, factor_two = norm_two_of(middle)
    gate_up = jnp.dot(normed_two_all, gate_up_w, preferred_element_type=jnp.float32)
    units = gate_up.shape[1] // 2
    gate, upward = gate_up[:, :units], gate_up[:, units:]
    sigmoid = jax.nn.sigmoid(gate)
    activated = gate * sigmoid
    hidden = (activated * upward).astype(jnp.bfloat16)
    grad_down_term = outer_sum(hidden, cotangent_all).astype(jnp.bfloat16)
    grad_down_pair = scatter_rows(grad_down_term, ROW_PAIRS)
    cotangent_all, grad_down_term = fence(cotangent_all, grad_down_term)
    grad_hidden = back_product(cotangent_all, down)
    grad_gate = grad_hidden * upward * sigmoid * (1.0 + gate * (1.0 - sigmoid))
    grad_upward = grad_hidden * activated
    grad_low = jnp.concatenate([grad_gate, grad_upward], axis=1).astype(jnp.bfloat16)

    def backward_part(grad, weight, k):
        return back_product(token_part(grad, k), weight).astype(jnp.bfloat16)

    far, far_other = fence(
        backward_part(grad_low, gate_up_w, 2), backward_part(grad_low, gate_up_w, 3)
    )
    grad_gate_up_term = outer_sum(normed_two_all, grad_low).astype(jnp.bfloat16)
    swapped, far, grad_gate_up_term, grad_low, grad_down_pair, hidden = fence(
        swap_cores(far_other), far, grad_gate_up_term, grad_low, grad_down_pair, hidden
    )
    grad_gate_up_pair = scatter_rows(grad_gate_up_term, ROW_PAIRS)
    far = add(far, swapped)
    *flight, near, near_other, forward_near, near_forward_other, forward_far, forward_other = fence(
        *send_quarters(far),
        backward_part(grad_low, gate_up_w, 0),
        backward_part(grad_low, gate_up_w, 1),
        *(project(token_part(hidden, k), down) for k in range(4)),
    )
    far = add_quarters(far, *flight)

    def feed_forward_back():
        *flight, swapped, forward_swapped = fence(
            *send_eighths(*far), swap_cores(near_other), swap_cores(forward_other)
        )
        next_row = add_eighths(*far, *flight).astype(jnp.bfloat16)
        near_sum = add(near, swapped)
        forward_sum = add(forward_far, forward_swapped)
        next_row, first, second, *flight = fence(
            swap_rows(next_row, 2), *send_quarters(near_sum), *send_quarters(forward_sum)
        )
        quarters = add_quarters(near_sum, first, second)
        forward_quarters = add_quarters(forward_sum, *flight)
        first, second, *flight = fence(
            *send_eighths(*quarters), *send_eighths(*forward_quarters)
        )
        scaled = mix_blocks(add_eighths(*quarters, first, second) + next_row.astype(jnp.float32))
        grad_middle = (
            cotangent.astype(jnp.float32)
            + factor_two * scaled
            - middle * factor_two**3 * jnp.mean(scaled * middle, axis=-1, keepdims=True)
        )
        return grad_middle, add_eighths(*forward_quarters, *flight).astype(jnp.bfloat16)

    grad_middle, forward_far = window(needed, feed_forward_back)
    wide_send = lax.dynamic_slice_in_dim(grad_gate_up_pair, (1 - step) * chip_rows, chip_rows)
    grad_middle, wide_send = fence(grad_middle, wide_send)
    wide_more = swap_rows(wide_send, 2)

    def gather_branch():
        block = grad_middle.astype(jnp.bfloat16)
        *flight, swapped = fence(*row_one(block), swap_cores(near_forward_other))
        held, flight = row_two(block, *flight)
        flight = fence(*flight)
        own, other = row_three(held, flight)
        forward_sum = add(forward_near, swapped)
        other, *flight = fence(other, *send_quarters(forward_sum))
        return jnp.concatenate([own, other]), add_quarters(forward_sum, *flight)

    grad_branch, forward_quarters = window(needed, gather_branch)

    down_own, down_send = own_rows(grad_down_pair, chunk)
    grad_branch, wide_more, down_send = fence(grad_branch, wide_more, down_send)

    def attention_back():
        grad_heads = back_product(grad_branch, out_proj).astype(jnp.bfloat16)
        grad_heads, *wide_halves = fence(
            grad_heads, *halves_of_chip((grad_gate_up_pair, step * chip_rows), (wide_more, 0))
        )
        flight = share_one(*wide_halves)
        down_more = swap_rows(down_send, 2)
        grad_mixed = attend_back(turned, mixed, grad_heads, *tables)
        grad_mixed, *near = fence(grad_mixed, *forward_quarters)
        grad_qkv_term = outer_sum(normed_all, grad_mixed).astype(jnp.bfloat16)
        arrived = fence(grad_qkv_term, down_more, *send_eighths(*near), *flight)
        return grad_mixed, wide_halves, arrived

    grad_mixed, wide_halves, arrived = window(needed, attention_back)
    grad_qkv_term, down_more, forward_first, forward_second, *wide_flight = arrived
    grad_qkv_rows = scatter_rows(grad_qkv_term, ROWS)
    wide_held, wide_flight = share_two(*wide_halves, *wide_flight)

    def inputs_back():
        back = backward(grad_mixed, qkv)
        swapped, near = fence(swap_cores(back[1]), back[0])
        near = add(near, swapped)
        near = add_quarters(near, *fence(*send_quarters(near)))
        scaled = add_eighths(*near, *fence(*send_eighths(*near)))
        return (
            grad_middle
            + factor_one * scaled
            - inputs * factor_one**3 * jnp.mean(scaled * inputs, axis=-1, keepdims=True)
        )

    grad_inputs = window(needed, inputs_back)

    grad_qkv_rows, grad_inputs, attended, forward_far, w_gate_up, down_own, down_more = fence(
        grad_qkv_rows, grad_inputs, attended, forward_far, w_gate_up, down_own, down_more
    )
    down_halves = halves(in_order(down_own, down_more, step))
    qkv_mine, qkv_swapped = halves_of_chip((grad_qkv_rows, 0))
    qkv_swapped, w_gate_up, attended, *down_halves = fence(
        qkv_swapped, w_gate_up, attended, *down_halves
    )
    qkv_halves = qkv_mine, qkv_swapped
    flight = *share_one(*qkv_halves), *share_one(*down_halves)
    grad_out_rows = scatter_rows(outer_sum(attended, grad_branch), ROWS)
    forward_next = swap_rows(forward_far, 2)
    grad_gate_up, gain_two_sums = merge_wide(
        shared(wide_held, wide_flight), w_gate_up, gain_two, place, 8, chunk
    )
    grad_gate_up, gain_two_sums, *flight = fence(grad_gate_up, gain_two_sums, *flight)
    qkv_held, qkv_flight = share_two(*qkv_halves, *flight[:2])
    down_held, down_flight = share_two(*down_halves, *flight[2:])
    grad_out_rows, *qkv_flight = fence(grad_out_rows, *qkv_flight)
    out_halves = halves(grad_out_rows)
    grad_qkv, gain_one_sums = merge_heads(
        shared(qkv_held, qkv_flight), w_qkv, gain_one, place, heads
    )
    grad_qkv, gain_one_sums, forward_next, *flight = fence(
        grad_qkv, gain_one_sums, forward_next, *down_flight, *share_one(*out_halves)
    )
    out_held, out_flight = share_two(*out_halves, *flight[2:])
    output = middle + forward_next.astype(jnp.float32)
    output = output + add_eighths(*forward_quarters, forward_first, forward_second)
    grad_down = place_rows(shared(down_held, flight[:2]), place)
    grad_down, output, *out_flight = fence(grad_down, output, *out_flight)
    return (
        output.astype(jnp.bfloat16)[None],
        grad_inputs[None],
        jnp.sum(gain_one_sums, axis=(0, 2)),
        grad_qkv,
        place_rows(shared(out_held, out_flight), place),
        jnp.sum(gain_two_sums, axis=(0, 2)),
        grad_gate_up,
        grad_down,
    )


def solution(mesh):
    seq, fsdp = mesh.shape["seq"], mesh.shape["fsdp"]

    def on_device(hidden_in, norm_one, w_qkv, w_out, norm_two, w_gate_up, w_down, grad_out):
        arrays = (hidden_in, norm_one, w_qkv, w_out, norm_two, w_gate_up, w_down, grad_out)
        if seq == 4 and fsdp == 8 and w_out.shape[0] == 4 * HEAD_DIM and w_down.shape[0] % 1024 == 0:
            return sliced_plan(*arrays)
        return gathered_plan(*arrays)

    placed = (
        P("fsdp", "seq", None),
        P("fsdp"),
        P("fsdp", None),
        P("fsdp", None),
        P("fsdp"),
        P("fsdp", None),
        P("fsdp", None),
        P("fsdp", "seq", None),
    )
    return jax.shard_map(
        on_device,
        mesh=mesh,
        in_specs=placed,
        out_specs=(
            P("fsdp", "seq", None),
            P("fsdp", "seq", None),
            P("fsdp"),
            P("fsdp", None),
            P("fsdp", None),
            P("fsdp"),
            P("fsdp", None),
            P("fsdp", None),
        ),
        check_vma=False,
    )
```
